512 devices in a mesh: lat: 64 (over z, y), lon: 8 (over x, core).
Axes of the slice: x: 4, y: 4, z: 16, core: 2. Of those that a mesh axis runs over, the one named last changes fastest.
Arguments:
- prior_sample_set: float32 [3, 80, 512, 1024], P(None, None, 'lat', 'lon'), may hold values from -6 to 6
- still_surface_thickness: float32 [512, 1024], P('lat', 'lon'), may hold values from 0.5 to 1.5
- lat_taper: float32 [32], replicated, may hold values from 0.1 to 1
- longitude_weight: float32 [256], replicated, may hold values from 0.1 to 1
- obs_cell: int32 [8192], P(('lat', 'lon')), may hold values from 0 to 524287, as said below
- obs_reach: int32 [8192], P(('lat', 'lon')), may hold values from 0 to 3
- obs_lon_reach: int32 [8192], P(('lat', 'lon')), may hold values from 0 to 1
- obs_batch: int32 [8192], P(('lat', 'lon')), may hold values from 0 to 1, as said below
- obs_value: float32 [8192], P(('lat', 'lon')), may hold values from -6 to 6
- obs_var: float32 [8192], P(('lat', 'lon')), may hold values from 0.2 to 2
Outputs:
- analysis: float32 [3, 80, 512, 1024], P(None, None, 'lat', 'lon')
The draws below stay inside these ranges and needn't reach their ends.
Inputs may be any that keep to these rules, and one draw needn't show every extreme that they name: `obs_cell`: each observation lies in the cell block of the device that holds its slot (slots are laid out by device, latitude band slowest). `obs_batch`: in the slots of one device each batch holds at most 12 observations; in every draw some device holds exactly 12 of batch 0 and some device exactly 12 of batch 1.
All inputs are finite; a program needn't handle non-finite values.
Results may differ from the reference program's by a relative error of at most 0.0037.
Values may be sent and summed in bfloat16 or wider, within the bound.
A program may use at most 64 MiB of HBM per device.

```python
import math
import jax
import jax.numpy as jnp
from jax import lax

MEMBERS = 80
CLAT = 8
CLON = 128
OBS_DEV = 16
REACH = 3
LON_REACH = 1
SUB = 4
MOST = 12
NLAT = 512
NLON = 1024
OBS = 8192
LATTAB = 32
LONTAB = 256
N_LAT = 64
N_LON = 8


def draw_obs_cell(key, part):
    key = jax.random.fold_in(key, 11)
    row_key, col_key = jax.random.split(key, 2)
    total = OBS_DEV * N_LAT * N_LON
    slot_ids = jnp.arange(total)
    device_ids = slot_ids // OBS_DEV
    band_ids = device_ids // N_LON
    sector_ids = device_ids % N_LON
    row_offset = jax.random.randint(row_key, (total,), 0, CLAT)
    col_offset = jax.random.randint(col_key, (total,), 0, CLON)
    row_offset = jnp.where(slot_ids == 0, 0, row_offset)
    col_offset = jnp.where(slot_ids == 0, 0, col_offset)
    row_offset = jnp.where(slot_ids == total - 1, CLAT - 1, row_offset)
    col_offset = jnp.where(slot_ids == total - 1, CLON - 1, col_offset)
    grid_row = band_ids * CLAT + row_offset
    grid_col = sector_ids * CLON + col_offset
    return (grid_row * (CLON * N_LON) + grid_col).astype(jnp.int32)


def draw_obs_batch(key, part):
    key = jax.random.fold_in(key, 23)
    count_key, full_key, other_key, perm_key = jax.random.split(key, 4)
    device_total = N_LAT * N_LON
    counts = jax.random.randint(count_key, (device_total,), OBS_DEV - MOST, MOST + 1)
    fullest = jax.random.randint(full_key, (), 0, device_total)
    emptiest = (fullest + jax.random.randint(other_key, (), 1, device_total)) % device_total
    device_ids = jnp.arange(device_total)
    counts = jnp.where(device_ids == fullest, MOST, counts)
    counts = jnp.where(device_ids == emptiest, OBS_DEV - MOST, counts)
    perm_keys = jax.random.split(perm_key, device_total)
    ranks = jax.vmap(lambda subkey: jax.random.permutation(subkey, OBS_DEV))(perm_keys)
    batches = (ranks >= counts[:, None]).astype(jnp.int32)
    return batches.reshape(-1)


def touch_ends(array, own_key, least, top_value):
    spot = [jax.random.randint(jax.random.fold_in(own_key, axis), (), 0, length) for axis, length in enumerate(array.shape)]
    widest = array.shape.index(max(array.shape))
    beside = spot[:widest] + [(spot[widest] + 1) % array.shape[widest]] + spot[widest + 1:]
    return array.at[tuple(spot)].set(least).at[tuple(beside)].set(top_value)


def steps_of(rng, extent, cuts, least, largest):
    def one(position, shards_of):
        steps = jax.random.uniform(jax.random.fold_in(jax.random.fold_in(rng, 6), position), (shards_of,), jnp.float32, least / len(cuts), largest / len(cuts))
        return jnp.repeat(jnp.exp(steps), extent[position] // shards_of).reshape((-1,) + (1,) * (len(extent) - position - 1))

    gain = one(*cuts[0])
    for cut in cuts[1:]:
        gain = gain * one(*cut)
    return gain


def gaussian(stream_key, dims, spread, limit, cuts=(), held_as=jnp.bfloat16):
    result = jax.random.normal(stream_key, dims, jnp.float32) * spread
    if len(cuts) > 0:
        result = steps_of(stream_key, dims, cuts, -0.22, 0.18) * result
    return jnp.clip(result, min=-limit, max=limit).astype(held_as)


def setup_inputs(seed: int = 0) -> dict:
    splits = jax.random.split(jax.random.key(seed), 11)
    prior_sample_set = gaussian(splits[0], (3, MEMBERS, NLAT, NLON), 1.0, 6.0, ((2, 64), (3, 8)), jnp.float32)
    still_surface_thickness = jnp.clip(0.5 + 1.0 * jax.random.uniform(splits[1], (NLAT, NLON), jnp.float32) ** steps_of(splits[1], (NLAT, NLON), ((0, 64), (1, 8)), -0.2, 0.2), 0.5, 1.5)
    lat_taper = jnp.clip(jnp.exp(jax.random.uniform(splits[2], (LATTAB,), jnp.float32, math.log(0.1), math.log(1.0))), 0.1, 1.0)
    longitude_weight = jnp.clip(jnp.exp(jax.random.uniform(splits[3], (LONTAB,), jnp.float32, math.log(0.1), math.log(1.0))), 0.1, 1.0)
    obs_cell = draw_obs_cell(jax.random.fold_in(splits[10], 71), 0)
    obs_reach = touch_ends(jax.random.randint(splits[5], (OBS,), 0, REACH + 1), jax.random.fold_in(splits[5], 1), 0, REACH).astype(jnp.int32)
    obs_lon_reach = touch_ends(jax.random.randint(splits[6], (OBS,), 0, LON_REACH + 1), jax.random.fold_in(splits[6], 1), 0, LON_REACH).astype(jnp.int32)
    obs_batch = draw_obs_batch(jax.random.fold_in(splits[10], 71), 0)
    obs_value = gaussian(splits[8], (OBS,), 1.5, 6.0, ((0, 512),), jnp.float32)
    obs_var = jnp.clip(jnp.exp(math.log(2.0) - 2.3025851 * jax.random.uniform(splits[9], (OBS,), jnp.float32) ** steps_of(splits[9], (OBS,), ((0, 512),), -0.2, 0.2)), 0.2, 2.0)
    return {"prior_sample_set": prior_sample_set, "still_surface_thickness": still_surface_thickness, "lat_taper": lat_taper, "longitude_weight": longitude_weight, "obs_cell": obs_cell, "obs_reach": obs_reach, "obs_lon_reach": obs_lon_reach, "obs_batch": obs_batch, "obs_value": obs_value, "obs_var": obs_var}


TIMESTEP = 0.5
CORIOLIS_FACTOR = 0.3

def east_diff(field):
    return 0.5 * (jnp.roll(field, -1, axis=2) - jnp.roll(field, 1, axis=2))

def north_diff(field):
    padded = jnp.pad(field, ((0, 0), (1, 1), (0, 0)))
    return 0.5 * (padded[:, 2:, :] - padded[:, :-2, :])

def propagate_forward(prior_sample_set, still_surface_thickness, rotation_frequency):
    height, eastward_speed, north_vel = (prior_sample_set[0], prior_sample_set[1], prior_sample_set[2])
    new_east = eastward_speed + TIMESTEP * (rotation_frequency * north_vel - east_diff(height))
    new_north = north_vel + TIMESTEP * (-rotation_frequency * eastward_speed - north_diff(height))
    new_height = height - TIMESTEP * still_surface_thickness * (east_diff(new_east) + north_diff(new_north))
    return jnp.stack([new_height, new_east, new_north])

def reference(prior_sample_set, still_surface_thickness, lat_taper, longitude_weight, obs_cell, obs_reach, obs_lon_reach, obs_batch, obs_value, obs_var):
    members = prior_sample_set.shape[1]
    grid_rows = jnp.arange(NLAT).astype(jnp.float32)
    rotation_frequency = (CORIOLIS_FACTOR * (2.0 * (grid_rows + 0.5) / NLAT - 1.0))[:, None]
    physical_fields_vector = prior_sample_set
    for substep in range(SUB):
        physical_fields_vector = propagate_forward(physical_fields_vector, still_surface_thickness, rotation_frequency)
    band_obs = N_LON * OBS_DEV
    window_len = (2 * REACH + 1) * band_obs
    for batch_id in range(2):
        flat_height = physical_fields_vector[0].reshape(members, NLAT * NLON)
        prior = jnp.take(flat_height, obs_cell, axis=1)
        live = (obs_batch == batch_id).astype(jnp.float32)
        ybar = lax.optimization_barrier(jnp.mean(prior, axis=0))
        deviation = prior - ybar
        spread_sq = lax.optimization_barrier(jnp.sum(deviation * deviation, axis=0)) / (members - 1)
        total_var = spread_sq + obs_var
        obs_dev = (deviation * live).astype(jnp.bfloat16)
        shift_coef = (live * (obs_value - ybar) / total_var).astype(jnp.bfloat16)
        spread_coef = (-live / (jnp.sqrt(total_var) * (jnp.sqrt(obs_var) + jnp.sqrt(total_var)))).astype(jnp.bfloat16)
        state_dev = (physical_fields_vector - lax.optimization_barrier(jnp.mean(physical_fields_vector, axis=1, keepdims=True))).astype(jnp.bfloat16)
        margin = REACH * band_obs
        pad_dev = jnp.pad(obs_dev, ((0, 0), (margin, margin)))
        pad_shift = jnp.pad(shift_coef, (margin, margin))
        pad_spread = jnp.pad(spread_coef, (margin, margin))
        pad_cell = jnp.pad(obs_cell, (margin, margin))
        pad_reach = jnp.pad(obs_reach, (margin, margin))
        pad_lreach = jnp.pad(obs_lon_reach, (margin, margin))
        all_cols = jnp.arange(NLON).astype(jnp.int32)

        def band_update(band_idx):
            start = (band_idx * band_obs).astype(jnp.int32)
            win_dev = lax.dynamic_slice_in_dim(pad_dev, start, window_len, 1).astype(jnp.float32)
            win_shift = lax.dynamic_slice_in_dim(pad_shift, start, window_len, 0).astype(jnp.float32)
            win_spread = lax.dynamic_slice_in_dim(pad_spread, start, window_len, 0).astype(jnp.float32)
            win_cell = lax.dynamic_slice_in_dim(pad_cell, start, window_len, 0)
            win_reach = lax.dynamic_slice_in_dim(pad_reach, start, window_len, 0)
            win_lreach = lax.dynamic_slice_in_dim(pad_lreach, start, window_len, 0)
            row_start = (band_idx * CLAT).astype(jnp.int32)
            band_dev = lax.dynamic_slice_in_dim(state_dev, row_start, CLAT, 2).astype(jnp.float32)
            obs_row = win_cell // NLON
            obs_col = win_cell % NLON
            band_rows = row_start + jnp.arange(CLAT).astype(jnp.int32)
            lat_w = jnp.take(lat_taper, jnp.abs(band_rows[:, None] - obs_row[None, :]), mode='clip')
            col_dist = jnp.abs(all_cols[:, None] - obs_col[None, :])
            col_dist = jnp.minimum(col_dist, NLON - col_dist)
            lon_w = jnp.take(longitude_weight, col_dist, mode='clip')
            sector_dist = jnp.abs(all_cols[:, None] // CLON - obs_col[None, :] // CLON)
            sector_dist = jnp.minimum(sector_dist, N_LON - sector_dist)
            lon_in = (sector_dist <= win_lreach[None, :]).astype(jnp.float32)
            in_reach = (jnp.abs(band_idx - obs_row // CLAT) <= win_reach).astype(jnp.float32)
            locality = lat_w[:, None, :] * (lon_w * lon_in)[None, :, :] * in_reach
            covariance = jnp.einsum('fmij,mk->fijk', band_dev, win_dev)
            kalman_gain = (covariance * locality / (members - 1)).astype(jnp.bfloat16)
            weights = (win_shift[None, :] + win_spread[None, :] * win_dev).astype(jnp.bfloat16)
            return jnp.einsum('fijk,mk->fmij', kalman_gain.astype(jnp.float32), weights.astype(jnp.float32))
        posterior_increments = lax.map(band_update, jnp.arange(N_LAT).astype(jnp.int32))
        posterior_increments = jnp.moveaxis(posterior_increments, 0, 2).reshape(3, members, NLAT, NLON)
        physical_fields_vector = physical_fields_vector + posterior_increments
    return physical_fields_vector
```

```python
import functools

import jax
import jax.numpy as jnp
from jax import lax
from jax.experimental import pallas as pl
from jax.experimental.pallas import tpu as pltpu
from jax.sharding import PartitionSpec as P

REACH = 3
SUB = 4
MOST = 12
TIMESTEP = 0.5
CORIOLIS_FACTOR = 0.3

MEMBERS = 80
ROWS = 8
COLS = 128
SLOTS = 16
PAIRS = 21
OBS = 256
MESH = pl.DeviceIdType.MESH
F32 = jnp.float32
BF16 = jnp.bfloat16

OFFSETS = [
    (dl, dn)
    for dl in sorted(range(-REACH, REACH + 1), key=lambda d: -abs(d))
    for dn in (-1, 1, 0)
    if (dl, dn) != (0, 0)
] + [(0, 0)]


def lanes_of(x, index):
    return jnp.take_along_axis(x, index, axis=1, mode="promise_in_bounds")


def kernel(
    n_lat,
    n_lon,
    state_hbm,
    still_hbm,
    lat_hbm,
    lon_hbm,
    cell_hbm,
    reach_hbm,
    lreach_hbm,
    batch_hbm,
    value_hbm,
    var_hbm,
    out_hbm,
    state,
    still,
    lat_tab,
    lon_tab,
    cell,
    reach,
    lreach,
    batch,
    value,
    var,
    work,
    ns_send,
    ns_recv,
    ew_send,
    ew_recv,
    lab_send,
    lab_recv,
    obs_send,
    obs_recv,
    loc,
    dev,
    small_sem,
    state_sem,
    out_sem,
    ns_ssem,
    ns_rsem,
    ew_ssem,
    ew_rsem,
    lab_ssem,
    lab_rsem,
    obs_ssem,
    obs_rsem,
):
    li = lax.axis_index("lat")
    lo = lax.axis_index("lon")

    def at(dl, dn):
        return (lax.rem(li + dl + n_lat, n_lat), lax.rem(lo + dn + n_lon, n_lon))

    ins = []
    for i, (src, dst) in enumerate(
        (
            (still_hbm, still),
            (lat_hbm, lat_tab),
            (lon_hbm, lon_tab),
            (cell_hbm, cell),
            (reach_hbm, reach),
            (lreach_hbm, lreach),
            (batch_hbm, batch),
            (value_hbm, value),
            (var_hbm, var),
        )
    ):
        ins.append(pltpu.make_async_copy(src, dst, small_sem.at[i]))
        ins[-1].start()
    fields_in = []
    for f in range(3):
        for r in range(ROWS):
            copy = pltpu.make_async_copy(
                state_hbm.at[f, :, r, :], state.at[f, r], state_sem.at[f, r]
            )
            copy.start()
            fields_in.append(copy)

    barrier = pltpu.get_barrier_semaphore()
    for dl, dn in OFFSETS[:-1]:
        pl.semaphore_signal(barrier, inc=1, device_id=at(dl, dn), device_id_type=MESH)

    tile_lane = lax.broadcasted_iota(jnp.int32, (MEMBERS, COLS), 1)
    row_lane = lax.broadcasted_iota(jnp.int32, (1, COLS), 1)

    for copy in ins:
        copy.wait()

    def as_row(ref, fill):
        x = ref[...].reshape(1, SLOTS)
        return jnp.concatenate([x, jnp.full((1, COLS - SLOTS), fill, x.dtype)], axis=1)

    cell_row = as_row(cell, 0)
    reach_row = as_row(reach, 0).astype(F32)
    lreach_row = as_row(lreach, 0).astype(F32)
    batch_row = as_row(batch, -1)
    value_row = as_row(value, 0.0)
    var_row = as_row(var, 1.0)
    lat_rows = cell_row // (COLS * n_lon) - li * ROWS
    lon_cols = lax.rem(cell_row, COLS * n_lon) - lo * COLS
    lat_rows = jnp.where(row_lane < SLOTS, lat_rows, 0)
    lon_cols = jnp.where(row_lane < SLOTS, lon_cols, 0)

    slot_of = lax.broadcasted_iota(jnp.int32, (SLOTS, COLS), 0)
    picks = []
    for b in range(2):
        live = (batch_row == b).astype(jnp.int32)
        upto = live
        for s in (1, 2, 4, 8):
            upto = upto + jnp.where(row_lane >= s, pltpu.roll(upto, s, 1), 0)
        rank = jnp.where(live == 1, upto - 1, -1)
        picks.append((slot_of == rank).astype(F32).astype(BF16))

    sub8 = lax.broadcasted_iota(jnp.int32, (8, COLS), 0)
    labels = jnp.where(
        sub8 == 0,
        lat_rows.astype(F32),
        jnp.where(
            sub8 == 1,
            lon_cols.astype(F32),
            jnp.where(sub8 == 2, reach_row, jnp.where(sub8 == 3, lreach_row, 0.0)),
        ),
    )
    zeros8 = jnp.zeros((8, COLS), F32)
    zeros_rest = jnp.zeros((COLS - 16, COLS), F32)
    rows_to_lanes = (((1,), (1,)), ((), ()))
    label_tile = 0.0
    for b in range(2):
        spread = jnp.concatenate([labels, zeros8] if b == 0 else [zeros8, labels], axis=0)
        spread = jnp.concatenate([spread, zeros_rest], axis=0).astype(BF16)
        label_tile = label_tile + lax.dot_general(
            picks[b], spread, rows_to_lanes, preferred_element_type=F32
        )
    label_tile = label_tile.astype(BF16)
    lab_send[...] = label_tile
    lab_recv[PAIRS - 1] = label_tile

    def send_to_all(src, land, ssem, rsem):
        for i, (dl, dn) in enumerate(OFFSETS[:-1]):
            pltpu.make_async_remote_copy(
                src_ref=src,
                dst_ref=land.at[OFFSETS.index((-dl, -dn))],
                send_sem=ssem,
                recv_sem=rsem,
                device_id=at(dl, dn),
                device_id_type=MESH,
            ).start()

    def all_of(land, ssem, rsem):
        block = land.at[pl.ds(0, PAIRS - 1)]
        return pltpu.make_async_remote_copy(
            src_ref=block,
            dst_ref=block,
            send_sem=ssem,
            recv_sem=rsem,
            device_id=at(0, 1),
            device_id_type=MESH,
        )

    def coriolis(r):
        row = (li * ROWS + r).astype(F32)
        cor = CORIOLIS_FACTOR * (2.0 * (row + 0.5) / (n_lat * ROWS) - 1.0)
        return TIMESTEP * cor

    def gather_rows(land, adjust):
        pieces = []
        for i in range(PAIRS):
            piece = land[i].astype(F32)[:MOST]
            if adjust:
                dl, dn = OFFSETS[i]
                inside = (li + dl >= 0) & (li + dl < n_lat)
                far = jnp.where(inside, -abs(dl), -100).astype(F32)
                lane = row_lane & 7
                piece = piece + (
                    jnp.where(lane == 0, float(dl * ROWS), 0.0)
                    + jnp.where(lane == 1, float(dn * COLS), 0.0)
                    + jnp.where(lane == 2, far, 0.0)
                    + jnp.where(lane == 3, float(-abs(dn)), 0.0)
                )
            pieces.append(piece)
        pieces.append(jnp.zeros((OBS - PAIRS * MOST, COLS), F32))
        return jnp.concatenate(pieces, axis=0)

    def make_locality(b):
        table = gather_rows(lab_recv, True)
        first = 8 * b
        rows = jnp.broadcast_to(table[:, first : first + 1], (OBS, COLS)).astype(jnp.int32)
        cols = jnp.broadcast_to(table[:, first + 1 : first + 2], (OBS, COLS)).astype(jnp.int32)
        within = (table[:, first + 2 : first + 3] >= 0) & (table[:, first + 3 : first + 4] >= 0)
        within = jnp.broadcast_to(jnp.where(within, 1.0 / (MEMBERS - 1), 0.0), (OBS, COLS))
        lane = lax.broadcasted_iota(jnp.int32, (OBS, COLS), 1)
        away = jnp.abs(lane - cols)
        lon_row = lon_tab[...].reshape(1, 2 * COLS)
        low = jnp.broadcast_to(lon_row[:, :COLS], (OBS, COLS))
        high = jnp.broadcast_to(lon_row[:, COLS:], (OBS, COLS))
        lon_w = jnp.where(
            away < COLS, lanes_of(low, away & (COLS - 1)), lanes_of(high, away & (COLS - 1))
        )
        lon_w = lon_w * within
        lat_row = lat_tab[...].reshape(1, 32)
        lat_row = jnp.concatenate([lat_row, jnp.zeros((1, COLS - 32), F32)], axis=1)
        lat_all = jnp.broadcast_to(lat_row, (OBS, COLS))
        for r in range(ROWS):
            loc[b, r] = lanes_of(lat_all, jnp.abs(rows - r)) * lon_w

    edge = jnp.where(
        tile_lane == 0, 0.5 * TIMESTEP, jnp.where(tile_lane == COLS - 1, -0.5 * TIMESTEP, 0.0)
    )
    north_live = (li > 0).astype(F32)
    south_live = (li < n_lat - 1).astype(F32)
    half = 0.5 * TIMESTEP
    sent = []

    for t in range(SUB):
        if t == 0:
            for copy in fields_in:
                copy.wait()
        for r in range(ROWS):
            work[r] = state[2, r] - coriolis(r) * state[1, r]
        ns_send[t, 0, :MEMBERS] = state[0, 0].astype(BF16)
        ns_send[t, 0, MEMBERS:] = (work[0] - half * state[0, 1]).astype(BF16)
        ns_send[t, 1, :MEMBERS] = state[0, ROWS - 1].astype(BF16)
        ns_send[t, 1, MEMBERS:] = (work[ROWS - 1] + half * state[0, ROWS - 2]).astype(BF16)
        if t == 0:
            pl.semaphore_wait(barrier, PAIRS - 1)
        waits = []
        for side, dl in ((0, -1), (1, 1)):
            copy = pltpu.make_async_remote_copy(
                src_ref=ns_send.at[t, side],
                dst_ref=ns_recv.at[t, side],
                send_sem=ns_ssem.at[t, side],
                recv_sem=ns_rsem.at[t, side],
                device_id=at(dl, 0),
                device_id_type=MESH,
            )
            copy.start()
            waits.append(copy)
        packed = jnp.zeros((MEMBERS, COLS), F32)
        for r in range(ROWS):
            h = state[0, r]
            left = pltpu.roll(h, 1, 1)
            right = pltpu.roll(h, COLS - 1, 1)
            z = state[1, r] + coriolis(r) * state[2, r]
            u = (
                z
                + jnp.where(tile_lane == 0, 0.0, half * left)
                - jnp.where(tile_lane == COLS - 1, 0.0, half * right)
            )
            state[1, r] = u
            mixed = jnp.where(tile_lane == COLS - 2, right, jnp.where(tile_lane == 1, left, u))
            packed = jnp.where((tile_lane >> 2) == r, pltpu.roll(mixed, 4 * r + 2, 1), packed)
        ew_send[t] = packed.astype(BF16)
        for side, dn in ((0, -1), (1, 1)):
            copy = pltpu.make_async_remote_copy(
                src_ref=ew_send.at[t],
                dst_ref=ew_recv.at[t, side],
                send_sem=ew_ssem.at[t, side],
                recv_sem=ew_rsem.at[t, side],
                device_id=at(0, dn),
                device_id_type=MESH,
            )
            copy.start()
            waits.append(copy)
        sent.extend(waits)
        if t == 0:
            send_to_all(lab_send, lab_recv, lab_ssem, lab_rsem)
        for r in range(1, ROWS - 1):
            state[2, r] = work[r] - half * (state[0, r + 1] - state[0, r - 1])
        if t == 1:
            all_of(lab_recv, lab_ssem, lab_rsem).wait_recv()
            make_locality(0)
        if t == 2:
            make_locality(1)
        for copy in waits:
            copy.wait_recv()
        south_h = ns_recv[t, 0, :MEMBERS].astype(F32) * south_live
        north_h = ns_recv[t, 1, :MEMBERS].astype(F32) * north_live
        south_v = (ns_recv[t, 0, MEMBERS:].astype(F32) + half * state[0, ROWS - 1]) * south_live
        north_v = (ns_recv[t, 1, MEMBERS:].astype(F32) - half * state[0, 0]) * north_live
        state[2, 0] = work[0] - half * (state[0, 1] - north_h)
        state[2, ROWS - 1] = work[ROWS - 1] - half * (south_h - state[0, ROWS - 2])
        merged = jnp.where(
            (tile_lane & 2) == 0, ew_recv[t, 1].astype(F32), ew_recv[t, 0].astype(F32)
        )
        for r in range(ROWS):
            h = state[0, r]
            far_h = lanes_of(merged, jnp.where(tile_lane == COLS - 1, 4 * r + 3, 4 * r))
            far_q = lanes_of(merged, jnp.where(tile_lane == COLS - 1, 4 * r + 2, 4 * r + 1))
            u = state[1, r] + edge * far_h
            state[1, r] = u
            far_u = far_q - edge * h
            left = jnp.where(tile_lane == 0, far_u, pltpu.roll(u, 1, 1))
            right = jnp.where(tile_lane == COLS - 1, far_u, pltpu.roll(u, COLS - 1, 1))
            below = south_v if r == ROWS - 1 else state[2, r + 1]
            above = north_v if r == 0 else state[2, r - 1]
            depth = half * still[r : r + 1, :]
            state[0, r] = h - depth * ((right - left) + (below - above))

    pick_lane = jnp.broadcast_to(lon_cols, (MEMBERS, COLS))

    def send_observations(b):
        prior = jnp.zeros((MEMBERS, COLS), F32)
        for r in range(ROWS):
            prior = jnp.where(lat_rows == r, lanes_of(state[0, r], pick_lane), prior)
        mean = jnp.sum(prior, axis=0, keepdims=True) / MEMBERS
        away = prior - mean
        total = jnp.sum(away * away, axis=0, keepdims=True) / (MEMBERS - 1) + var_row
        shift = (value_row - mean) / total
        spread = -1.0 / (jnp.sqrt(total) * (jnp.sqrt(var_row) + jnp.sqrt(total)))
        coefs = jnp.where(sub8 == 0, shift, jnp.where(sub8 == 1, spread, 0.0))
        rows = jnp.concatenate(
            [away, coefs, jnp.zeros((COLS - MEMBERS - 8, COLS), F32)], axis=0
        ).astype(BF16)
        tile = lax.dot_general(picks[b], rows, rows_to_lanes, preferred_element_type=F32)
        tile = tile.astype(BF16)
        obs_send[b] = tile
        obs_recv[b, PAIRS - 1] = tile
        send_to_all(obs_send.at[b], obs_recv.at[b], obs_ssem.at[b], obs_rsem.at[b])

    def make_dev(f):
        for r in range(ROWS):
            x = state[f, r]
            mean = jnp.sum(x, axis=0, keepdims=True) / MEMBERS
            dev[f, :, r * COLS : (r + 1) * COLS] = (x - mean).astype(BF16)

    def receive(b):
        all_of(obs_recv.at[b], obs_ssem.at[b], obs_rsem.at[b]).wait_recv()
        table = gather_rows(obs_recv.at[b], False)
        obs_dev = table.astype(BF16)[:, :MEMBERS]
        weights = table[:, MEMBERS : MEMBERS + 1] + table[:, MEMBERS + 1 : MEMBERS + 2] * table
        weights = weights.astype(BF16).astype(F32)
        weights = jnp.transpose(weights).astype(BF16)[:MEMBERS]
        return obs_dev, weights

    def update(b, f, obs_dev, weights, last):
        for pair in range(ROWS // 2):
            lanes = slice(2 * pair * COLS, 2 * (pair + 1) * COLS)
            cov = jnp.dot(obs_dev, dev[f, :, lanes], preferred_element_type=F32)
            taper = jnp.concatenate([loc[b, 2 * pair], loc[b, 2 * pair + 1]], axis=1)
            gain = (cov * taper).astype(BF16)
            step = jnp.dot(weights, gain, preferred_element_type=F32)
            for i in range(2):
                r = 2 * pair + i
                state[f, r] = state[f, r] + step[:, i * COLS : (i + 1) * COLS]
                if last:
                    copy = pltpu.make_async_copy(
                        state.at[f, r], out_hbm.at[f, :, r, :], out_sem.at[f, r]
                    )
                    copy.start()
                    outs.append(copy)

    outs = []
    send_observations(0)
    for f in range(3):
        make_dev(f)
    obs_dev, weights = receive(0)
    update(0, 0, obs_dev, weights, False)
    send_observations(1)
    for f in (1, 2):
        update(0, f, obs_dev, weights, False)
    for f in range(3):
        make_dev(f)
    obs_dev, weights = receive(1)
    for f in range(3):
        update(1, f, obs_dev, weights, True)

    for copy in sent:
        copy.wait_send()
    all_of(lab_recv, lab_ssem, lab_rsem).wait_send()
    for b in range(2):
        all_of(obs_recv.at[b], obs_ssem.at[b], obs_rsem.at[b]).wait_send()
    for copy in outs:
        copy.wait()


def per_device(n_lat, n_lon, *args):
    any_space = pl.BlockSpec(memory_space=pl.ANY)
    vmem = pltpu.VMEM
    dma = pltpu.SemaphoreType.DMA
    ints = vmem((SLOTS,), jnp.int32)
    floats = vmem((SLOTS,), F32)
    return pl.pallas_call(
        functools.partial(kernel, n_lat, n_lon),
        out_shape=jax.ShapeDtypeStruct(args[0].shape, F32),
        in_specs=[any_space] * len(args),
        out_specs=any_space,
        scratch_shapes=[
            vmem((3, ROWS, MEMBERS, COLS), F32),
            vmem((ROWS, COLS), F32),
            vmem((32,), F32),
            vmem((256,), F32),
            ints,
            ints,
            ints,
            ints,
            floats,
            floats,
            vmem((ROWS, MEMBERS, COLS), F32),
            vmem((SUB, 2, 2 * MEMBERS, COLS), BF16),
            vmem((SUB, 2, 2 * MEMBERS, COLS), BF16),
            vmem((SUB, MEMBERS, COLS), BF16),
            vmem((SUB, 2, MEMBERS, COLS), BF16),
            vmem((SLOTS, COLS), BF16),
            vmem((PAIRS, SLOTS, COLS), BF16),
            vmem((2, SLOTS, COLS), BF16),
            vmem((2, PAIRS, SLOTS, COLS), BF16),
            vmem((2, ROWS, OBS, COLS), F32),
            vmem((3, MEMBERS, ROWS * COLS), BF16),
            dma((9,)),
            dma((3, ROWS)),
            dma((3, ROWS)),
            dma((SUB, 2)),
            dma((SUB, 2)),
            dma((SUB, 2)),
            dma((SUB, 2)),
            dma,
            dma,
            dma((2,)),
            dma((2,)),
        ],
        compiler_params=pltpu.CompilerParams(
            collective_id=0, has_side_effects=True, vmem_limit_bytes=32 * 1024 * 1024
        ),
        name="window",
    )(*args)


def solution(mesh):
    return jax.shard_map(
        functools.partial(per_device, mesh.shape["lat"], mesh.shape["lon"]),
        mesh=mesh,
        in_specs=(
            P(None, None, "lat", "lon"),
            P("lat", "lon"),
            P(),
            P(),
            P(("lat", "lon")),
            P(("lat", "lon")),
            P(("lat", "lon")),
            P(("lat", "lon")),
            P(("lat", "lon")),
            P(("lat", "lon")),
        ),
        out_specs=P(None, None, "lat", "lon"),
        check_vma=False,
    )
```

```python
import functools

import jax
import jax.numpy as jnp
from jax import lax
from jax.experimental import pallas as pl
from jax.experimental.pallas import tpu as pltpu
from jax.sharding import PartitionSpec as P

REACH = 3
SUB = 4
MOST = 12
TIMESTEP = 0.5
CORIOLIS_FACTOR = 0.3

MEMBERS = 80
ROWS = 8
COLS = 128
SLOTS = 16
PAIRS = 21
OBS = 256
MESH = pl.DeviceIdType.MESH
F32 = jnp.float32
BF16 = jnp.bfloat16

BANDS = (-3, 3, -2, 2, -1, 1, 0)
SECTORS = (-1, 1, 0)
OFFSETS = [(dl, dn) for dl in BANDS for dn in SECTORS]


def lanes_of(x, index):
    return jnp.take_along_axis(x, index, axis=1, mode="promise_in_bounds")


def kernel(
    n_lat,
    n_lon,
    state_hbm,
    still_hbm,
    lat_hbm,
    lon_hbm,
    cell_hbm,
    reach_hbm,
    lreach_hbm,
    batch_hbm,
    value_hbm,
    var_hbm,
    out,
    state,
    still,
    lat_tab,
    lon_tab,
    cell,
    reach,
    lreach,
    batch,
    value,
    var,
    work,
    ns_send,
    ns_recv,
    ew_send,
    ew_recv,
    lab_send,
    lab_recv,
    obs_send,
    obs_recv,
    loc,
    dev,
    small_sem,
    state_sem,
    ns_ssem,
    ns_rsem,
    ew_ssem,
    ew_rsem,
    lab_ssem,
    lab_rsem,
    obs_ssem,
    obs_rsem,
):
    li = lax.axis_index("lat")
    lo = lax.axis_index("lon")

    def at(dl, dn):
        return (li + dl, lax.rem(lo + dn + n_lon, n_lon))

    def if_band(dl, act):
        if dl == 0:
            act()
        else:
            pl.when((li + dl >= 0) & (li + dl < n_lat))(act)

    def unless_band(dl, act):
        if dl != 0:
            pl.when((li + dl < 0) | (li + dl >= n_lat))(act)

    ins = []
    for i, (src, dst) in enumerate(
        (
            (still_hbm, still),
            (lat_hbm, lat_tab),
            (lon_hbm, lon_tab),
            (cell_hbm, cell),
            (reach_hbm, reach),
            (lreach_hbm, lreach),
            (batch_hbm, batch),
            (value_hbm, value),
            (var_hbm, var),
        )
    ):
        ins.append(pltpu.make_async_copy(src, dst, small_sem.at[i]))
        ins[-1].start()
    fields_in = []
    for f in range(3):
        for r in range(ROWS):
            copy = pltpu.make_async_copy(
                state_hbm.at[f, :, r, :], state.at[f, r], state_sem.at[f, r]
            )
            copy.start()
            fields_in.append(copy)

    barrier = pltpu.get_barrier_semaphore()
    for dl in BANDS:

        def greet(dl=dl):
            for dn in SECTORS:
                if (dl, dn) != (0, 0):
                    pl.semaphore_signal(barrier, inc=1, device_id=at(dl, dn), device_id_type=MESH)

        if_band(dl, greet)

    def met_all():
        def meet(bands):
            pl.semaphore_wait(barrier, 2 + 3 * bands)

        for k in range(REACH):
            pl.when(li == k)(lambda k=k: meet(REACH + k))
            pl.when(li == n_lat - 1 - k)(lambda k=k: meet(REACH + k))
        pl.when((li >= REACH) & (li < n_lat - REACH))(lambda: meet(2 * REACH))

    for g, dl in enumerate(BANDS):

        def clear(g=g, dl=dl):
            group = pl.ds(3 * g, 3)
            lab_recv[group] = jnp.zeros((3, SLOTS, COLS), BF16)
            for b in range(2):
                obs_recv[b, group] = jnp.zeros((3, SLOTS, COLS), BF16)
            if abs(dl) == 1:
                for t in range(SUB):
                    ns_recv[t, (1 - dl) // 2] = jnp.zeros((2 * MEMBERS, COLS), BF16)

        unless_band(dl, clear)

    tile_lane = lax.broadcasted_iota(jnp.int32, (MEMBERS, COLS), 1)
    row_lane = lax.broadcasted_iota(jnp.int32, (1, COLS), 1)

    for copy in ins:
        copy.wait()

    def as_row(ref, fill):
        x = ref[...].reshape(1, SLOTS)
        return jnp.concatenate([x, jnp.full((1, COLS - SLOTS), fill, x.dtype)], axis=1)

    cell_row = as_row(cell, 0)
    reach_row = as_row(reach, 0).astype(F32)
    lreach_row = as_row(lreach, 0).astype(F32)
    batch_row = as_row(batch, -1)
    value_row = as_row(value, 0.0)
    var_row = as_row(var, 1.0)
    lat_rows = cell_row // (COLS * n_lon) - li * ROWS
    lon_cols = lax.rem(cell_row, COLS * n_lon) - lo * COLS
    lat_rows = jnp.where(row_lane < SLOTS, lat_rows, 0)
    lon_cols = jnp.where(row_lane < SLOTS, lon_cols, 0)

    slot_of = lax.broadcasted_iota(jnp.int32, (SLOTS, COLS), 0)
    picks = []
    for b in range(2):
        live = (batch_row == b).astype(jnp.int32)
        upto = live
        for s in (1, 2, 4, 8):
            upto = upto + jnp.where(row_lane >= s, pltpu.roll(upto, s, 1), 0)
        rank = jnp.where(live == 1, upto - 1, -1)
        picks.append((slot_of == rank).astype(F32).astype(BF16))

    sub8 = lax.broadcasted_iota(jnp.int32, (8, COLS), 0)
    labels = jnp.where(
        sub8 == 0,
        lat_rows.astype(F32),
        jnp.where(
            sub8 == 1,
            lon_cols.astype(F32),
            jnp.where(sub8 == 2, reach_row, jnp.where(sub8 == 3, lreach_row, 0.0)),
        ),
    )
    zeros8 = jnp.zeros((8, COLS), F32)
    zeros_rest = jnp.zeros((COLS - 16, COLS), F32)
    rows_to_lanes = (((1,), (1,)), ((), ()))
    label_tile = 0.0
    for b in range(2):
        spread = jnp.concatenate([labels, zeros8] if b == 0 else [zeros8, labels], axis=0)
        spread = jnp.concatenate([spread, zeros_rest], axis=0).astype(BF16)
        label_tile = label_tile + lax.dot_general(
            picks[b], spread, rows_to_lanes, preferred_element_type=F32
        )
    label_tile = label_tile.astype(BF16)
    lab_send[...] = label_tile
    lab_recv[PAIRS - 1] = label_tile

    def send_to_all(src, land, ssem, rsem):
        for g, dl in enumerate(BANDS):

            def send(g=g, dl=dl):
                for dn in SECTORS:
                    if (dl, dn) != (0, 0):
                        pltpu.make_async_remote_copy(
                            src_ref=src,
                            dst_ref=land.at[OFFSETS.index((-dl, -dn))],
                            send_sem=ssem.at[g],
                            recv_sem=rsem.at[BANDS.index(-dl)],
                            device_id=at(dl, dn),
                            device_id_type=MESH,
                        ).start()

            if_band(dl, send)

    def for_all(land, ssem, rsem, act):
        for g, dl in enumerate(BANDS):

            def wait(g=g, dl=dl):
                block = land.at[pl.ds(3 * g, 2 if dl == 0 else 3)]
                act(
                    pltpu.make_async_remote_copy(
                        src_ref=block,
                        dst_ref=block,
                        send_sem=ssem.at[g],
                        recv_sem=rsem.at[g],
                        device_id=at(0, 1),
                        device_id_type=MESH,
                    )
                )

            if_band(dl, wait)

    def all_received(*refs):
        for_all(*refs, lambda copy: copy.wait_recv())

    def all_sent(*refs):
        for_all(*refs, lambda copy: copy.wait_send())

    def coriolis(r):
        row = (li * ROWS + r).astype(F32)
        cor = CORIOLIS_FACTOR * (2.0 * (row + 0.5) / (n_lat * ROWS) - 1.0)
        return TIMESTEP * cor

    def gather_rows(land, adjust):
        pieces = []
        for i in range(PAIRS):
            piece = land[i].astype(F32)[:MOST]
            if adjust:
                dl, dn = OFFSETS[i]
                inside = (li + dl >= 0) & (li + dl < n_lat)
                far = jnp.where(inside, -abs(dl), -100).astype(F32)
                lane = row_lane & 7
                piece = piece + (
                    jnp.where(lane == 0, float(dl * ROWS), 0.0)
                    + jnp.where(lane == 1, float(dn * COLS), 0.0)
                    + jnp.where(lane == 2, far, 0.0)
                    + jnp.where(lane == 3, float(-abs(dn)), 0.0)
                )
            pieces.append(piece)
        pieces.append(jnp.zeros((OBS - PAIRS * MOST, COLS), F32))
        return jnp.concatenate(pieces, axis=0)

    def make_locality(b):
        table = gather_rows(lab_recv, True)
        first = 8 * b
        rows = jnp.broadcast_to(table[:, first : first + 1], (OBS, COLS)).astype(jnp.int32)
        cols = jnp.broadcast_to(table[:, first + 1 : first + 2], (OBS, COLS)).astype(jnp.int32)
        within = (table[:, first + 2 : first + 3] >= 0) & (table[:, first + 3 : first + 4] >= 0)
        within = jnp.broadcast_to(jnp.where(within, 1.0 / (MEMBERS - 1), 0.0), (OBS, COLS))
        lane = lax.broadcasted_iota(jnp.int32, (OBS, COLS), 1)
        away = jnp.abs(lane - cols)
        lon_row = lon_tab[...].reshape(1, 2 * COLS)
        low = jnp.broadcast_to(lon_row[:, :COLS], (OBS, COLS))
        high = jnp.broadcast_to(lon_row[:, COLS:], (OBS, COLS))
        lon_w = jnp.where(
            away < COLS, lanes_of(low, away & (COLS - 1)), lanes_of(high, away & (COLS - 1))
        )
        lon_w = lon_w * within
        lat_row = lat_tab[...].reshape(1, 32)
        lat_row = jnp.concatenate([lat_row, jnp.zeros((1, COLS - 32), F32)], axis=1)
        lat_all = jnp.broadcast_to(lat_row, (OBS, COLS))
        for r in range(ROWS):
            loc[b, r] = lanes_of(lat_all, jnp.abs(rows - r)) * lon_w

    edge = jnp.where(
        tile_lane == 0, 0.5 * TIMESTEP, jnp.where(tile_lane == COLS - 1, -0.5 * TIMESTEP, 0.0)
    )
    north_live = (li > 0).astype(F32)
    south_live = (li < n_lat - 1).astype(F32)
    half = 0.5 * TIMESTEP
    sent = []

    for t in range(SUB):
        if t == 0:
            for copy in fields_in:
                copy.wait()
        for r in range(ROWS):
            work[r] = state[2, r] - coriolis(r) * state[1, r]
        ns_send[t, 0, :MEMBERS] = state[0, 0].astype(BF16)
        ns_send[t, 0, MEMBERS:] = (work[0] - half * state[0, 1]).astype(BF16)
        ns_send[t, 1, :MEMBERS] = state[0, ROWS - 1].astype(BF16)
        ns_send[t, 1, MEMBERS:] = (work[ROWS - 1] + half * state[0, ROWS - 2]).astype(BF16)
        if t == 0:
            met_all()
        copies = []
        for side, dl in ((0, -1), (1, 1)):
            copy = pltpu.make_async_remote_copy(
                src_ref=ns_send.at[t, side],
                dst_ref=ns_recv.at[t, side],
                send_sem=ns_ssem.at[t, side],
                recv_sem=ns_rsem.at[t, side],
                device_id=at(dl, 0),
                device_id_type=MESH,
            )
            if_band(dl, copy.start)
            copies.append((copy, dl, -dl))
        packed = jnp.zeros((MEMBERS, COLS), F32)
        for r in range(ROWS):
            h = state[0, r]
            left = pltpu.roll(h, 1, 1)
            right = pltpu.roll(h, COLS - 1, 1)
            z = state[1, r] + coriolis(r) * state[2, r]
            u = (
                z
                + jnp.where(tile_lane == 0, 0.0, half * left)
                - jnp.where(tile_lane == COLS - 1, 0.0, half * right)
            )
            state[1, r] = u
            mixed = jnp.where(tile_lane == COLS - 2, right, jnp.where(tile_lane == 1, left, u))
            packed = jnp.where((tile_lane >> 2) == r, pltpu.roll(mixed, 4 * r + 2, 1), packed)
        ew_send[t] = packed.astype(BF16)
        for side, dn in ((0, -1), (1, 1)):
            copy = pltpu.make_async_remote_copy(
                src_ref=ew_send.at[t],
                dst_ref=ew_recv.at[t, side],
                send_sem=ew_ssem.at[t, side],
                recv_sem=ew_rsem.at[t, side],
                device_id=at(0, dn),
                device_id_type=MESH,
            )
            copy.start()
            copies.append((copy, 0, 0))
        sent.extend(copies)
        if t == 0:
            send_to_all(lab_send, lab_recv, lab_ssem, lab_rsem)
        for r in range(1, ROWS - 1):
            state[2, r] = work[r] - half * (state[0, r + 1] - state[0, r - 1])
        if t == 1:
            all_received(lab_recv, lab_ssem, lab_rsem)
            make_locality(0)
        if t == 2:
            make_locality(1)
        for copy, _, dl in copies:
            if_band(dl, copy.wait_recv)
        south_h = ns_recv[t, 0, :MEMBERS].astype(F32) * south_live
        north_h = ns_recv[t, 1, :MEMBERS].astype(F32) * north_live
        south_v = (ns_recv[t, 0, MEMBERS:].astype(F32) + half * state[0, ROWS - 1]) * south_live
        north_v = (ns_recv[t, 1, MEMBERS:].astype(F32) - half * state[0, 0]) * north_live
        state[2, 0] = work[0] - half * (state[0, 1] - north_h)
        state[2, ROWS - 1] = work[ROWS - 1] - half * (south_h - state[0, ROWS - 2])
        merged = jnp.where(
            (tile_lane & 2) == 0, ew_recv[t, 1].astype(F32), ew_recv[t, 0].astype(F32)
        )
        for r in range(ROWS):
            h = state[0, r]
            far_h = lanes_of(merged, jnp.where(tile_lane == COLS - 1, 4 * r + 3, 4 * r))
            far_q = lanes_of(merged, jnp.where(tile_lane == COLS - 1, 4 * r + 2, 4 * r + 1))
            u = state[1, r] + edge * far_h
            state[1, r] = u
            far_u = far_q - edge * h
            left = jnp.where(tile_lane == 0, far_u, pltpu.roll(u, 1, 1))
            right = jnp.where(tile_lane == COLS - 1, far_u, pltpu.roll(u, COLS - 1, 1))
            below = south_v if r == ROWS - 1 else state[2, r + 1]
            above = north_v if r == 0 else state[2, r - 1]
            depth = half * still[r : r + 1, :]
            state[0, r] = h - depth * ((right - left) + (below - above))

    pick_lane = jnp.broadcast_to(lon_cols, (MEMBERS, COLS))

    def send_observations(b):
        prior = jnp.zeros((MEMBERS, COLS), F32)
        for r in range(ROWS):
            prior = jnp.where(lat_rows == r, lanes_of(state[0, r], pick_lane), prior)
        mean = jnp.sum(prior, axis=0, keepdims=True) / MEMBERS
        away = prior - mean
        total = jnp.sum(away * away, axis=0, keepdims=True) / (MEMBERS - 1) + var_row
        shift = (value_row - mean) / total
        spread = -1.0 / (jnp.sqrt(total) * (jnp.sqrt(var_row) + jnp.sqrt(total)))
        coefs = jnp.where(sub8 == 0, shift, jnp.where(sub8 == 1, spread, 0.0))
        rows = jnp.concatenate(
            [away, coefs, jnp.zeros((COLS - MEMBERS - 8, COLS), F32)], axis=0
        ).astype(BF16)
        tile = lax.dot_general(picks[b], rows, rows_to_lanes, preferred_element_type=F32)
        tile = tile.astype(BF16)
        obs_send[b] = tile
        obs_recv[b, PAIRS - 1] = tile
        send_to_all(obs_send.at[b], obs_recv.at[b], obs_ssem.at[b], obs_rsem.at[b])

    def make_dev(f):
        for r in range(ROWS):
            x = state[f, r]
            mean = jnp.sum(x, axis=0, keepdims=True) / MEMBERS
            dev[f, :, r * COLS : (r + 1) * COLS] = (x - mean).astype(BF16)

    def receive(b):
        all_received(obs_recv.at[b], obs_ssem.at[b], obs_rsem.at[b])
        table = gather_rows(obs_recv.at[b], False)
        obs_dev = table.astype(BF16)[:, :MEMBERS]
        weights = table[:, MEMBERS : MEMBERS + 1] + table[:, MEMBERS + 1 : MEMBERS + 2] * table
        weights = weights.astype(BF16).astype(F32)
        weights = jnp.transpose(weights).astype(BF16)[:MEMBERS]
        return obs_dev, weights

    def update(b, f, obs_dev, weights, last):
        for pair in range(ROWS // 2):
            lanes = slice(2 * pair * COLS, 2 * (pair + 1) * COLS)
            cov = jnp.dot(obs_dev, dev[f, :, lanes], preferred_element_type=F32)
            taper = jnp.concatenate([loc[b, 2 * pair], loc[b, 2 * pair + 1]], axis=1)
            gain = (cov * taper).astype(BF16)
            step = jnp.dot(weights, gain, preferred_element_type=F32)
            for i in range(2):
                r = 2 * pair + i
                new = state[f, r] + step[:, i * COLS : (i + 1) * COLS]
                if last:
                    out[f, :, r, :] = new
                else:
                    state[f, r] = new

    send_observations(0)
    for f in range(3):
        make_dev(f)
    obs_dev, weights = receive(0)
    update(0, 0, obs_dev, weights, False)
    send_observations(1)
    for f in (1, 2):
        update(0, f, obs_dev, weights, False)
    for f in range(3):
        make_dev(f)
    obs_dev, weights = receive(1)
    for f in range(3):
        update(1, f, obs_dev, weights, True)

    for copy, dl, _ in sent:
        if_band(dl, copy.wait_send)
    all_sent(lab_recv, lab_ssem, lab_rsem)
    for b in range(2):
        all_sent(obs_recv.at[b], obs_ssem.at[b], obs_rsem.at[b])


def per_device(n_lat, n_lon, *args):
    args = [pltpu.with_memory_space_constraint(arg, pltpu.HBM) for arg in args]
    vmem = pltpu.VMEM
    dma = pltpu.SemaphoreType.DMA
    ints = vmem((SLOTS,), jnp.int32)
    floats = vmem((SLOTS,), F32)
    return pl.pallas_call(
        functools.partial(kernel, n_lat, n_lon),
        out_shape=vmem(args[0].shape, F32),
        in_specs=[pl.BlockSpec(memory_space=pltpu.HBM)] * len(args),
        out_specs=pl.BlockSpec(memory_space=vmem),
        scratch_shapes=[
            vmem((3, ROWS, MEMBERS, COLS), F32),
            vmem((ROWS, COLS), F32),
            vmem((32,), F32),
            vmem((256,), F32),
            ints,
            ints,
            ints,
            ints,
            floats,
            floats,
            vmem((ROWS, MEMBERS, COLS), F32),
            vmem((SUB, 2, 2 * MEMBERS, COLS), BF16),
            vmem((SUB, 2, 2 * MEMBERS, COLS), BF16),
            vmem((SUB, MEMBERS, COLS), BF16),
            vmem((SUB, 2, MEMBERS, COLS), BF16),
            vmem((SLOTS, COLS), BF16),
            vmem((PAIRS, SLOTS, COLS), BF16),
            vmem((2, SLOTS, COLS), BF16),
            vmem((2, PAIRS, SLOTS, COLS), BF16),
            vmem((2, ROWS, OBS, COLS), F32),
            vmem((3, MEMBERS, ROWS * COLS), BF16),
            dma((9,)),
            dma((3, ROWS)),
            dma((SUB, 2)),
            dma((SUB, 2)),
            dma((SUB, 2)),
            dma((SUB, 2)),
            dma((len(BANDS),)),
            dma((len(BANDS),)),
            dma((2, len(BANDS))),
            dma((2, len(BANDS))),
        ],
        compiler_params=pltpu.CompilerParams(
            collective_id=0, has_side_effects=True, vmem_limit_bytes=60 * 1024 * 1024
        ),
        name="window",
    )(*args)


def solution(mesh):
    return jax.shard_map(
        functools.partial(per_device, mesh.shape["lat"], mesh.shape["lon"]),
        mesh=mesh,
        in_specs=(
            P(None, None, "lat", "lon"),
            P("lat", "lon"),
            P(),
            P(),
            P(("lat", "lon")),
            P(("lat", "lon")),
            P(("lat", "lon")),
            P(("lat", "lon")),
            P(("lat", "lon")),
            P(("lat", "lon")),
        ),
        out_specs=P(None, None, "lat", "lon"),
        check_vma=False,
    )
```

```python
import functools

import jax
import jax.numpy as jnp
from jax import lax
from jax.experimental import pallas as pl
from jax.experimental.pallas import tpu as pltpu
from jax.sharding import PartitionSpec as P

REACH = 3
SUB = 4
MOST = 12
TIMESTEP = 0.5
CORIOLIS_FACTOR = 0.3

MEMBERS = 80
ROWS = 8
COLS = 128
SLOTS = 16
PAIRS = 21
OBS = 256
MESH = pl.DeviceIdType.MESH
F32 = jnp.float32
BF16 = jnp.bfloat16

BANDS = (-3, 3, -2, 2, -1, 1, 0)
SECTORS = (-1, 1, 0)
OFFSETS = [(dl, dn) for dl in BANDS for dn in SECTORS]
SIDES = [(0, -1), (0, 1), (-1, -1), (-1, 1), (1, -1), (1, 1)]


def lanes_of(x, index):
    return jnp.take_along_axis(x, index, axis=1, mode="promise_in_bounds")


def kernel(
    n_lat,
    n_lon,
    state_hbm,
    still_hbm,
    lat_hbm,
    lon_hbm,
    cell_hbm,
    reach_hbm,
    lreach_hbm,
    batch_hbm,
    value_hbm,
    var_hbm,
    out,
    state,
    still,
    lat_tab,
    lon_tab,
    cell,
    reach,
    lreach,
    batch,
    value,
    var,
    work,
    outside,
    ns_send,
    ns_recv,
    ew_send,
    ew_recv,
    lab_send,
    lab_recv,
    obs_send,
    obs_recv,
    loc,
    dev,
    small_sem,
    state_sem,
    ns_ssem,
    ns_rsem,
    ew_ssem,
    ew_rsem,
    lab_ssem,
    lab_rsem,
    obs_ssem,
    obs_rsem,
):
    li = lax.axis_index("lat")
    lo = lax.axis_index("lon")

    def at(dl, dn):
        return (li + dl, lax.rem(lo + dn + n_lon, n_lon))

    def if_band(dl, act):
        if dl == 0:
            act()
        else:
            pl.when((li + dl >= 0) & (li + dl < n_lat))(act)

    def unless_band(dl, act):
        if dl != 0:
            pl.when((li + dl < 0) | (li + dl >= n_lat))(act)

    ins = []
    for i, (src, dst) in enumerate(
        (
            (still_hbm, still),
            (lat_hbm, lat_tab),
            (lon_hbm, lon_tab),
            (cell_hbm, cell),
            (reach_hbm, reach),
            (lreach_hbm, lreach),
            (batch_hbm, batch),
            (value_hbm, value),
            (var_hbm, var),
        )
    ):
        ins.append(pltpu.make_async_copy(src, dst, small_sem.at[i]))
        ins[-1].start()
    fields_in = []
    for f in range(3):
        for r in range(ROWS):
            copy = pltpu.make_async_copy(
                state_hbm.at[f, :, r, :], state.at[f, r], state_sem.at[f, r]
            )
            copy.start()
            fields_in.append(copy)

    barrier = pltpu.get_barrier_semaphore()
    for dl in BANDS:

        def greet(dl=dl):
            for dn in SECTORS:
                if (dl, dn) != (0, 0):
                    pl.semaphore_signal(barrier, inc=1, device_id=at(dl, dn), device_id_type=MESH)

        if_band(dl, greet)

    def met_all():
        def meet(bands):
            pl.semaphore_wait(barrier, 2 + 3 * bands)

        for k in range(REACH):
            pl.when(li == k)(lambda k=k: meet(REACH + k))
            pl.when(li == n_lat - 1 - k)(lambda k=k: meet(REACH + k))
        pl.when((li >= REACH) & (li < n_lat - REACH))(lambda: meet(2 * REACH))

    for g, dl in enumerate(BANDS):

        def clear(g=g, dl=dl):
            group = pl.ds(3 * g, 3)
            lab_recv[group] = jnp.zeros((3, SLOTS, COLS), BF16)
            for b in range(2):
                obs_recv[b, group] = jnp.zeros((3, SLOTS, COLS), BF16)
            if abs(dl) == 1:
                for t in range(SUB // 2):
                    ns_recv[t, (1 - dl) // 2] = jnp.zeros(ns_recv.shape[2:], BF16)
                    for dn in (-1, 1):
                        ew_recv[t, SIDES.index((-dl, dn))] = jnp.zeros(ew_recv.shape[2:], BF16)

        unless_band(dl, clear)

    tile_lane = lax.broadcasted_iota(jnp.int32, (MEMBERS, COLS), 1)
    row_lane = lax.broadcasted_iota(jnp.int32, (1, COLS), 1)

    for copy in ins:
        copy.wait()

    def as_row(ref, fill):
        x = ref[...].reshape(1, SLOTS)
        return jnp.concatenate([x, jnp.full((1, COLS - SLOTS), fill, x.dtype)], axis=1)

    cell_row = as_row(cell, 0)
    reach_row = as_row(reach, 0).astype(F32)
    lreach_row = as_row(lreach, 0).astype(F32)
    batch_row = as_row(batch, -1)
    value_row = as_row(value, 0.0)
    var_row = as_row(var, 1.0)
    lat_rows = cell_row // (COLS * n_lon) - li * ROWS
    lon_cols = lax.rem(cell_row, COLS * n_lon) - lo * COLS
    lat_rows = jnp.where(row_lane < SLOTS, lat_rows, 0)
    lon_cols = jnp.where(row_lane < SLOTS, lon_cols, 0)

    slot_of = lax.broadcasted_iota(jnp.int32, (SLOTS, COLS), 0)
    picks = []
    for b in range(2):
        live = (batch_row == b).astype(jnp.int32)
        upto = live
        for s in (1, 2, 4, 8):
            upto = upto + jnp.where(row_lane >= s, pltpu.roll(upto, s, 1), 0)
        rank = jnp.where(live == 1, upto - 1, -1)
        picks.append((slot_of == rank).astype(F32).astype(BF16))

    sub8 = lax.broadcasted_iota(jnp.int32, (8, COLS), 0)
    labels = jnp.where(
        sub8 == 0,
        lat_rows.astype(F32),
        jnp.where(
            sub8 == 1,
            lon_cols.astype(F32),
            jnp.where(sub8 == 2, reach_row, jnp.where(sub8 == 3, lreach_row, 0.0)),
        ),
    )
    zeros8 = jnp.zeros((8, COLS), F32)
    zeros_rest = jnp.zeros((COLS - 16, COLS), F32)
    rows_to_lanes = (((1,), (1,)), ((), ()))
    label_tile = 0.0
    for b in range(2):
        spread = jnp.concatenate([labels, zeros8] if b == 0 else [zeros8, labels], axis=0)
        spread = jnp.concatenate([spread, zeros_rest], axis=0).astype(BF16)
        label_tile = label_tile + lax.dot_general(
            picks[b], spread, rows_to_lanes, preferred_element_type=F32
        )
    label_tile = label_tile.astype(BF16)
    lab_send[...] = label_tile
    lab_recv[PAIRS - 1] = label_tile

    def send_to_all(src, land, ssem, rsem):
        for g, dl in enumerate(BANDS):

            def send(g=g, dl=dl):
                for dn in SECTORS:
                    if (dl, dn) != (0, 0):
                        pltpu.make_async_remote_copy(
                            src_ref=src,
                            dst_ref=land.at[OFFSETS.index((-dl, -dn))],
                            send_sem=ssem.at[g],
                            recv_sem=rsem.at[BANDS.index(-dl)],
                            device_id=at(dl, dn),
                            device_id_type=MESH,
                        ).start()

            if_band(dl, send)

    def for_all(land, ssem, rsem, act):
        for g, dl in enumerate(BANDS):

            def wait(g=g, dl=dl):
                block = land.at[pl.ds(3 * g, 2 if dl == 0 else 3)]
                act(
                    pltpu.make_async_remote_copy(
                        src_ref=block,
                        dst_ref=block,
                        send_sem=ssem.at[g],
                        recv_sem=rsem.at[g],
                        device_id=at(0, 1),
                        device_id_type=MESH,
                    )
                )

            if_band(dl, wait)

    def all_received(*refs):
        for_all(*refs, lambda copy: copy.wait_recv())

    def all_sent(*refs):
        for_all(*refs, lambda copy: copy.wait_send())

    def coriolis(r):
        row = (li * ROWS + r).astype(F32)
        cor = CORIOLIS_FACTOR * (2.0 * (row + 0.5) / (n_lat * ROWS) - 1.0)
        return TIMESTEP * cor

    def gather_rows(land, adjust):
        pieces = []
        for i in range(PAIRS):
            piece = land[i].astype(F32)[:MOST]
            if adjust:
                dl, dn = OFFSETS[i]
                inside = (li + dl >= 0) & (li + dl < n_lat)
                far = jnp.where(inside, -abs(dl), -100).astype(F32)
                lane = row_lane & 7
                piece = piece + (
                    jnp.where(lane == 0, float(dl * ROWS), 0.0)
                    + jnp.where(lane == 1, float(dn * COLS), 0.0)
                    + jnp.where(lane == 2, far, 0.0)
                    + jnp.where(lane == 3, float(-abs(dn)), 0.0)
                )
            pieces.append(piece)
        pieces.append(jnp.zeros((OBS - PAIRS * MOST, COLS), F32))
        return jnp.concatenate(pieces, axis=0)

    def make_locality(b):
        table = gather_rows(lab_recv, True)
        first = 8 * b
        rows = jnp.broadcast_to(table[:, first : first + 1], (OBS, COLS)).astype(jnp.int32)
        cols = jnp.broadcast_to(table[:, first + 1 : first + 2], (OBS, COLS)).astype(jnp.int32)
        within = (table[:, first + 2 : first + 3] >= 0) & (table[:, first + 3 : first + 4] >= 0)
        within = jnp.broadcast_to(jnp.where(within, 1.0 / (MEMBERS - 1), 0.0), (OBS, COLS))
        lane = lax.broadcasted_iota(jnp.int32, (OBS, COLS), 1)
        away = jnp.abs(lane - cols)
        lon_row = lon_tab[...].reshape(1, 2 * COLS)
        low = jnp.broadcast_to(lon_row[:, :COLS], (OBS, COLS))
        high = jnp.broadcast_to(lon_row[:, COLS:], (OBS, COLS))
        lon_w = jnp.where(
            away < COLS, lanes_of(low, away & (COLS - 1)), lanes_of(high, away & (COLS - 1))
        )
        lon_w = lon_w * within
        lat_row = lat_tab[...].reshape(1, 32)
        lat_row = jnp.concatenate([lat_row, jnp.zeros((1, COLS - 32), F32)], axis=1)
        lat_all = jnp.broadcast_to(lat_row, (OBS, COLS))
        for r in range(ROWS):
            loc[b, r] = lanes_of(lat_all, jnp.abs(rows - r)) * lon_w

    first = tile_lane == 0
    final = tile_lane == COLS - 1
    half = 0.5 * TIMESTEP
    edge = jnp.where(first, half, jnp.where(final, -half, 0.0))
    corner = jnp.where(
        first,
        1.0,
        jnp.where(final, -1.0, jnp.where((tile_lane == 1) | (tile_lane == COLS - 2), half, 0.0)),
    )
    north_live = (li > 0).astype(F32)
    south_live = (li < n_lat - 1).astype(F32)
    sent = []
    bottom = ROWS - 1

    def rolled(x, steps):
        return pltpu.roll(x, steps % COLS, 1)

    def depth(r):
        return half * still[r : r + 1, :]

    def apart(u, outside):
        left = jnp.where(first, outside, rolled(u, 1))
        right = jnp.where(final, outside, rolled(u, -1))
        return right - left

    def at_ends(x, a, b):
        return lanes_of(x, jnp.where(final, b, a))

    def at_four(x, a, b, c, d):
        near = jnp.where(tile_lane == 1, b, a)
        return lanes_of(x, jnp.where(final, d, jnp.where(tile_lane == COLS - 2, c, near)))

    def put(packed, place, x):
        return jnp.where((tile_lane >> 2) == place, rolled(x, 4 * place + 2), packed)

    def middle(ends, second_last, second):
        return jnp.where(
            tile_lane == COLS - 2, second_last, jnp.where(tile_lane == 1, second, ends)
        )

    for t in range(SUB // 2):
        if t == 0:
            for copy in fields_in:
                copy.wait()
        packed = jnp.zeros((MEMBERS, COLS), F32)

        def velocities(r, packed):
            h, u, v = state[0, r], state[1, r], state[2, r]
            left, right = rolled(h, 1), rolled(h, -1)
            turn = coriolis(r)
            new_u = u + turn * v + jnp.where(first, 0.0, half * left)
            new_u = new_u - jnp.where(final, 0.0, half * right)
            new_v = v - turn * u
            if r > 0:
                new_v = new_v + half * state[0, r - 1]
            if r < bottom:
                new_v = new_v - half * state[0, r + 1]
            state[1, r] = new_u
            state[2, r] = new_v
            return put(packed, r, middle(new_u, right, left))

        def heights(r):
            h = state[0, r]
            above = state[2, r - 1] if r > 0 else -half * north_live * h
            below = state[2, r + 1] if r < bottom else half * south_live * h
            around = apart(state[1, r], -edge * h) + (below - above)
            work[r] = h - depth(r) * around

        for r in (0, 1, 2, 7, 6, 5):
            packed = velocities(r, packed)
        for r in (0, 1, 7, 6):
            heights(r)
        for side, outer, inner, sign in ((0, 0, 1, -half), (1, bottom, bottom - 1, half)):
            second = state[2, outer] - coriolis(outer) * state[1, outer] + sign * work[inner]
            for i, x in enumerate((state[0, outer], state[2, outer], work[outer], second)):
                ns_send[t, side, i * MEMBERS : (i + 1) * MEMBERS] = x.astype(BF16)
            if t == 0:
                rows = jnp.concatenate(
                    [depth(outer), depth(inner), jnp.zeros((14, COLS), F32)], axis=0
                )
                ns_send[t, side, 4 * MEMBERS :] = rows.astype(BF16)
        if t == 0:
            met_all()
        copies = []
        for side, dl in ((0, -1), (1, 1)):
            rows = pl.ds(0, 4 * MEMBERS + (16 if t == 0 else 0))
            copy = pltpu.make_async_remote_copy(
                src_ref=ns_send.at[t, side, rows],
                dst_ref=ns_recv.at[t, side, rows],
                send_sem=ns_ssem.at[t, side],
                recv_sem=ns_rsem.at[t, side],
                device_id=at(dl, 0),
                device_id_type=MESH,
            )
            if_band(dl, copy.start)
            copies.append((copy, dl, -dl))
        for r in (3, 4):
            packed = velocities(r, packed)
        for r in (2, 3, 4, 5):
            heights(r)
        for r in range(ROWS):
            h = work[r]
            left, right = rolled(h, 1), rolled(h, -1)
            second = state[1, r] + coriolis(r) * state[2, r]
            second = second + jnp.where(final, half * left, -half * right)
            packed = put(packed, ROWS + r, middle(second, right, left))
        for i, x in enumerate((state[2, 0], state[2, bottom], state[0, 0], state[0, bottom])):
            packed = put(packed, 2 * ROWS + i, x)
        ew_send[t, :MEMBERS] = packed.astype(BF16)
        if t == 0:
            rows = jnp.concatenate([half * still[...], zeros8], axis=0)
            ew_send[t, MEMBERS:] = rows.astype(BF16)
        for i, (dl, dn) in enumerate(SIDES):
            rows = pl.ds(0, MEMBERS + (16 if t == 0 else 0))
            copy = pltpu.make_async_remote_copy(
                src_ref=ew_send.at[t, rows],
                dst_ref=ew_recv.at[t, i, rows],
                send_sem=ew_ssem.at[t, i],
                recv_sem=ew_rsem.at[t, i],
                device_id=at(dl, dn),
                device_id_type=MESH,
            )
            if_band(dl, copy.start)
            copies.append((copy, dl, -dl))
        sent.extend(copies)
        if t == 0:
            send_to_all(lab_send, lab_recv, lab_ssem, lab_rsem)
        if t == 1:
            all_received(lab_recv, lab_ssem, lab_rsem)
            make_locality(0)
        for copy, _, dl in copies:
            if_band(dl, copy.wait_recv)

        def from_ends(dl):
            west = ew_recv[t, SIDES.index((-dl, 1)), :MEMBERS].astype(F32)
            east = ew_recv[t, SIDES.index((-dl, -1)), :MEMBERS].astype(F32)
            return jnp.where((tile_lane & 2) == 0, west, east)

        def from_rows(side):
            x = [ns_recv[t, side, i * MEMBERS : (i + 1) * MEMBERS].astype(F32) for i in range(4)]
            rows = ns_recv[0, side, 4 * MEMBERS :].astype(F32)
            return x + [rows[0:1], rows[1:2]]

        south_h, south_v, south_h1, south_v2, south_d1, south_d2 = from_rows(0)
        north_h, north_v, north_h1, north_v2, north_d1, north_d2 = from_rows(1)
        ends_d = [
            ew_recv[0, SIDES.index((0, dn)), MEMBERS:].astype(F32)[:ROWS] for dn in (1, -1)
        ]
        end_lane = lax.broadcasted_iota(jnp.int32, (ROWS, COLS), 1)
        d1, d2 = (
            jnp.where(
                end_lane == 0,
                rolled(ends_d[0], k),
                jnp.where(end_lane == COLS - 1, rolled(ends_d[1], -k), 0.0),
            )
            for k in (1, 2)
        )
        corners = {}
        for name, dl, outer, inner, k in (("n", -1, bottom, bottom - 1, 1), ("s", 1, 0, 1, 0)):
            x = from_ends(dl)
            v, h = 4 * (2 * ROWS + k), 4 * (2 * ROWS + 2 + k)
            corners[name] = (
                at_ends(x, 4 * outer, 4 * outer + 3),
                at_four(x, 4 * outer + 1, 4 * outer, 4 * outer + 3, 4 * outer + 2),
                at_four(x, 4 * inner + 1, 4 * inner, 4 * inner + 3, 4 * inner + 2),
                at_ends(x, v + 1, v + 2),
                at_ends(x, v, v + 3),
                at_ends(x, h, h + 3),
            )
        n_h, n_row1, n_row2, n_v, n_v_in, n_h_in = corners["n"]
        s_h, s_row1, s_row2, s_v, s_v_in, s_h_in = corners["s"]

        top, low = state[0, 0], state[0, bottom]
        top_v = state[2, 0] + half * north_h
        low_v = state[2, bottom] - half * south_h
        state[2, 0] = top_v
        state[2, bottom] = low_v
        north_v = (north_v - half * top) * north_live
        south_v = (south_v + half * low) * south_live
        north_h1 = north_h1 - north_d1 * (top_v - half * north_h) + north_d1 * corner * n_row1
        south_h1 = south_h1 + south_d1 * (low_v + half * south_h) + south_d1 * corner * s_row1
        north_h1 = north_h1 * north_live
        south_h1 = south_h1 * south_live
        north_v2 = north_v2 - half * top * (1.0 - half * north_d2)
        north_v2 = north_v2 + half * north_d2 * corner * n_row2 - coriolis(-1) * edge * n_h
        south_v2 = south_v2 + half * low * (1.0 - half * south_d2)
        south_v2 = south_v2 - half * south_d2 * corner * s_row2 - coriolis(ROWS) * edge * s_h

        ends = from_ends(0)
        for r in range(ROWS):
            h = state[0, r]
            a, b = 4 * r, 4 * (ROWS + r)
            far_h = at_ends(ends, a, a + 3)
            far_u = at_ends(ends, a + 1, a + 2)
            far_h1 = at_ends(ends, b, b + 3)
            far_u2 = at_ends(ends, b + 1, b + 2)
            u = state[1, r] + edge * far_h
            state[1, r] = u
            above = state[2, r - 1] if r > 0 else north_v
            below = state[2, r + 1] if r < bottom else south_v
            work[r] = h - depth(r) * (apart(u, far_u - edge * h) + (below - above))
            end_d1, end_d2 = d1[r : r + 1], d2[r : r + 1]
            far_h1 = far_h1 - end_d1 * (edge * (1.0 / half) * u - half * far_h)
            far_u2 = far_u2 - edge * h * (1.0 - half * end_d2)
            if r == 0:
                far_h1 = far_h1 + end_d1 * n_v
                far_u2 = far_u2 + coriolis(r) * half * n_h + edge * end_d2 * n_v_in
            if r == 1:
                far_h1 = far_h1 + half * end_d1 * n_h
                far_u2 = far_u2 + half * edge * end_d2 * n_h_in
            if r == bottom - 1:
                far_h1 = far_h1 + half * end_d1 * s_h
                far_u2 = far_u2 + half * edge * end_d2 * s_h_in
            if r == bottom:
                far_h1 = far_h1 - end_d1 * s_v
                far_u2 = far_u2 - coriolis(r) * half * s_h - edge * end_d2 * s_v_in
            outside[0, r] = far_h1
            outside[1, r] = far_u2
        for r in range(ROWS):
            h, u, v = work[r], state[1, r], state[2, r]
            above = work[r - 1] if r > 0 else north_h1
            below = work[r + 1] if r < bottom else south_h1
            state[1, r] = u + coriolis(r) * v - half * apart(h, outside[0, r])
            state[2, r] = v - coriolis(r) * u - half * (below - above)
        north_v2 = (north_v2 - half * work[0]) * north_live
        south_v2 = (south_v2 + half * work[bottom]) * south_live
        for r in range(ROWS):
            h = work[r]
            above = state[2, r - 1] if r > 0 else north_v2
            below = state[2, r + 1] if r < bottom else south_v2
            around = apart(state[1, r], outside[1, r] - edge * h) + (below - above)
            state[0, r] = h - depth(r) * around

    pick_lane = jnp.broadcast_to(lon_cols, (MEMBERS, COLS))

    def send_observations(b):
        prior = jnp.zeros((MEMBERS, COLS), F32)
        for r in range(ROWS):
            prior = jnp.where(lat_rows == r, lanes_of(state[0, r], pick_lane), prior)
        mean = jnp.sum(prior, axis=0, keepdims=True) / MEMBERS
        away = prior - mean
        total = jnp.sum(away * away, axis=0, keepdims=True) / (MEMBERS - 1) + var_row
        shift = (value_row - mean) / total
        spread = -1.0 / (jnp.sqrt(total) * (jnp.sqrt(var_row) + jnp.sqrt(total)))
        coefs = jnp.where(sub8 == 0, shift, jnp.where(sub8 == 1, spread, 0.0))
        rows = jnp.concatenate(
            [away, coefs, jnp.zeros((COLS - MEMBERS - 8, COLS), F32)], axis=0
        ).astype(BF16)
        tile = lax.dot_general(picks[b], rows, rows_to_lanes, preferred_element_type=F32)
        tile = tile.astype(BF16)
        obs_send[b] = tile
        obs_recv[b, PAIRS - 1] = tile
        send_to_all(obs_send.at[b], obs_recv.at[b], obs_ssem.at[b], obs_rsem.at[b])

    def make_dev(f):
        for r in range(ROWS):
            x = state[f, r]
            mean = jnp.sum(x, axis=0, keepdims=True) / MEMBERS
            dev[f, :, r * COLS : (r + 1) * COLS] = (x - mean).astype(BF16)

    def receive(b):
        all_received(obs_recv.at[b], obs_ssem.at[b], obs_rsem.at[b])
        table = gather_rows(obs_recv.at[b], False)
        obs_dev = table.astype(BF16)[:, :MEMBERS]
        weights = table[:, MEMBERS : MEMBERS + 1] + table[:, MEMBERS + 1 : MEMBERS + 2] * table
        weights = weights.astype(BF16).astype(F32)
        weights = jnp.transpose(weights).astype(BF16)[:MEMBERS]
        return obs_dev, weights

    def update(b, f, obs_dev, weights, last):
        for pair in range(ROWS // 2):
            lanes = slice(2 * pair * COLS, 2 * (pair + 1) * COLS)
            cov = jnp.dot(obs_dev, dev[f, :, lanes], preferred_element_type=F32)
            taper = jnp.concatenate([loc[b, 2 * pair], loc[b, 2 * pair + 1]], axis=1)
            gain = (cov * taper).astype(BF16)
            step = jnp.dot(weights, gain, preferred_element_type=F32)
            for i in range(2):
                r = 2 * pair + i
                new = state[f, r] + step[:, i * COLS : (i + 1) * COLS]
                if last:
                    out[f, :, r, :] = new
                else:
                    state[f, r] = new

    send_observations(0)
    for f in range(3):
        make_dev(f)
    make_locality(1)
    obs_dev, weights = receive(0)
    update(0, 0, obs_dev, weights, False)
    send_observations(1)
    for f in (1, 2):
        update(0, f, obs_dev, weights, False)
    for f in range(3):
        make_dev(f)
    obs_dev, weights = receive(1)
    for f in range(3):
        update(1, f, obs_dev, weights, True)

    for copy, dl, _ in sent:
        if_band(dl, copy.wait_send)
    all_sent(lab_recv, lab_ssem, lab_rsem)
    for b in range(2):
        all_sent(obs_recv.at[b], obs_ssem.at[b], obs_rsem.at[b])


def per_device(n_lat, n_lon, *args):
    args = [pltpu.with_memory_space_constraint(arg, pltpu.HBM) for arg in args]
    vmem = pltpu.VMEM
    dma = pltpu.SemaphoreType.DMA
    ints = vmem((SLOTS,), jnp.int32)
    floats = vmem((SLOTS,), F32)
    return pl.pallas_call(
        functools.partial(kernel, n_lat, n_lon),
        out_shape=vmem(args[0].shape, F32),
        in_specs=[pl.BlockSpec(memory_space=pltpu.HBM)] * len(args),
        out_specs=pl.BlockSpec(memory_space=vmem),
        scratch_shapes=[
            vmem((3, ROWS, MEMBERS, COLS), F32),
            vmem((ROWS, COLS), F32),
            vmem((32,), F32),
            vmem((256,), F32),
            ints,
            ints,
            ints,
            ints,
            floats,
            floats,
            vmem((ROWS, MEMBERS, COLS), F32),
            vmem((2, ROWS, MEMBERS, COLS), F32),
            vmem((SUB // 2, 2, 4 * MEMBERS + 16, COLS), BF16),
            vmem((SUB // 2, 2, 4 * MEMBERS + 16, COLS), BF16),
            vmem((SUB // 2, MEMBERS + 16, COLS), BF16),
            vmem((SUB // 2, len(SIDES), MEMBERS + 16, COLS), BF16),
            vmem((SLOTS, COLS), BF16),
            vmem((PAIRS, SLOTS, COLS), BF16),
            vmem((2, SLOTS, COLS), BF16),
            vmem((2, PAIRS, SLOTS, COLS), BF16),
            vmem((2, ROWS, OBS, COLS), F32),
            vmem((3, MEMBERS, ROWS * COLS), BF16),
            dma((9,)),
            dma((3, ROWS)),
            dma((SUB // 2, 2)),
            dma((SUB // 2, 2)),
            dma((SUB // 2, len(SIDES))),
            dma((SUB // 2, len(SIDES))),
            dma((len(BANDS),)),
            dma((len(BANDS),)),
            dma((2, len(BANDS))),
            dma((2, len(BANDS))),
        ],
        compiler_params=pltpu.CompilerParams(
            collective_id=0, has_side_effects=True, vmem_limit_bytes=60 * 1024 * 1024
        ),
        name="window",
    )(*args)


def solution(mesh):
    return jax.shard_map(
        functools.partial(per_device, mesh.shape["lat"], mesh.shape["lon"]),
        mesh=mesh,
        in_specs=(
            P(None, None, "lat", "lon"),
            P("lat", "lon"),
            P(),
            P(),
            P(("lat", "lon")),
            P(("lat", "lon")),
            P(("lat", "lon")),
            P(("lat", "lon")),
            P(("lat", "lon")),
            P(("lat", "lon")),
        ),
        out_specs=P(None, None, "lat", "lon"),
        check_vma=False,
    )
```

```python
import functools

import jax
import jax.numpy as jnp
from jax import lax
from jax.experimental import pallas as pl
from jax.experimental.pallas import tpu as pltpu
from jax.sharding import PartitionSpec as P

REACH = 3
SUB = 4
MOST = 12
TIMESTEP = 0.5
CORIOLIS_FACTOR = 0.3

MEMBERS = 80
ROWS = 8
COLS = 128
SLOTS = 16
PAIRS = 21
OBS = 256
MESH = pl.DeviceIdType.MESH
F32 = jnp.float32
BF16 = jnp.bfloat16

BANDS = (-2, 2, -3, 3, -1, 1, 0)
SECTORS = (-1, 1, 0)
OFFSETS = [(dl, dn) for dl in BANDS for dn in SECTORS]
SIDES = [(0, -1), (0, 1)]
CORNERS = [(-1, -1), (-1, 1), (1, -1), (1, 1)]


def lanes_of(x, index):
    return jnp.take_along_axis(x, index, axis=1, mode="promise_in_bounds")


def kernel(
    n_lat,
    n_lon,
    state_hbm,
    still_hbm,
    lat_hbm,
    lon_hbm,
    cell_hbm,
    reach_hbm,
    lreach_hbm,
    batch_hbm,
    value_hbm,
    var_hbm,
    out,
    state,
    still,
    lat_tab,
    lon_tab,
    cell,
    reach,
    lreach,
    batch,
    value,
    var,
    work,
    outside,
    ns_send,
    ns_recv,
    ew_send,
    ew_recv,
    corner_send,
    corner_recv,
    lab_send,
    lab_recv,
    obs_send,
    obs_recv,
    loc,
    dev,
    small_sem,
    state_sem,
    ns_ssem,
    ns_rsem,
    ew_ssem,
    ew_rsem,
    corner_ssem,
    corner_rsem,
    lab_ssem,
    lab_rsem,
    obs_ssem,
    obs_rsem,
):
    li = lax.axis_index("lat")
    lo = lax.axis_index("lon")

    def at(dl, dn):
        return (li + dl, lax.rem(lo + dn + n_lon, n_lon))

    def if_band(dl, act):
        if dl == 0:
            act()
        else:
            pl.when((li + dl >= 0) & (li + dl < n_lat))(act)

    def unless_band(dl, act):
        if dl != 0:
            pl.when((li + dl < 0) | (li + dl >= n_lat))(act)

    ins = []
    for i, (src, dst) in enumerate(
        (
            (still_hbm, still),
            (lat_hbm, lat_tab),
            (lon_hbm, lon_tab),
            (cell_hbm, cell),
            (reach_hbm, reach),
            (lreach_hbm, lreach),
            (batch_hbm, batch),
            (value_hbm, value),
            (var_hbm, var),
        )
    ):
        ins.append(pltpu.make_async_copy(src, dst, small_sem.at[i]))
        ins[-1].start()
    rows_in = {}
    for r in (0, 1, 2, 7, 6, 5, 3, 4):
        rows_in[r] = [
            pltpu.make_async_copy(state_hbm.at[f, :, r, :], state.at[f, r], state_sem.at[f, r])
            for f in range(3)
        ]
        for copy in rows_in[r]:
            copy.start()

    barrier = pltpu.get_barrier_semaphore()
    for dl in (-1, 1, 0):

        def greet(dl=dl):
            for dn in SECTORS:
                if (dl, dn) != (0, 0):
                    pl.semaphore_signal(barrier, inc=1, device_id=at(dl, dn), device_id_type=MESH)

        if_band(dl, greet)

    def met_all():
        inner = (li > 0) & (li < n_lat - 1)
        pl.when(inner)(lambda: pl.semaphore_wait(barrier, 8))
        pl.when(jnp.logical_not(inner))(lambda: pl.semaphore_wait(barrier, 5))

    for g, dl in enumerate(BANDS):

        def clear(g=g, dl=dl):
            group = pl.ds(3 * g, 3)
            lab_recv[group] = jnp.zeros((3, SLOTS, COLS), BF16)
            for b in range(2):
                obs_recv[b, group] = jnp.zeros((3, SLOTS, COLS), BF16)
            if abs(dl) == 1:
                for t in range(SUB // 2):
                    ns_recv[t, (1 - dl) // 2] = jnp.zeros(ns_recv.shape[2:], BF16)
                    for dn in (-1, 1):
                        i = CORNERS.index((-dl, dn))
                        corner_recv[t, i] = jnp.zeros((SLOTS, COLS), BF16)

        unless_band(dl, clear)

    tile_lane = lax.broadcasted_iota(jnp.int32, (MEMBERS, COLS), 1)
    row_lane = lax.broadcasted_iota(jnp.int32, (1, COLS), 1)

    for copy in ins:
        copy.wait()

    def as_row(ref, fill):
        x = ref[...].reshape(1, SLOTS)
        return jnp.concatenate([x, jnp.full((1, COLS - SLOTS), fill, x.dtype)], axis=1)

    cell_row = as_row(cell, 0)
    reach_row = as_row(reach, 0).astype(F32)
    lreach_row = as_row(lreach, 0).astype(F32)
    batch_row = as_row(batch, -1)
    value_row = as_row(value, 0.0)
    var_row = as_row(var, 1.0)
    lat_rows = cell_row // (COLS * n_lon) - li * ROWS
    lon_cols = lax.rem(cell_row, COLS * n_lon) - lo * COLS
    lat_rows = jnp.where(row_lane < SLOTS, lat_rows, 0)
    lon_cols = jnp.where(row_lane < SLOTS, lon_cols, 0)

    slot_of = lax.broadcasted_iota(jnp.int32, (SLOTS, COLS), 0)
    slot_lane = lax.broadcasted_iota(jnp.int32, (SLOTS, COLS), 1)
    picks = []
    for b in range(2):
        live = (batch_row == b).astype(jnp.int32)
        upto = live
        for s in (1, 2, 4, 8):
            upto = upto + jnp.where(row_lane >= s, pltpu.roll(upto, s, 1), 0)
        rank = jnp.where(live == 1, upto - 1, -1)
        picks.append((slot_of == rank).astype(F32).astype(BF16))

    sub8 = lax.broadcasted_iota(jnp.int32, (8, COLS), 0)
    labels = jnp.where(
        sub8 == 0,
        lat_rows.astype(F32),
        jnp.where(
            sub8 == 1,
            lon_cols.astype(F32),
            jnp.where(sub8 == 2, reach_row, jnp.where(sub8 == 3, lreach_row, 0.0)),
        ),
    )
    zeros8 = jnp.zeros((8, COLS), F32)
    zeros_rest = jnp.zeros((COLS - 16, COLS), F32)
    rows_to_lanes = (((1,), (1,)), ((), ()))
    label_tile = 0.0
    for b in range(2):
        spread = jnp.concatenate([labels, zeros8] if b == 0 else [zeros8, labels], axis=0)
        spread = jnp.concatenate([spread, zeros_rest], axis=0).astype(BF16)
        label_tile = label_tile + lax.dot_general(
            picks[b], spread, rows_to_lanes, preferred_element_type=F32
        )
    label_tile = label_tile.astype(BF16)
    lab_send[...] = label_tile
    lab_recv[PAIRS - 1] = label_tile

    def send_to_all(src, land, ssem, rsem, bands=BANDS):
        for dl in bands:
            g = BANDS.index(dl)

            def send(g=g, dl=dl):
                for dn in SECTORS:
                    if (dl, dn) != (0, 0):
                        pltpu.make_async_remote_copy(
                            src_ref=src,
                            dst_ref=land.at[OFFSETS.index((-dl, -dn))],
                            send_sem=ssem.at[g],
                            recv_sem=rsem.at[BANDS.index(-dl)],
                            device_id=at(dl, dn),
                            device_id_type=MESH,
                        ).start()

            if_band(dl, send)

    def for_all(land, ssem, rsem, act):
        for g, dl in enumerate(BANDS):

            def wait(g=g, dl=dl):
                block = land.at[pl.ds(3 * g, 2 if dl == 0 else 3)]
                act(
                    pltpu.make_async_remote_copy(
                        src_ref=block,
                        dst_ref=block,
                        send_sem=ssem.at[g],
                        recv_sem=rsem.at[g],
                        device_id=at(0, 1),
                        device_id_type=MESH,
                    )
                )

            if_band(dl, wait)

    def all_received(*refs):
        for_all(*refs, lambda copy: copy.wait_recv())

    def all_sent(*refs):
        for_all(*refs, lambda copy: copy.wait_send())

    def coriolis(r):
        row = (li * ROWS + r).astype(F32)
        cor = CORIOLIS_FACTOR * (2.0 * (row + 0.5) / (n_lat * ROWS) - 1.0)
        return TIMESTEP * cor

    def gather_rows(land, adjust):
        pieces = []
        for i in range(PAIRS):
            piece = land[i].astype(F32)[:MOST]
            if adjust:
                dl, dn = OFFSETS[i]
                inside = (li + dl >= 0) & (li + dl < n_lat)
                far = jnp.where(inside, -abs(dl), -100).astype(F32)
                lane = row_lane & 7
                piece = piece + (
                    jnp.where(lane == 0, float(dl * ROWS), 0.0)
                    + jnp.where(lane == 1, float(dn * COLS), 0.0)
                    + jnp.where(lane == 2, far, 0.0)
                    + jnp.where(lane == 3, float(-abs(dn)), 0.0)
                )
            pieces.append(piece)
        pieces.append(jnp.zeros((OBS - PAIRS * MOST, COLS), F32))
        return jnp.concatenate(pieces, axis=0)

    def make_locality(b):
        table = gather_rows(lab_recv, True)
        first = 8 * b
        rows = jnp.broadcast_to(table[:, first : first + 1], (OBS, COLS)).astype(jnp.int32)
        cols = jnp.broadcast_to(table[:, first + 1 : first + 2], (OBS, COLS)).astype(jnp.int32)
        within = (table[:, first + 2 : first + 3] >= 0) & (table[:, first + 3 : first + 4] >= 0)
        within = jnp.broadcast_to(jnp.where(within, 1.0 / (MEMBERS - 1), 0.0), (OBS, COLS))
        lane = lax.broadcasted_iota(jnp.int32, (OBS, COLS), 1)
        away = jnp.abs(lane - cols)
        lon_row = lon_tab[...].reshape(1, 2 * COLS)
        low = jnp.broadcast_to(lon_row[:, :COLS], (OBS, COLS))
        high = jnp.broadcast_to(lon_row[:, COLS:], (OBS, COLS))
        lon_w = jnp.where(
            away < COLS, lanes_of(low, away & (COLS - 1)), lanes_of(high, away & (COLS - 1))
        )
        lon_w = lon_w * within
        lat_row = lat_tab[...].reshape(1, 32)
        lat_row = jnp.concatenate([lat_row, jnp.zeros((1, COLS - 32), F32)], axis=1)
        lat_all = jnp.broadcast_to(lat_row, (OBS, COLS))
        for r in range(ROWS):
            loc[b, r] = lanes_of(lat_all, jnp.abs(rows - r)) * lon_w

    first = tile_lane == 0
    final = tile_lane == COLS - 1
    half = 0.5 * TIMESTEP
    edge = jnp.where(first, half, jnp.where(final, -half, 0.0))
    corner = jnp.where(
        first,
        1.0,
        jnp.where(final, -1.0, jnp.where((tile_lane == 1) | (tile_lane == COLS - 2), half, 0.0)),
    )
    north_live = (li > 0).astype(F32)
    south_live = (li < n_lat - 1).astype(F32)
    sent = []
    bottom = ROWS - 1

    def rolled(x, steps):
        return pltpu.roll(x, steps % COLS, 1)

    def depth(r):
        return half * still[r : r + 1, :]

    def apart(u, outside):
        left = jnp.where(first, outside, rolled(u, 1))
        right = jnp.where(final, outside, rolled(u, -1))
        return right - left

    def at_ends(x, a, b):
        return lanes_of(x, jnp.where(final, b, a))

    def at_four(x, a, b, c, d):
        near = jnp.where(tile_lane == 1, b, a)
        return lanes_of(x, jnp.where(final, d, jnp.where(tile_lane == COLS - 2, c, near)))

    def put(packed, place, x):
        return jnp.where((tile_lane >> 2) == place, rolled(x, 4 * place + 2), packed)

    def middle(ends, second_last, second):
        return jnp.where(
            tile_lane == COLS - 2, second_last, jnp.where(tile_lane == 1, second, ends)
        )

    def labels_to(bands):
        send_to_all(lab_send, lab_recv, lab_ssem, lab_rsem, bands)

    for t in range(SUB // 2):
        packed = jnp.zeros((MEMBERS, COLS), F32)
        corner_tiles = [jnp.zeros((MEMBERS, COLS), F32) for _ in range(2)]

        def velocities(r):
            if t == 0:
                for q in (r - 1, r, r + 1):
                    for copy in rows_in.pop(q, ()):
                        copy.wait()
            h, u, v = state[0, r], state[1, r], state[2, r]
            left, right = rolled(h, 1), rolled(h, -1)
            turn = coriolis(r)
            new_u = u + turn * v + jnp.where(first, 0.0, half * left)
            new_u = new_u - jnp.where(final, 0.0, half * right)
            new_v = v - turn * u
            if r > 0:
                new_v = new_v + half * state[0, r - 1]
            if r < bottom:
                new_v = new_v - half * state[0, r + 1]
            state[1, r] = new_u
            state[2, r] = new_v
            return middle(new_u, right, left)

        def heights(r):
            h = state[0, r]
            above = state[2, r - 1] if r > 0 else -half * north_live * h
            below = state[2, r + 1] if r < bottom else half * south_live * h
            around = apart(state[1, r], -edge * h) + (below - above)
            work[r] = h - depth(r) * around

        for r in (0, 1, 2, 7, 6, 5):
            ends = velocities(r)
            packed = put(packed, r, ends)
            if r in (0, 1):
                corner_tiles[0] = put(corner_tiles[0], r, ends)
            if r in (bottom, bottom - 1):
                corner_tiles[1] = put(corner_tiles[1], bottom - r, ends)
        for side, outer in ((0, 0), (1, bottom)):
            tile = put(put(corner_tiles[side], 2, state[2, outer]), 3, state[0, outer])
            folded = tile[:SLOTS]
            for g in range(1, MEMBERS // SLOTS):
                part = rolled(tile[g * SLOTS : (g + 1) * SLOTS], 16 * g)
                folded = jnp.where((slot_lane >> 4) == g, part, folded)
            corner_send[t, side] = folded.astype(BF16)
        for r in (0, 1, 7, 6):
            heights(r)
        for side, outer, inner, sign in ((0, 0, 1, -half), (1, bottom, bottom - 1, half)):
            second = state[2, outer] - coriolis(outer) * state[1, outer] + sign * work[inner]
            for i, x in enumerate((state[0, outer], state[2, outer], work[outer], second)):
                ns_send[t, side, i * MEMBERS : (i + 1) * MEMBERS] = x.astype(BF16)
            if t == 0:
                rows = jnp.concatenate(
                    [depth(outer), depth(inner), jnp.zeros((14, COLS), F32)], axis=0
                )
                ns_send[t, side, 4 * MEMBERS :] = rows.astype(BF16)
        if t == 0:
            met_all()
        copies = []
        for i, (dl, dn) in enumerate(CORNERS):
            copy = pltpu.make_async_remote_copy(
                src_ref=corner_send.at[t, (1 + dl) // 2],
                dst_ref=corner_recv.at[t, i],
                send_sem=corner_ssem.at[t, i],
                recv_sem=corner_rsem.at[t, i],
                device_id=at(dl, dn),
                device_id_type=MESH,
            )
            if_band(dl, copy.start)
            copies.append((copy, dl, -dl))
        for side, dl in ((0, -1), (1, 1)):
            rows = pl.ds(0, 4 * MEMBERS + (16 if t == 0 else 0))
            copy = pltpu.make_async_remote_copy(
                src_ref=ns_send.at[t, side, rows],
                dst_ref=ns_recv.at[t, side, rows],
                send_sem=ns_ssem.at[t, side],
                recv_sem=ns_rsem.at[t, side],
                device_id=at(dl, 0),
                device_id_type=MESH,
            )
            if_band(dl, copy.start)
            copies.append((copy, dl, -dl))
        for r in (3, 4):
            packed = put(packed, r, velocities(r))
        for r in (2, 3, 4, 5):
            heights(r)
        for r in range(ROWS):
            h = work[r]
            left, right = rolled(h, 1), rolled(h, -1)
            second = state[1, r] + coriolis(r) * state[2, r]
            second = second + jnp.where(final, half * left, -half * right)
            packed = put(packed, ROWS + r, middle(second, right, left))
        ew_send[t, :MEMBERS] = packed.astype(BF16)
        if t == 0:
            rows = jnp.concatenate([half * still[...], zeros8], axis=0)
            ew_send[t, MEMBERS:] = rows.astype(BF16)
        for i, (dl, dn) in enumerate(SIDES):
            rows = pl.ds(0, MEMBERS + (16 if t == 0 else 0))
            copy = pltpu.make_async_remote_copy(
                src_ref=ew_send.at[t, rows],
                dst_ref=ew_recv.at[t, i, rows],
                send_sem=ew_ssem.at[t, i],
                recv_sem=ew_rsem.at[t, i],
                device_id=at(dl, dn),
                device_id_type=MESH,
            )
            if_band(dl, copy.start)
            copies.append((copy, dl, -dl))
        sent.extend(copies)
        labels_to((-1, 1, 0) if t == 0 else (-2, 2))
        for copy, _, dl in copies:
            if_band(dl, copy.wait_recv)
        if t == SUB // 2 - 1:
            labels_to((-3, 3))

        def merged(west, east):
            lane = lax.broadcasted_iota(jnp.int32, west.shape, 1)
            return jnp.where((lane & 2) == 0, west.astype(F32), east.astype(F32))

        def from_rows(side):
            x = [ns_recv[t, side, i * MEMBERS : (i + 1) * MEMBERS].astype(F32) for i in range(4)]
            rows = ns_recv[0, side, 4 * MEMBERS :].astype(F32)
            return x + [rows[0:1], rows[1:2]]

        south_h, south_v, south_h1, south_v2, south_d1, south_d2 = from_rows(0)
        north_h, north_v, north_h1, north_v2, north_d1, north_d2 = from_rows(1)
        ends_d = [
            ew_recv[0, SIDES.index((0, dn)), MEMBERS:].astype(F32)[:ROWS] for dn in (1, -1)
        ]
        end_lane = lax.broadcasted_iota(jnp.int32, (ROWS, COLS), 1)
        d1, d2 = (
            jnp.where(
                end_lane == 0,
                rolled(ends_d[0], k),
                jnp.where(end_lane == COLS - 1, rolled(ends_d[1], -k), 0.0),
            )
            for k in (1, 2)
        )
        corners = {}
        for name, dl in (("n", -1), ("s", 1)):
            folded = merged(
                *(corner_recv[t, CORNERS.index((-dl, dn))] for dn in (1, -1))
            )
            x = jnp.concatenate(
                [folded] + [rolled(folded, -16 * g) for g in range(1, MEMBERS // SLOTS)], axis=0
            )
            corners[name] = (
                at_ends(x, 0, 3),
                at_four(x, 1, 0, 3, 2),
                at_four(x, 5, 4, 7, 6),
                at_ends(x, 9, 10),
                at_ends(x, 8, 11),
                at_ends(x, 12, 15),
            )
        n_h, n_row1, n_row2, n_v, n_v_in, n_h_in = corners["n"]
        s_h, s_row1, s_row2, s_v, s_v_in, s_h_in = corners["s"]

        top, low = state[0, 0], state[0, bottom]
        top_v = state[2, 0] + half * north_h
        low_v = state[2, bottom] - half * south_h
        state[2, 0] = top_v
        state[2, bottom] = low_v
        north_v = (north_v - half * top) * north_live
        south_v = (south_v + half * low) * south_live
        north_h1 = north_h1 - north_d1 * (top_v - half * north_h) + north_d1 * corner * n_row1
        south_h1 = south_h1 + south_d1 * (low_v + half * south_h) + south_d1 * corner * s_row1
        north_h1 = north_h1 * north_live
        south_h1 = south_h1 * south_live
        north_v2 = north_v2 - half * top * (1.0 - half * north_d2)
        north_v2 = north_v2 + half * north_d2 * corner * n_row2 - coriolis(-1) * edge * n_h
        south_v2 = south_v2 + half * low * (1.0 - half * south_d2)
        south_v2 = south_v2 - half * south_d2 * corner * s_row2 - coriolis(ROWS) * edge * s_h

        ends = merged(*(ew_recv[t, SIDES.index((0, dn)), :MEMBERS] for dn in (1, -1)))
        for r in range(ROWS):
            h = state[0, r]
            a, b = 4 * r, 4 * (ROWS + r)
            far_h = at_ends(ends, a, a + 3)
            far_u = at_ends(ends, a + 1, a + 2)
            far_h1 = at_ends(ends, b, b + 3)
            far_u2 = at_ends(ends, b + 1, b + 2)
            u = state[1, r] + edge * far_h
            state[1, r] = u
            above = state[2, r - 1] if r > 0 else north_v
            below = state[2, r + 1] if r < bottom else south_v
            work[r] = h - depth(r) * (apart(u, far_u - edge * h) + (below - above))
            end_d1, end_d2 = d1[r : r + 1], d2[r : r + 1]
            far_h1 = far_h1 - end_d1 * (edge * (1.0 / half) * u - half * far_h)
            far_u2 = far_u2 - edge * h * (1.0 - half * end_d2)
            if r == 0:
                far_h1 = far_h1 + end_d1 * n_v
                far_u2 = far_u2 + coriolis(r) * half * n_h + edge * end_d2 * n_v_in
            if r == 1:
                far_h1 = far_h1 + half * end_d1 * n_h
                far_u2 = far_u2 + half * edge * end_d2 * n_h_in
            if r == bottom - 1:
                far_h1 = far_h1 + half * end_d1 * s_h
                far_u2 = far_u2 + half * edge * end_d2 * s_h_in
            if r == bottom:
                far_h1 = far_h1 - end_d1 * s_v
                far_u2 = far_u2 - coriolis(r) * half * s_h - edge * end_d2 * s_v_in
            outside[0, r] = far_h1
            outside[1, r] = far_u2
        for r in range(ROWS):
            h, u, v = work[r], state[1, r], state[2, r]
            above = work[r - 1] if r > 0 else north_h1
            below = work[r + 1] if r < bottom else south_h1
            state[1, r] = u + coriolis(r) * v - half * apart(h, outside[0, r])
            state[2, r] = v - coriolis(r) * u - half * (below - above)
        north_v2 = (north_v2 - half * work[0]) * north_live
        south_v2 = (south_v2 + half * work[bottom]) * south_live
        for r in range(ROWS):
            h = work[r]
            above = state[2, r - 1] if r > 0 else north_v2
            below = state[2, r + 1] if r < bottom else south_v2
            around = apart(state[1, r], outside[1, r] - edge * h) + (below - above)
            state[0, r] = h - depth(r) * around

    pick_lane = jnp.broadcast_to(lon_cols, (MEMBERS, COLS))

    def send_observations(b):
        prior = jnp.zeros((MEMBERS, COLS), F32)
        for r in range(ROWS):
            prior = jnp.where(lat_rows == r, lanes_of(state[0, r], pick_lane), prior)
        mean = jnp.sum(prior, axis=0, keepdims=True) / MEMBERS
        away = prior - mean
        total = jnp.sum(away * away, axis=0, keepdims=True) / (MEMBERS - 1) + var_row
        shift = (value_row - mean) / total
        spread = -1.0 / (jnp.sqrt(total) * (jnp.sqrt(var_row) + jnp.sqrt(total)))
        coefs = jnp.where(sub8 == 0, shift, jnp.where(sub8 == 1, spread, 0.0))
        rows = jnp.concatenate(
            [away, coefs, jnp.zeros((COLS - MEMBERS - 8, COLS), F32)], axis=0
        ).astype(BF16)
        tile = lax.dot_general(picks[b], rows, rows_to_lanes, preferred_element_type=F32)
        tile = tile.astype(BF16)
        obs_send[b] = tile
        obs_recv[b, PAIRS - 1] = tile
        send_to_all(obs_send.at[b], obs_recv.at[b], obs_ssem.at[b], obs_rsem.at[b])

    def make_dev(f):
        for r in range(ROWS):
            x = state[f, r]
            mean = jnp.sum(x, axis=0, keepdims=True) / MEMBERS
            dev[f, :, r * COLS : (r + 1) * COLS] = (x - mean).astype(BF16)

    def receive(b):
        all_received(obs_recv.at[b], obs_ssem.at[b], obs_rsem.at[b])
        table = gather_rows(obs_recv.at[b], False)
        obs_dev = table.astype(BF16)[:, :MEMBERS]
        weights = table[:, MEMBERS : MEMBERS + 1] + table[:, MEMBERS + 1 : MEMBERS + 2] * table
        weights = weights.astype(BF16).astype(F32)
        weights = jnp.transpose(weights).astype(BF16)[:MEMBERS]
        return obs_dev, weights

    def update(b, f, obs_dev, weights, last):
        for pair in range(ROWS // 2):
            lanes = slice(2 * pair * COLS, 2 * (pair + 1) * COLS)
            cov = jnp.dot(obs_dev, dev[f, :, lanes], preferred_element_type=F32)
            taper = jnp.concatenate([loc[b, 2 * pair], loc[b, 2 * pair + 1]], axis=1)
            gain = (cov * taper).astype(BF16)
            step = jnp.dot(weights, gain, preferred_element_type=F32)
            for i in range(2):
                r = 2 * pair + i
                new = state[f, r] + step[:, i * COLS : (i + 1) * COLS]
                if last:
                    out[f, :, r, :] = new
                else:
                    state[f, r] = new

    send_observations(0)
    for f in range(3):
        make_dev(f)
    all_received(lab_recv, lab_ssem, lab_rsem)
    make_locality(0)
    obs_dev, weights = receive(0)
    update(0, 0, obs_dev, weights, False)
    send_observations(1)
    for f in (1, 2):
        update(0, f, obs_dev, weights, False)
    for f in range(3):
        make_dev(f)
    make_locality(1)
    obs_dev, weights = receive(1)
    for f in range(3):
        update(1, f, obs_dev, weights, True)

    for copy, dl, _ in sent:
        if_band(dl, copy.wait_send)
    all_sent(lab_recv, lab_ssem, lab_rsem)
    for b in range(2):
        all_sent(obs_recv.at[b], obs_ssem.at[b], obs_rsem.at[b])


def per_device(n_lat, n_lon, *args):
    args = [pltpu.with_memory_space_constraint(arg, pltpu.HBM) for arg in args]
    vmem = pltpu.VMEM
    dma = pltpu.SemaphoreType.DMA
    ints = vmem((SLOTS,), jnp.int32)
    floats = vmem((SLOTS,), F32)
    return pl.pallas_call(
        functools.partial(kernel, n_lat, n_lon),
        out_shape=vmem(args[0].shape, F32),
        in_specs=[pl.BlockSpec(memory_space=pltpu.HBM)] * len(args),
        out_specs=pl.BlockSpec(memory_space=vmem),
        scratch_shapes=[
            vmem((3, ROWS, MEMBERS, COLS), F32),
            vmem((ROWS, COLS), F32),
            vmem((32,), F32),
            vmem((256,), F32),
            ints,
            ints,
            ints,
            ints,
            floats,
            floats,
            vmem((ROWS, MEMBERS, COLS), F32),
            vmem((2, ROWS, MEMBERS, COLS), F32),
            vmem((SUB // 2, 2, 4 * MEMBERS + 16, COLS), BF16),
            vmem((SUB // 2, 2, 4 * MEMBERS + 16, COLS), BF16),
            vmem((SUB // 2, MEMBERS + 16, COLS), BF16),
            vmem((SUB // 2, len(SIDES), MEMBERS + 16, COLS), BF16),
            vmem((SUB // 2, 2, SLOTS, COLS), BF16),
            vmem((SUB // 2, len(CORNERS), SLOTS, COLS), BF16),
            vmem((SLOTS, COLS), BF16),
            vmem((PAIRS, SLOTS, COLS), BF16),
            vmem((2, SLOTS, COLS), BF16),
            vmem((2, PAIRS, SLOTS, COLS), BF16),
            vmem((2, ROWS, OBS, COLS), F32),
            vmem((3, MEMBERS, ROWS * COLS), BF16),
            dma((9,)),
            dma((3, ROWS)),
            dma((SUB // 2, 2)),
            dma((SUB // 2, 2)),
            dma((SUB // 2, len(SIDES))),
            dma((SUB // 2, len(SIDES))),
            dma((SUB // 2, len(CORNERS))),
            dma((SUB // 2, len(CORNERS))),
            dma((len(BANDS),)),
            dma((len(BANDS),)),
            dma((2, len(BANDS))),
            dma((2, len(BANDS))),
        ],
        compiler_params=pltpu.CompilerParams(
            collective_id=0, has_side_effects=True, vmem_limit_bytes=60 * 1024 * 1024
        ),
        name="window",
    )(*args)


def solution(mesh):
    return jax.shard_map(
        functools.partial(per_device, mesh.shape["lat"], mesh.shape["lon"]),
        mesh=mesh,
        in_specs=(
            P(None, None, "lat", "lon"),
            P("lat", "lon"),
            P(),
            P(),
            P(("lat", "lon")),
            P(("lat", "lon")),
            P(("lat", "lon")),
            P(("lat", "lon")),
            P(("lat", "lon")),
            P(("lat", "lon")),
        ),
        out_specs=P(None, None, "lat", "lon"),
        check_vma=False,
    )
```

```python
import functools

import jax
import jax.numpy as jnp
from jax import lax
from jax.experimental import pallas as pl
from jax.experimental.pallas import tpu as pltpu
from jax.sharding import PartitionSpec as P

REACH = 3
SUB = 4
MOST = 12
TIMESTEP = 0.5
CORIOLIS_FACTOR = 0.3

MEMBERS = 80
ROWS = 8
COLS = 128
SLOTS = 16
PAIRS = 21
OBS = 256
MESH = pl.DeviceIdType.MESH
F32 = jnp.float32
BF16 = jnp.bfloat16

BANDS = (-2, 2, -3, 3, -1, 1, 0)
SECTORS = (-1, 1, 0)
OFFSETS = [(dl, dn) for dl in BANDS for dn in SECTORS]
SIDES = [(0, -1), (0, 1)]
CORNERS = [(-1, -1), (-1, 1), (1, -1), (1, 1)]


def lanes_of(x, index):
    return jnp.take_along_axis(x, index, axis=1, mode="promise_in_bounds")


def kernel(
    n_lat,
    n_lon,
    state_hbm,
    still_hbm,
    lat_hbm,
    lon_hbm,
    cell_hbm,
    reach_hbm,
    lreach_hbm,
    batch_hbm,
    value_hbm,
    var_hbm,
    out,
    state,
    still,
    lat_tab,
    lon_tab,
    cell,
    reach,
    lreach,
    batch,
    value,
    var,
    work,
    outside,
    ns_send,
    ns_recv,
    ew_send,
    ew_recv,
    corner_send,
    corner_recv,
    lab_send,
    lab_recv,
    obs_send,
    obs_recv,
    loc,
    dev,
    small_sem,
    state_sem,
    ns_ssem,
    ns_rsem,
    ew_ssem,
    ew_rsem,
    corner_ssem,
    corner_rsem,
    lab_ssem,
    lab_rsem,
    obs_ssem,
    obs_rsem,
):
    li = lax.axis_index("lat")
    lo = lax.axis_index("lon")

    def at(dl, dn):
        return (li + dl, lax.rem(lo + dn + n_lon, n_lon))

    def if_band(dl, act):
        if dl == 0:
            act()
        else:
            pl.when((li + dl >= 0) & (li + dl < n_lat))(act)

    def unless_band(dl, act):
        if dl != 0:
            pl.when((li + dl < 0) | (li + dl >= n_lat))(act)

    barrier = pltpu.get_barrier_semaphore()
    for dl in (-1, 1, 0):

        def greet(dl=dl):
            for dn in SECTORS:
                if (dl, dn) != (0, 0):
                    pl.semaphore_signal(barrier, inc=1, device_id=at(dl, dn), device_id_type=MESH)

        if_band(dl, greet)

    still_in = pltpu.make_async_copy(still_hbm, still, small_sem.at[8])
    still_in.start()
    rows_in = {}
    for r in (0, 7, 1, 6, 2, 5, 3, 4):
        rows_in[r] = [
            pltpu.make_async_copy(state_hbm.at[f, :, r, :], state.at[f, r], state_sem.at[f, r])
            for f in range(3)
        ]
        for copy in rows_in[r]:
            copy.start()

    ins = []
    for i, (src, dst) in enumerate(
        (
            (lat_hbm, lat_tab),
            (lon_hbm, lon_tab),
            (cell_hbm, cell),
            (reach_hbm, reach),
            (lreach_hbm, lreach),
            (batch_hbm, batch),
            (value_hbm, value),
            (var_hbm, var),
        )
    ):
        ins.append(pltpu.make_async_copy(src, dst, small_sem.at[i]))
        ins[-1].start()
    def met_all():
        inner = (li > 0) & (li < n_lat - 1)
        pl.when(inner)(lambda: pl.semaphore_wait(barrier, 8))
        pl.when(jnp.logical_not(inner))(lambda: pl.semaphore_wait(barrier, 5))

    for g, dl in enumerate(BANDS):

        def clear(g=g, dl=dl):
            group = pl.ds(3 * g, 3)
            lab_recv[group] = jnp.zeros((3, SLOTS, COLS), BF16)
            for b in range(2):
                obs_recv[b, group] = jnp.zeros((3, SLOTS, COLS), BF16)
            if abs(dl) == 1:
                for t in range(SUB // 2):
                    ns_recv[t, (1 - dl) // 2] = jnp.zeros(ns_recv.shape[2:], BF16)
                    for dn in (-1, 1):
                        i = CORNERS.index((-dl, dn))
                        corner_recv[t, i] = jnp.zeros((SLOTS, COLS), BF16)

        unless_band(dl, clear)

    tile_lane = lax.broadcasted_iota(jnp.int32, (MEMBERS, COLS), 1)
    row_lane = lax.broadcasted_iota(jnp.int32, (1, COLS), 1)

    def as_row(ref, fill):
        x = ref[...].reshape(1, SLOTS)
        return jnp.concatenate([x, jnp.full((1, COLS - SLOTS), fill, x.dtype)], axis=1)

    sub8 = lax.broadcasted_iota(jnp.int32, (8, COLS), 0)
    zeros8 = jnp.zeros((8, COLS), F32)
    zeros_rest = jnp.zeros((COLS - 16, COLS), F32)
    rows_to_lanes = (((1,), (1,)), ((), ()))
    slot_lane = lax.broadcasted_iota(jnp.int32, (SLOTS, COLS), 1)

    def observed():
        for copy in ins:
            copy.wait()

        cell_row = as_row(cell, 0)
        reach_row = as_row(reach, 0).astype(F32)
        lreach_row = as_row(lreach, 0).astype(F32)
        batch_row = as_row(batch, -1)
        value_row = as_row(value, 0.0)
        var_row = as_row(var, 1.0)
        lat_rows = cell_row // (COLS * n_lon) - li * ROWS
        lon_cols = lax.rem(cell_row, COLS * n_lon) - lo * COLS
        lat_rows = jnp.where(row_lane < SLOTS, lat_rows, 0)
        lon_cols = jnp.where(row_lane < SLOTS, lon_cols, 0)
        return lat_rows, lon_cols, reach_row, lreach_row, batch_row, value_row, var_row

    def make_labels():
        slot_of = lax.broadcasted_iota(jnp.int32, (SLOTS, COLS), 0)
        picks = []
        for b in range(2):
            live = (batch_row == b).astype(jnp.int32)
            upto = live
            for s in (1, 2, 4, 8):
                upto = upto + jnp.where(row_lane >= s, pltpu.roll(upto, s, 1), 0)
            rank = jnp.where(live == 1, upto - 1, -1)
            picks.append((slot_of == rank).astype(F32).astype(BF16))

        labels = jnp.where(
            sub8 == 0,
            lat_rows.astype(F32),
            jnp.where(
                sub8 == 1,
                lon_cols.astype(F32),
                jnp.where(sub8 == 2, reach_row, jnp.where(sub8 == 3, lreach_row, 0.0)),
            ),
        )
        label_tile = 0.0
        for b in range(2):
            spread = jnp.concatenate([labels, zeros8] if b == 0 else [zeros8, labels], axis=0)
            spread = jnp.concatenate([spread, zeros_rest], axis=0).astype(BF16)
            label_tile = label_tile + lax.dot_general(
                picks[b], spread, rows_to_lanes, preferred_element_type=F32
            )
        label_tile = label_tile.astype(BF16)
        lab_send[...] = label_tile
        lab_recv[PAIRS - 1] = label_tile
        return picks

    def send_to_all(src, land, ssem, rsem, bands=BANDS):
        for dl in bands:
            g = BANDS.index(dl)

            def send(g=g, dl=dl):
                for dn in SECTORS:
                    if (dl, dn) != (0, 0):
                        pltpu.make_async_remote_copy(
                            src_ref=src,
                            dst_ref=land.at[OFFSETS.index((-dl, -dn))],
                            send_sem=ssem.at[g],
                            recv_sem=rsem.at[BANDS.index(-dl)],
                            device_id=at(dl, dn),
                            device_id_type=MESH,
                        ).start()

            if_band(dl, send)

    def for_all(land, ssem, rsem, act):
        for g, dl in enumerate(BANDS):

            def wait(g=g, dl=dl):
                block = land.at[pl.ds(3 * g, 2 if dl == 0 else 3)]
                act(
                    pltpu.make_async_remote_copy(
                        src_ref=block,
                        dst_ref=block,
                        send_sem=ssem.at[g],
                        recv_sem=rsem.at[g],
                        device_id=at(0, 1),
                        device_id_type=MESH,
                    )
                )

            if_band(dl, wait)

    def all_received(*refs):
        for_all(*refs, lambda copy: copy.wait_recv())

    def all_sent(*refs):
        for_all(*refs, lambda copy: copy.wait_send())

    def coriolis(r):
        row = (li * ROWS + r).astype(F32)
        cor = CORIOLIS_FACTOR * (2.0 * (row + 0.5) / (n_lat * ROWS) - 1.0)
        return TIMESTEP * cor

    def gather_rows(land, adjust):
        pieces = []
        for i in range(PAIRS):
            piece = land[i].astype(F32)[:MOST]
            if adjust:
                dl, dn = OFFSETS[i]
                inside = (li + dl >= 0) & (li + dl < n_lat)
                far = jnp.where(inside, -abs(dl), -100).astype(F32)
                lane = row_lane & 7
                piece = piece + (
                    jnp.where(lane == 0, float(dl * ROWS), 0.0)
                    + jnp.where(lane == 1, float(dn * COLS), 0.0)
                    + jnp.where(lane == 2, far, 0.0)
                    + jnp.where(lane == 3, float(-abs(dn)), 0.0)
                )
            pieces.append(piece)
        pieces.append(jnp.zeros((OBS - PAIRS * MOST, COLS), F32))
        return jnp.concatenate(pieces, axis=0)

    def make_locality(b):
        table = gather_rows(lab_recv, True)
        first = 8 * b
        rows = jnp.broadcast_to(table[:, first : first + 1], (OBS, COLS)).astype(jnp.int32)
        cols = jnp.broadcast_to(table[:, first + 1 : first + 2], (OBS, COLS)).astype(jnp.int32)
        within = (table[:, first + 2 : first + 3] >= 0) & (table[:, first + 3 : first + 4] >= 0)
        within = jnp.broadcast_to(jnp.where(within, 1.0 / (MEMBERS - 1), 0.0), (OBS, COLS))
        lane = lax.broadcasted_iota(jnp.int32, (OBS, COLS), 1)
        away = jnp.abs(lane - cols)
        lon_row = lon_tab[...].reshape(1, 2 * COLS)
        low = jnp.broadcast_to(lon_row[:, :COLS], (OBS, COLS))
        high = jnp.broadcast_to(lon_row[:, COLS:], (OBS, COLS))
        lon_w = jnp.where(
            away < COLS, lanes_of(low, away & (COLS - 1)), lanes_of(high, away & (COLS - 1))
        )
        lon_w = lon_w * within
        lat_row = lat_tab[...].reshape(1, 32)
        lat_row = jnp.concatenate([lat_row, jnp.zeros((1, COLS - 32), F32)], axis=1)
        lat_all = jnp.broadcast_to(lat_row, (OBS, COLS))
        for r in range(ROWS):
            loc[b, r] = lanes_of(lat_all, jnp.abs(rows - r)) * lon_w

    first = tile_lane == 0
    final = tile_lane == COLS - 1
    half = 0.5 * TIMESTEP
    edge = jnp.where(first, half, jnp.where(final, -half, 0.0))
    corner = jnp.where(
        first,
        1.0,
        jnp.where(final, -1.0, jnp.where((tile_lane == 1) | (tile_lane == COLS - 2), half, 0.0)),
    )
    north_live = (li > 0).astype(F32)
    south_live = (li < n_lat - 1).astype(F32)
    sent = []
    bottom = ROWS - 1

    def rolled(x, steps):
        return pltpu.roll(x, steps % COLS, 1)

    def depth(r):
        return half * still[r : r + 1, :]

    def apart(u, outside):
        left = jnp.where(first, outside, rolled(u, 1))
        right = jnp.where(final, outside, rolled(u, -1))
        return right - left

    def at_ends(x, a, b):
        return lanes_of(x, jnp.where(final, b, a))

    def at_four(x, a, b, c, d):
        near = jnp.where(tile_lane == 1, b, a)
        return lanes_of(x, jnp.where(final, d, jnp.where(tile_lane == COLS - 2, c, near)))

    def put(packed, place, x):
        return jnp.where((tile_lane >> 2) == place, rolled(x, 4 * place + 2), packed)

    def middle(ends, second_last, second):
        return jnp.where(
            tile_lane == COLS - 2, second_last, jnp.where(tile_lane == 1, second, ends)
        )

    def labels_to(bands):
        send_to_all(lab_send, lab_recv, lab_ssem, lab_rsem, bands)

    pending = {}

    def finish(*which):
        for r in which:
            if r in pending:
                pending.pop(r)()

    for t in range(SUB // 2):
        packed = jnp.zeros((MEMBERS, COLS), F32)
        corner_tiles = [jnp.zeros((MEMBERS, COLS), F32) for _ in range(2)]
        copies = []
        rows_copies = []
        corner_copies = []

        def send(group, src, dst, ssem, rsem, dl, dn):
            copy = pltpu.make_async_remote_copy(
                src_ref=src,
                dst_ref=dst,
                send_sem=ssem,
                recv_sem=rsem,
                device_id=at(dl, dn),
                device_id_type=MESH,
            )
            if_band(dl, copy.start)
            group.append((copy, dl, -dl))

        def velocities(r):
            if t == 0:
                for q in (r - 1, r, r + 1):
                    for copy in rows_in.pop(q, ()):
                        copy.wait()
            h, u, v = state[0, r], state[1, r], state[2, r]
            left, right = rolled(h, 1), rolled(h, -1)
            turn = coriolis(r)
            new_u = u + turn * v + jnp.where(first, 0.0, half * left)
            new_u = new_u - jnp.where(final, 0.0, half * right)
            new_v = v - turn * u
            if r > 0:
                new_v = new_v + half * state[0, r - 1]
            if r < bottom:
                new_v = new_v - half * state[0, r + 1]
            state[1, r] = new_u
            state[2, r] = new_v
            return middle(new_u, right, left)

        def heights(r):
            h = state[0, r]
            above = state[2, r - 1] if r > 0 else -half * north_live * h
            below = state[2, r + 1] if r < bottom else half * south_live * h
            around = apart(state[1, r], -edge * h) + (below - above)
            work[r] = h - depth(r) * around

        def send_rows(part, rows):
            for side, dl in ((0, -1), (1, 1)):
                send(
                    rows_copies if part else copies,
                    ns_send.at[t, side, rows],
                    ns_recv.at[t, side, rows],
                    ns_ssem.at[t, side, part],
                    ns_rsem.at[t, side, part],
                    dl,
                    0,
                )

        finish(0, 1, 7, 6)
        for side, outer in ((0, 0), (1, bottom)):
            ends = velocities(outer)
            packed = put(packed, outer, ends)
            tile = put(corner_tiles[side], 0, ends)
            tile = put(tile, 2, state[2, outer])
            corner_tiles[side] = put(tile, 3, state[0, outer])
            ns_send[t, side, :MEMBERS] = state[0, outer].astype(BF16)
            ns_send[t, side, MEMBERS : 2 * MEMBERS] = state[2, outer].astype(BF16)
        if t == 0:
            met_all()
        send_rows(0, pl.ds(0, 2 * MEMBERS))
        finish(2, 5)
        for side, inner in ((0, 1), (1, bottom - 1)):
            ends = velocities(inner)
            packed = put(packed, inner, ends)
            tile = put(corner_tiles[side], 1, ends)
            folded = tile[:SLOTS]
            for g in range(1, MEMBERS // SLOTS):
                part = rolled(tile[g * SLOTS : (g + 1) * SLOTS], 16 * g)
                folded = jnp.where((slot_lane >> 4) == g, part, folded)
            corner_send[t, side] = folded.astype(BF16)
        for i, (dl, dn) in enumerate(CORNERS):
            send(
                corner_copies,
                corner_send.at[t, (1 + dl) // 2],
                corner_recv.at[t, i],
                corner_ssem.at[t, i],
                corner_rsem.at[t, i],
                dl,
                dn,
            )
        finish(3, 4)
        for r in (2, 5):
            packed = put(packed, r, velocities(r))
        if t == 0:
            still_in.wait()
        for r in (0, 1, 7, 6):
            heights(r)
        for side, outer, inner, sign in ((0, 0, 1, -half), (1, bottom, bottom - 1, half)):
            second = state[2, outer] - coriolis(outer) * state[1, outer] + sign * work[inner]
            ns_send[t, side, 2 * MEMBERS : 3 * MEMBERS] = work[outer].astype(BF16)
            ns_send[t, side, 3 * MEMBERS : 4 * MEMBERS] = second.astype(BF16)
            if t == 0:
                rows = jnp.concatenate(
                    [depth(outer), depth(inner), jnp.zeros((14, COLS), F32)], axis=0
                )
                ns_send[t, side, 4 * MEMBERS :] = rows.astype(BF16)
        send_rows(1, pl.ds(2 * MEMBERS, 2 * MEMBERS + (16 if t == 0 else 0)))
        for r in (3, 4):
            packed = put(packed, r, velocities(r))
        for r in (2, 3, 4, 5):
            heights(r)
        for r in range(ROWS):
            h = work[r]
            left, right = rolled(h, 1), rolled(h, -1)
            second = state[1, r] + coriolis(r) * state[2, r]
            second = second + jnp.where(final, half * left, -half * right)
            packed = put(packed, ROWS + r, middle(second, right, left))
        ew_send[t, :MEMBERS] = packed.astype(BF16)
        if t == 0:
            rows = jnp.concatenate([half * still[...], zeros8], axis=0)
            ew_send[t, MEMBERS:] = rows.astype(BF16)
        for i, (dl, dn) in enumerate(SIDES):
            rows = pl.ds(0, MEMBERS + (16 if t == 0 else 0))
            send(
                copies,
                ew_send.at[t, rows],
                ew_recv.at[t, i, rows],
                ew_ssem.at[t, i],
                ew_rsem.at[t, i],
                dl,
                dn,
            )
        sent.extend(copies + rows_copies + corner_copies)
        if t == 0:
            (lat_rows, lon_cols, reach_row, lreach_row, batch_row, value_row, var_row) = observed()
            picks = make_labels()
        labels_to((-1, 1, 0) if t == 0 else (-2, 2))
        for copy, _, dl in copies:
            if_band(dl, copy.wait_recv)

        def merged(west, east):
            lane = lax.broadcasted_iota(jnp.int32, west.shape, 1)
            return jnp.where((lane & 2) == 0, west.astype(F32), east.astype(F32))

        def from_rows(side, i):
            return ns_recv[t, side, i * MEMBERS : (i + 1) * MEMBERS].astype(F32)

        def edge_depths(side):
            rows = ns_recv[0, side, 4 * MEMBERS :].astype(F32)
            return rows[0:1], rows[1:2]

        south_h, south_v = from_rows(0, 0), from_rows(0, 1)
        north_h, north_v = from_rows(1, 0), from_rows(1, 1)
        ends_d = [
            ew_recv[0, SIDES.index((0, dn)), MEMBERS:].astype(F32)[:ROWS] for dn in (1, -1)
        ]
        end_lane = lax.broadcasted_iota(jnp.int32, (ROWS, COLS), 1)
        d1, d2 = (
            jnp.where(
                end_lane == 0,
                rolled(ends_d[0], k),
                jnp.where(end_lane == COLS - 1, rolled(ends_d[1], -k), 0.0),
            )
            for k in (1, 2)
        )
        top, low = state[0, 0], state[0, bottom]
        top_v = state[2, 0] + half * north_h
        low_v = state[2, bottom] - half * south_h
        state[2, 0] = top_v
        state[2, bottom] = low_v
        north_v = (north_v - half * top) * north_live
        south_v = (south_v + half * low) * south_live
        ends = merged(*(ew_recv[t, SIDES.index((0, dn)), :MEMBERS] for dn in (1, -1)))
        for r in range(ROWS):
            h = state[0, r]
            a, b = 4 * r, 4 * (ROWS + r)
            far_h = at_ends(ends, a, a + 3)
            far_u = at_ends(ends, a + 1, a + 2)
            far_h1 = at_ends(ends, b, b + 3)
            far_u2 = at_ends(ends, b + 1, b + 2)
            u = state[1, r] + edge * far_h
            state[1, r] = u
            above = state[2, r - 1] if r > 0 else north_v
            below = state[2, r + 1] if r < bottom else south_v
            work[r] = h - depth(r) * (apart(u, far_u - edge * h) + (below - above))
            end_d1, end_d2 = d1[r : r + 1], d2[r : r + 1]
            outside[0, r] = far_h1 - end_d1 * (edge * (1.0 / half) * u - half * far_h)
            outside[1, r] = far_u2 - edge * h * (1.0 - half * end_d2)

        for copy, _, dl in corner_copies + rows_copies:
            if_band(dl, copy.wait_recv)
        if t == SUB // 2 - 1:
            labels_to((-3, 3))
        corners = {}
        for name, dl in (("n", -1), ("s", 1)):
            folded = merged(
                *(corner_recv[t, CORNERS.index((-dl, dn))] for dn in (1, -1))
            )
            x = jnp.concatenate(
                [folded] + [rolled(folded, -16 * g) for g in range(1, MEMBERS // SLOTS)], axis=0
            )
            corners[name] = (
                at_ends(x, 0, 3),
                at_four(x, 1, 0, 3, 2),
                at_four(x, 5, 4, 7, 6),
                at_ends(x, 9, 10),
                at_ends(x, 8, 11),
                at_ends(x, 12, 15),
            )
        n_h, n_row1, n_row2, n_v, n_v_in, n_h_in = corners["n"]
        s_h, s_row1, s_row2, s_v, s_v_in, s_h_in = corners["s"]
        south_h1, south_v2 = from_rows(0, 2), from_rows(0, 3)
        north_h1, north_v2 = from_rows(1, 2), from_rows(1, 3)
        south_d1, south_d2 = edge_depths(0)
        north_d1, north_d2 = edge_depths(1)
        north_h1 = north_h1 - north_d1 * (top_v - half * north_h) + north_d1 * corner * n_row1
        south_h1 = south_h1 + south_d1 * (low_v + half * south_h) + south_d1 * corner * s_row1
        north_h1 = north_h1 * north_live
        south_h1 = south_h1 * south_live
        north_v2 = north_v2 - half * top * (1.0 - half * north_d2)
        north_v2 = north_v2 + half * north_d2 * corner * n_row2 - coriolis(-1) * edge * n_h
        south_v2 = south_v2 + half * low * (1.0 - half * south_d2)
        south_v2 = south_v2 - half * south_d2 * corner * s_row2 - coriolis(ROWS) * edge * s_h
        for r, far_h1, far_u2 in (
            (0, n_v, coriolis(0) * half * n_h + edge * d2[0:1] * n_v_in),
            (1, half * n_h, half * edge * d2[1:2] * n_h_in),
            (6, half * s_h, half * edge * d2[6:7] * s_h_in),
            (7, -s_v, -coriolis(7) * half * s_h - edge * d2[7:8] * s_v_in),
        ):
            outside[0, r] = outside[0, r] + d1[r : r + 1] * far_h1
            outside[1, r] = outside[1, r] + far_u2
        for r in (0, 1, 7, 6, 2, 5, 3, 4):
            h, u, v = work[r], state[1, r], state[2, r]
            above = work[r - 1] if r > 0 else north_h1
            below = work[r + 1] if r < bottom else south_h1
            state[1, r] = u + coriolis(r) * v - half * apart(h, outside[0, r])
            state[2, r] = v - coriolis(r) * u - half * (below - above)
        north_v2 = (north_v2 - half * work[0]) * north_live
        south_v2 = (south_v2 + half * work[bottom]) * south_live

        def last_height(r, north_v2, south_v2):
            h = work[r]
            above = state[2, r - 1] if r > 0 else north_v2
            below = state[2, r + 1] if r < bottom else south_v2
            around = apart(state[1, r], outside[1, r] - edge * h) + (below - above)
            state[0, r] = h - depth(r) * around

        for r in range(ROWS):
            pending[r] = functools.partial(last_height, r, north_v2, south_v2)

    finish(*range(ROWS))

    pick_lane = jnp.broadcast_to(lon_cols, (MEMBERS, COLS))

    def send_observations(b):
        prior = jnp.zeros((MEMBERS, COLS), F32)
        for r in range(ROWS):
            prior = jnp.where(lat_rows == r, lanes_of(state[0, r], pick_lane), prior)
        mean = jnp.sum(prior, axis=0, keepdims=True) / MEMBERS
        away = prior - mean
        total = jnp.sum(away * away, axis=0, keepdims=True) / (MEMBERS - 1) + var_row
        shift = (value_row - mean) / total
        spread = -1.0 / (jnp.sqrt(total) * (jnp.sqrt(var_row) + jnp.sqrt(total)))
        coefs = jnp.where(sub8 == 0, shift, jnp.where(sub8 == 1, spread, 0.0))
        rows = jnp.concatenate(
            [away, coefs, jnp.zeros((COLS - MEMBERS - 8, COLS), F32)], axis=0
        ).astype(BF16)
        tile = lax.dot_general(picks[b], rows, rows_to_lanes, preferred_element_type=F32)
        tile = tile.astype(BF16)
        obs_send[b] = tile
        obs_recv[b, PAIRS - 1] = tile
        send_to_all(obs_send.at[b], obs_recv.at[b], obs_ssem.at[b], obs_rsem.at[b])

    def make_dev(f):
        for r in range(ROWS):
            x = state[f, r]
            mean = jnp.sum(x, axis=0, keepdims=True) / MEMBERS
            dev[f, :, r * COLS : (r + 1) * COLS] = (x - mean).astype(BF16)

    def receive(b):
        all_received(obs_recv.at[b], obs_ssem.at[b], obs_rsem.at[b])
        table = gather_rows(obs_recv.at[b], False)
        obs_dev = table.astype(BF16)[:, :MEMBERS]
        weights = table[:, MEMBERS : MEMBERS + 1] + table[:, MEMBERS + 1 : MEMBERS + 2] * table
        weights = weights.astype(BF16).astype(F32)
        weights = jnp.transpose(weights).astype(BF16)[:MEMBERS]
        return obs_dev, weights

    def update(b, f, obs_dev, weights, last):
        for pair in range(ROWS // 2):
            lanes = slice(2 * pair * COLS, 2 * (pair + 1) * COLS)
            cov = jnp.dot(obs_dev, dev[f, :, lanes], preferred_element_type=F32)
            taper = jnp.concatenate([loc[b, 2 * pair], loc[b, 2 * pair + 1]], axis=1)
            gain = (cov * taper).astype(BF16)
            step = jnp.dot(weights, gain, preferred_element_type=F32)
            for i in range(2):
                r = 2 * pair + i
                new = state[f, r] + step[:, i * COLS : (i + 1) * COLS]
                if last:
                    out[f, :, r, :] = new
                else:
                    state[f, r] = new

    send_observations(0)
    for f in range(3):
        make_dev(f)
    all_received(lab_recv, lab_ssem, lab_rsem)
    make_locality(0)
    obs_dev, weights = receive(0)
    update(0, 0, obs_dev, weights, False)
    send_observations(1)
    for f in (1, 2):
        update(0, f, obs_dev, weights, False)
    for f in range(3):
        make_dev(f)
    make_locality(1)
    obs_dev, weights = receive(1)
    for f in range(3):
        update(1, f, obs_dev, weights, True)

    for copy, dl, _ in sent:
        if_band(dl, copy.wait_send)
    all_sent(lab_recv, lab_ssem, lab_rsem)
    for b in range(2):
        all_sent(obs_recv.at[b], obs_ssem.at[b], obs_rsem.at[b])


def per_device(n_lat, n_lon, *args):
    args = [pltpu.with_memory_space_constraint(arg, pltpu.HBM) for arg in args]
    vmem = pltpu.VMEM
    dma = pltpu.SemaphoreType.DMA
    ints = vmem((SLOTS,), jnp.int32)
    floats = vmem((SLOTS,), F32)
    return pl.pallas_call(
        functools.partial(kernel, n_lat, n_lon),
        out_shape=vmem(args[0].shape, F32),
        in_specs=[pl.BlockSpec(memory_space=pltpu.HBM)] * len(args),
        out_specs=pl.BlockSpec(memory_space=vmem),
        scratch_shapes=[
            vmem((3, ROWS, MEMBERS, COLS), F32),
            vmem((ROWS, COLS), F32),
            vmem((32,), F32),
            vmem((256,), F32),
            ints,
            ints,
            ints,
            ints,
            floats,
            floats,
            vmem((ROWS, MEMBERS, COLS), F32),
            vmem((2, ROWS, MEMBERS, COLS), F32),
            vmem((SUB // 2, 2, 4 * MEMBERS + 16, COLS), BF16),
            vmem((SUB // 2, 2, 4 * MEMBERS + 16, COLS), BF16),
            vmem((SUB // 2, MEMBERS + 16, COLS), BF16),
            vmem((SUB // 2, len(SIDES), MEMBERS + 16, COLS), BF16),
            vmem((SUB // 2, 2, SLOTS, COLS), BF16),
            vmem((SUB // 2, len(CORNERS), SLOTS, COLS), BF16),
            vmem((SLOTS, COLS), BF16),
            vmem((PAIRS, SLOTS, COLS), BF16),
            vmem((2, SLOTS, COLS), BF16),
            vmem((2, PAIRS, SLOTS, COLS), BF16),
            vmem((2, ROWS, OBS, COLS), F32),
            vmem((3, MEMBERS, ROWS * COLS), BF16),
            dma((9,)),
            dma((3, ROWS)),
            dma((SUB // 2, 2, 2)),
            dma((SUB // 2, 2, 2)),
            dma((SUB // 2, len(SIDES))),
            dma((SUB // 2, len(SIDES))),
            dma((SUB // 2, len(CORNERS))),
            dma((SUB // 2, len(CORNERS))),
            dma((len(BANDS),)),
            dma((len(BANDS),)),
            dma((2, len(BANDS))),
            dma((2, len(BANDS))),
        ],
        compiler_params=pltpu.CompilerParams(
            collective_id=0, has_side_effects=True, vmem_limit_bytes=60 * 1024 * 1024
        ),
        name="window",
    )(*args)


def solution(mesh):
    return jax.shard_map(
        functools.partial(per_device, mesh.shape["lat"], mesh.shape["lon"]),
        mesh=mesh,
        in_specs=(
            P(None, None, "lat", "lon"),
            P("lat", "lon"),
            P(),
            P(),
            P(("lat", "lon")),
            P(("lat", "lon")),
            P(("lat", "lon")),
            P(("lat", "lon")),
            P(("lat", "lon")),
            P(("lat", "lon")),
        ),
        out_specs=P(None, None, "lat", "lon"),
        check_vma=False,
    )
```

```python
import functools

import jax
import jax.numpy as jnp
from jax import lax
from jax.experimental import pallas as pl
from jax.experimental.pallas import tpu as pltpu
from jax.sharding import PartitionSpec as P

REACH = 3
SUB = 4
MOST = 12
TIMESTEP = 0.5
CORIOLIS_FACTOR = 0.3

MEMBERS = 80
ROWS = 8
COLS = 128
SLOTS = 16
PAIRS = 21
OBS = 256
MESH = pl.DeviceIdType.MESH
F32 = jnp.float32
BF16 = jnp.bfloat16

BANDS = (-2, 2, -3, 3, -1, 1, 0)
SECTORS = (-1, 1, 0)
OFFSETS = [(dl, dn) for dl in BANDS for dn in SECTORS]
SIDES = [(0, -1), (0, 1)]
CORNERS = [(-1, -1), (-1, 1), (1, -1), (1, 1)]


def lanes_of(x, index):
    return jnp.take_along_axis(x, index, axis=1, mode="promise_in_bounds")


def kernel(
    n_lat,
    n_lon,
    state_hbm,
    still_hbm,
    lat_hbm,
    lon_hbm,
    cell_hbm,
    reach_hbm,
    lreach_hbm,
    batch_hbm,
    value_hbm,
    var_hbm,
    out,
    state,
    still,
    lat_tab,
    lon_tab,
    cell,
    reach,
    lreach,
    batch,
    value,
    var,
    work,
    outside,
    ns_send,
    ns_recv,
    ew_send,
    ew_recv,
    corner_send,
    corner_recv,
    lab_send,
    lab_recv,
    obs_send,
    obs_recv,
    loc,
    dev,
    small_sem,
    state_sem,
    ns_ssem,
    ns_rsem,
    ew_ssem,
    ew_rsem,
    corner_ssem,
    corner_rsem,
    lab_ssem,
    lab_rsem,
    obs_ssem,
    obs_rsem,
):
    li = lax.axis_index("lat")
    lo = lax.axis_index("lon")

    def at(dl, dn):
        return (li + dl, lax.rem(lo + dn + n_lon, n_lon))

    def if_band(dl, act):
        if dl == 0:
            act()
        else:
            pl.when((li + dl >= 0) & (li + dl < n_lat))(act)

    def unless_band(dl, act):
        if dl != 0:
            pl.when((li + dl < 0) | (li + dl >= n_lat))(act)

    barrier = pltpu.get_barrier_semaphore()
    for dl in (-1, 1, 0):

        def greet(dl=dl):
            for dn in SECTORS:
                if (dl, dn) != (0, 0):
                    pl.semaphore_signal(barrier, inc=1, device_id=at(dl, dn), device_id_type=MESH)

        if_band(dl, greet)

    still_in = pltpu.make_async_copy(still_hbm, still, small_sem.at[8])
    still_in.start()
    rows_in = {}
    for r in (0, 7, 1, 6, 2, 5, 3, 4):
        rows_in[r] = [
            pltpu.make_async_copy(state_hbm.at[f, :, r, :], state.at[f, r], state_sem.at[f, r])
            for f in range(3)
        ]
        for copy in rows_in[r]:
            copy.start()

    ins = []
    for i, (src, dst) in enumerate(
        (
            (lat_hbm, lat_tab),
            (lon_hbm, lon_tab),
            (cell_hbm, cell),
            (reach_hbm, reach),
            (lreach_hbm, lreach),
            (batch_hbm, batch),
            (value_hbm, value),
            (var_hbm, var),
        )
    ):
        ins.append(pltpu.make_async_copy(src, dst, small_sem.at[i]))
        ins[-1].start()
    def met_all():
        inner = (li > 0) & (li < n_lat - 1)
        pl.when(inner)(lambda: pl.semaphore_wait(barrier, 8))
        pl.when(jnp.logical_not(inner))(lambda: pl.semaphore_wait(barrier, 5))

    for g, dl in enumerate(BANDS):

        def clear(g=g, dl=dl):
            group = pl.ds(3 * g, 3)
            lab_recv[group] = jnp.zeros((3, SLOTS, COLS), BF16)
            for b in range(2):
                obs_recv[b, group] = jnp.zeros((3, SLOTS, COLS), BF16)
            if abs(dl) == 1:
                for t in range(SUB // 2):
                    ns_recv[t, (1 - dl) // 2] = jnp.zeros(ns_recv.shape[2:], BF16)
                    for dn in (-1, 1):
                        i = CORNERS.index((-dl, dn))
                        corner_recv[t, i] = jnp.zeros((SLOTS, COLS), BF16)

        unless_band(dl, clear)

    tile_lane = lax.broadcasted_iota(jnp.int32, (MEMBERS, COLS), 1)
    row_lane = lax.broadcasted_iota(jnp.int32, (1, COLS), 1)

    def as_row(ref, fill):
        x = ref[...].reshape(1, SLOTS)
        return jnp.concatenate([x, jnp.full((1, COLS - SLOTS), fill, x.dtype)], axis=1)

    sub8 = lax.broadcasted_iota(jnp.int32, (8, COLS), 0)
    zeros8 = jnp.zeros((8, COLS), F32)
    zeros_rest = jnp.zeros((COLS - 16, COLS), F32)
    rows_to_lanes = (((1,), (1,)), ((), ()))
    slot_lane = lax.broadcasted_iota(jnp.int32, (SLOTS, COLS), 1)

    def observed():
        for copy in ins:
            copy.wait()

        cell_row = as_row(cell, 0)
        reach_row = as_row(reach, 0).astype(F32)
        lreach_row = as_row(lreach, 0).astype(F32)
        batch_row = as_row(batch, -1)
        value_row = as_row(value, 0.0)
        var_row = as_row(var, 1.0)
        lat_rows = cell_row // (COLS * n_lon) - li * ROWS
        lon_cols = lax.rem(cell_row, COLS * n_lon) - lo * COLS
        lat_rows = jnp.where(row_lane < SLOTS, lat_rows, 0)
        lon_cols = jnp.where(row_lane < SLOTS, lon_cols, 0)
        return lat_rows, lon_cols, reach_row, lreach_row, batch_row, value_row, var_row

    def make_labels():
        slot_of = lax.broadcasted_iota(jnp.int32, (SLOTS, COLS), 0)
        picks = []
        for b in range(2):
            live = (batch_row == b).astype(jnp.int32)
            upto = live
            for s in (1, 2, 4, 8):
                upto = upto + jnp.where(row_lane >= s, pltpu.roll(upto, s, 1), 0)
            rank = jnp.where(live == 1, upto - 1, -1)
            picks.append((slot_of == rank).astype(F32).astype(BF16))

        labels = jnp.where(
            sub8 == 0,
            lat_rows.astype(F32),
            jnp.where(
                sub8 == 1,
                lon_cols.astype(F32),
                jnp.where(sub8 == 2, reach_row, jnp.where(sub8 == 3, lreach_row, 0.0)),
            ),
        )
        label_tile = 0.0
        for b in range(2):
            spread = jnp.concatenate([labels, zeros8] if b == 0 else [zeros8, labels], axis=0)
            spread = jnp.concatenate([spread, zeros_rest], axis=0).astype(BF16)
            label_tile = label_tile + lax.dot_general(
                picks[b], spread, rows_to_lanes, preferred_element_type=F32
            )
        label_tile = label_tile.astype(BF16)
        lab_send[...] = label_tile
        lab_recv[PAIRS - 1] = label_tile
        return picks

    def send_to_all(src, land, ssem, rsem, bands=BANDS):
        for dl in bands:
            g = BANDS.index(dl)

            def send(g=g, dl=dl):
                for dn in SECTORS:
                    if (dl, dn) != (0, 0):
                        pltpu.make_async_remote_copy(
                            src_ref=src,
                            dst_ref=land.at[OFFSETS.index((-dl, -dn))],
                            send_sem=ssem.at[g],
                            recv_sem=rsem.at[BANDS.index(-dl)],
                            device_id=at(dl, dn),
                            device_id_type=MESH,
                        ).start()

            if_band(dl, send)

    def for_all(land, ssem, rsem, act):
        for g, dl in enumerate(BANDS):

            def wait(g=g, dl=dl):
                block = land.at[pl.ds(3 * g, 2 if dl == 0 else 3)]
                act(
                    pltpu.make_async_remote_copy(
                        src_ref=block,
                        dst_ref=block,
                        send_sem=ssem.at[g],
                        recv_sem=rsem.at[g],
                        device_id=at(0, 1),
                        device_id_type=MESH,
                    )
                )

            if_band(dl, wait)

    def all_received(*refs):
        for_all(*refs, lambda copy: copy.wait_recv())

    def all_sent(*refs):
        for_all(*refs, lambda copy: copy.wait_send())

    def coriolis(r):
        row = (li * ROWS + r).astype(F32)
        cor = CORIOLIS_FACTOR * (2.0 * (row + 0.5) / (n_lat * ROWS) - 1.0)
        return TIMESTEP * cor

    def gather_rows(land, adjust):
        pieces = []
        for i in range(PAIRS):
            piece = land[i].astype(F32)[:MOST]
            if adjust:
                dl, dn = OFFSETS[i]
                inside = (li + dl >= 0) & (li + dl < n_lat)
                far = jnp.where(inside, -abs(dl), -100).astype(F32)
                lane = row_lane & 7
                piece = piece + (
                    jnp.where(lane == 0, float(dl * ROWS), 0.0)
                    + jnp.where(lane == 1, float(dn * COLS), 0.0)
                    + jnp.where(lane == 2, far, 0.0)
                    + jnp.where(lane == 3, float(-abs(dn)), 0.0)
                )
            pieces.append(piece)
        pieces.append(jnp.zeros((OBS - PAIRS * MOST, COLS), F32))
        return jnp.concatenate(pieces, axis=0)

    def make_locality(b):
        table = gather_rows(lab_recv, True)
        first = 8 * b
        rows = jnp.broadcast_to(table[:, first : first + 1], (OBS, COLS)).astype(jnp.int32)
        cols = jnp.broadcast_to(table[:, first + 1 : first + 2], (OBS, COLS)).astype(jnp.int32)
        within = (table[:, first + 2 : first + 3] >= 0) & (table[:, first + 3 : first + 4] >= 0)
        within = jnp.broadcast_to(jnp.where(within, 1.0 / (MEMBERS - 1), 0.0), (OBS, COLS))
        lane = lax.broadcasted_iota(jnp.int32, (OBS, COLS), 1)
        away = jnp.abs(lane - cols)
        lon_row = lon_tab[...].reshape(1, 2 * COLS)
        low = jnp.broadcast_to(lon_row[:, :COLS], (OBS, COLS))
        high = jnp.broadcast_to(lon_row[:, COLS:], (OBS, COLS))
        lon_w = jnp.where(
            away < COLS, lanes_of(low, away & (COLS - 1)), lanes_of(high, away & (COLS - 1))
        )
        lon_w = lon_w * within
        lat_row = lat_tab[...].reshape(1, 32)
        lat_row = jnp.concatenate([lat_row, jnp.zeros((1, COLS - 32), F32)], axis=1)
        lat_all = jnp.broadcast_to(lat_row, (OBS, COLS))
        for r in range(ROWS):
            loc[b, r] = lanes_of(lat_all, jnp.abs(rows - r)) * lon_w

    first = tile_lane == 0
    final = tile_lane == COLS - 1
    half = 0.5 * TIMESTEP
    edge = jnp.where(first, half, jnp.where(final, -half, 0.0))
    corner = jnp.where(
        first,
        1.0,
        jnp.where(final, -1.0, jnp.where((tile_lane == 1) | (tile_lane == COLS - 2), half, 0.0)),
    )
    north_live = (li > 0).astype(F32)
    south_live = (li < n_lat - 1).astype(F32)
    sent = []
    bottom = ROWS - 1

    def rolled(x, steps):
        return pltpu.roll(x, steps % COLS, 1)

    def depth(r):
        return half * still[r : r + 1, :]

    def apart(u, outside):
        left = jnp.where(first, outside, rolled(u, 1))
        right = jnp.where(final, outside, rolled(u, -1))
        return right - left

    def at_ends(x, a, b):
        return lanes_of(x, jnp.where(final, b, a))

    def at_four(x, a, b, c, d):
        near = jnp.where(tile_lane == 1, b, a)
        return lanes_of(x, jnp.where(final, d, jnp.where(tile_lane == COLS - 2, c, near)))

    def put(packed, place, x):
        return jnp.where((tile_lane >> 2) == place, rolled(x, 4 * place + 2), packed)

    def middle(ends, second_last, second):
        return jnp.where(
            tile_lane == COLS - 2, second_last, jnp.where(tile_lane == 1, second, ends)
        )

    def labels_to(bands):
        send_to_all(lab_send, lab_recv, lab_ssem, lab_rsem, bands)

    pending = {}

    def finish(*which):
        for r in which:
            if r in pending:
                pending.pop(r)()

    for t in range(SUB // 2):
        packed = jnp.zeros((MEMBERS, COLS), F32)
        corner_tiles = [jnp.zeros((MEMBERS, COLS), F32) for _ in range(2)]
        copies = []
        rows_copies = []
        corner_copies = []

        def send(group, src, dst, ssem, rsem, dl, dn):
            copy = pltpu.make_async_remote_copy(
                src_ref=src,
                dst_ref=dst,
                send_sem=ssem,
                recv_sem=rsem,
                device_id=at(dl, dn),
                device_id_type=MESH,
            )
            if_band(dl, copy.start)
            group.append((copy, dl, -dl))

        def velocities(r):
            if t == 0:
                for q in (r - 1, r, r + 1):
                    for copy in rows_in.pop(q, ()):
                        copy.wait()
            h, u, v = state[0, r], state[1, r], state[2, r]
            left, right = rolled(h, 1), rolled(h, -1)
            turn = coriolis(r)
            new_u = u + turn * v + jnp.where(first, 0.0, half * left)
            new_u = new_u - jnp.where(final, 0.0, half * right)
            new_v = v - turn * u
            if r > 0:
                new_v = new_v + half * state[0, r - 1]
            if r < bottom:
                new_v = new_v - half * state[0, r + 1]
            state[1, r] = new_u
            state[2, r] = new_v
            return middle(new_u, right, left)

        def heights(r):
            h = state[0, r]
            above = state[2, r - 1] if r > 0 else -half * north_live * h
            below = state[2, r + 1] if r < bottom else half * south_live * h
            around = apart(state[1, r], -edge * h) + (below - above)
            work[r] = h - depth(r) * around

        def send_rows(part, rows):
            for side, dl in ((0, -1), (1, 1)):
                send(
                    rows_copies if part else copies,
                    ns_send.at[t, side, rows],
                    ns_recv.at[t, side, rows],
                    ns_ssem.at[t, side, part],
                    ns_rsem.at[t, side, part],
                    dl,
                    0,
                )

        finish(0, 1, 7, 6)
        for side, outer in ((0, 0), (1, bottom)):
            ends = velocities(outer)
            packed = put(packed, outer, ends)
            tile = put(corner_tiles[side], 0, ends)
            tile = put(tile, 2, state[2, outer])
            corner_tiles[side] = put(tile, 3, state[0, outer])
            ns_send[t, side, :MEMBERS] = state[0, outer].astype(BF16)
            ns_send[t, side, MEMBERS : 2 * MEMBERS] = state[2, outer].astype(BF16)
        if t == 0:
            met_all()
        send_rows(0, pl.ds(0, 2 * MEMBERS))
        finish(2, 5)
        for side, inner in ((0, 1), (1, bottom - 1)):
            ends = velocities(inner)
            packed = put(packed, inner, ends)
            tile = put(corner_tiles[side], 1, ends)
            folded = tile[:SLOTS]
            for g in range(1, MEMBERS // SLOTS):
                part = rolled(tile[g * SLOTS : (g + 1) * SLOTS], 16 * g)
                folded = jnp.where((slot_lane >> 4) == g, part, folded)
            corner_send[t, side] = folded.astype(BF16)
        for i, (dl, dn) in enumerate(CORNERS):
            send(
                corner_copies,
                corner_send.at[t, (1 + dl) // 2],
                corner_recv.at[t, i],
                corner_ssem.at[t, i],
                corner_rsem.at[t, i],
                dl,
                dn,
            )
        finish(3, 4)
        for r in (2, 5):
            packed = put(packed, r, velocities(r))
        if t == 0:
            still_in.wait()
        for r in (0, 1, 7, 6):
            heights(r)
        for side, outer, inner, sign in ((0, 0, 1, -half), (1, bottom, bottom - 1, half)):
            second = state[2, outer] - coriolis(outer) * state[1, outer] + sign * work[inner]
            ns_send[t, side, 2 * MEMBERS : 3 * MEMBERS] = work[outer].astype(BF16)
            ns_send[t, side, 3 * MEMBERS : 4 * MEMBERS] = second.astype(BF16)
            if t == 0:
                rows = jnp.concatenate(
                    [depth(outer), depth(inner), jnp.zeros((14, COLS), F32)], axis=0
                )
                ns_send[t, side, 4 * MEMBERS :] = rows.astype(BF16)
        send_rows(1, pl.ds(2 * MEMBERS, 2 * MEMBERS + (16 if t == 0 else 0)))
        for r in (3, 4):
            packed = put(packed, r, velocities(r))
        for r in (2, 3, 4, 5):
            heights(r)
        for r in range(ROWS):
            h = work[r]
            left, right = rolled(h, 1), rolled(h, -1)
            second = state[1, r] + coriolis(r) * state[2, r]
            second = second + jnp.where(final, half * left, -half * right)
            packed = put(packed, ROWS + r, middle(second, right, left))
        ew_send[t, :MEMBERS] = packed.astype(BF16)
        if t == 0:
            rows = jnp.concatenate([half * still[...], zeros8], axis=0)
            ew_send[t, MEMBERS:] = rows.astype(BF16)
        for i, (dl, dn) in enumerate(SIDES):
            rows = pl.ds(0, MEMBERS + (16 if t == 0 else 0))
            send(
                copies,
                ew_send.at[t, rows],
                ew_recv.at[t, i, rows],
                ew_ssem.at[t, i],
                ew_rsem.at[t, i],
                dl,
                dn,
            )
        sent.extend(copies + rows_copies + corner_copies)
        if t == 0:
            (lat_rows, lon_cols, reach_row, lreach_row, batch_row, value_row, var_row) = observed()
            picks = make_labels()
        labels_to((-1, 1, 0) if t == 0 else (-2, 2))
        for copy, _, dl in copies:
            if_band(dl, copy.wait_recv)

        def merged(west, east):
            lane = lax.broadcasted_iota(jnp.int32, west.shape, 1)
            return jnp.where((lane & 2) == 0, west.astype(F32), east.astype(F32))

        def from_rows(side, i):
            return ns_recv[t, side, i * MEMBERS : (i + 1) * MEMBERS].astype(F32)

        def edge_depths(side):
            rows = ns_recv[0, side, 4 * MEMBERS :].astype(F32)
            return rows[0:1], rows[1:2]

        south_h, south_v = from_rows(0, 0), from_rows(0, 1)
        north_h, north_v = from_rows(1, 0), from_rows(1, 1)
        ends_d = [
            ew_recv[0, SIDES.index((0, dn)), MEMBERS:].astype(F32)[:ROWS] for dn in (1, -1)
        ]
        end_lane = lax.broadcasted_iota(jnp.int32, (ROWS, COLS), 1)
        d1, d2 = (
            jnp.where(
                end_lane == 0,
                rolled(ends_d[0], k),
                jnp.where(end_lane == COLS - 1, rolled(ends_d[1], -k), 0.0),
            )
            for k in (1, 2)
        )
        top, low = state[0, 0], state[0, bottom]
        top_v = state[2, 0] + half * north_h
        low_v = state[2, bottom] - half * south_h
        state[2, 0] = top_v
        state[2, bottom] = low_v
        north_v = (north_v - half * top) * north_live
        south_v = (south_v + half * low) * south_live
        ends = merged(*(ew_recv[t, SIDES.index((0, dn)), :MEMBERS] for dn in (1, -1)))
        for r in range(ROWS):
            h = state[0, r]
            a, b = 4 * r, 4 * (ROWS + r)
            far_h = at_ends(ends, a, a + 3)
            far_u = at_ends(ends, a + 1, a + 2)
            far_h1 = at_ends(ends, b, b + 3)
            far_u2 = at_ends(ends, b + 1, b + 2)
            u = state[1, r] + edge * far_h
            state[1, r] = u
            above = state[2, r - 1] if r > 0 else north_v
            below = state[2, r + 1] if r < bottom else south_v
            work[r] = h - depth(r) * (apart(u, far_u - edge * h) + (below - above))
            end_d1, end_d2 = d1[r : r + 1], d2[r : r + 1]
            outside[0, r] = far_h1 - end_d1 * (edge * (1.0 / half) * u - half * far_h)
            outside[1, r] = far_u2 - edge * h * (1.0 - half * end_d2)

        for copy, _, dl in corner_copies + rows_copies:
            if_band(dl, copy.wait_recv)
        if t == SUB // 2 - 1:
            labels_to((-3, 3))
        corners = {}
        for name, dl in (("n", -1), ("s", 1)):
            folded = merged(
                *(corner_recv[t, CORNERS.index((-dl, dn))] for dn in (1, -1))
            )
            x = jnp.concatenate(
                [folded] + [rolled(folded, -16 * g) for g in range(1, MEMBERS // SLOTS)], axis=0
            )
            corners[name] = (
                at_ends(x, 0, 3),
                at_four(x, 1, 0, 3, 2),
                at_four(x, 5, 4, 7, 6),
                at_ends(x, 9, 10),
                at_ends(x, 8, 11),
                at_ends(x, 12, 15),
            )
        n_h, n_row1, n_row2, n_v, n_v_in, n_h_in = corners["n"]
        s_h, s_row1, s_row2, s_v, s_v_in, s_h_in = corners["s"]
        south_h1, south_v2 = from_rows(0, 2), from_rows(0, 3)
        north_h1, north_v2 = from_rows(1, 2), from_rows(1, 3)
        south_d1, south_d2 = edge_depths(0)
        north_d1, north_d2 = edge_depths(1)
        north_h1 = north_h1 - north_d1 * (top_v - half * north_h) + north_d1 * corner * n_row1
        south_h1 = south_h1 + south_d1 * (low_v + half * south_h) + south_d1 * corner * s_row1
        north_h1 = north_h1 * north_live
        south_h1 = south_h1 * south_live
        north_v2 = north_v2 - half * top * (1.0 - half * north_d2)
        north_v2 = north_v2 + half * north_d2 * corner * n_row2 - coriolis(-1) * edge * n_h
        south_v2 = south_v2 + half * low * (1.0 - half * south_d2)
        south_v2 = south_v2 - half * south_d2 * corner * s_row2 - coriolis(ROWS) * edge * s_h
        for r, far_h1, far_u2 in (
            (0, n_v, coriolis(0) * half * n_h + edge * d2[0:1] * n_v_in),
            (1, half * n_h, half * edge * d2[1:2] * n_h_in),
            (6, half * s_h, half * edge * d2[6:7] * s_h_in),
            (7, -s_v, -coriolis(7) * half * s_h - edge * d2[7:8] * s_v_in),
        ):
            outside[0, r] = outside[0, r] + d1[r : r + 1] * far_h1
            outside[1, r] = outside[1, r] + far_u2
        for r in (0, 1, 7, 6, 2, 5, 3, 4):
            h, u, v = work[r], state[1, r], state[2, r]
            above = work[r - 1] if r > 0 else north_h1
            below = work[r + 1] if r < bottom else south_h1
            state[1, r] = u + coriolis(r) * v - half * apart(h, outside[0, r])
            state[2, r] = v - coriolis(r) * u - half * (below - above)
        north_v2 = (north_v2 - half * work[0]) * north_live
        south_v2 = (south_v2 + half * work[bottom]) * south_live

        def last_height(r, north_v2, south_v2):
            h = work[r]
            above = state[2, r - 1] if r > 0 else north_v2
            below = state[2, r + 1] if r < bottom else south_v2
            around = apart(state[1, r], outside[1, r] - edge * h) + (below - above)
            state[0, r] = h - depth(r) * around

        for r in range(ROWS):
            pending[r] = functools.partial(last_height, r, north_v2, south_v2)

    finish(*range(ROWS))

    pick_lane = jnp.broadcast_to(lon_cols, (MEMBERS, COLS))

    def send_observations(b):
        prior = jnp.zeros((MEMBERS, COLS), F32)
        for r in range(ROWS):
            prior = jnp.where(lat_rows == r, lanes_of(state[0, r], pick_lane), prior)
        mean = jnp.sum(prior, axis=0, keepdims=True) / MEMBERS
        away = prior - mean
        total = jnp.sum(away * away, axis=0, keepdims=True) / (MEMBERS - 1) + var_row
        shift = (value_row - mean) / total
        spread = -1.0 / (jnp.sqrt(total) * (jnp.sqrt(var_row) + jnp.sqrt(total)))
        coefs = jnp.where(sub8 == 0, shift, jnp.where(sub8 == 1, spread, 0.0))
        rows = jnp.concatenate(
            [away, coefs, jnp.zeros((COLS - MEMBERS - 8, COLS), F32)], axis=0
        ).astype(BF16)
        tile = lax.dot_general(picks[b], rows, rows_to_lanes, preferred_element_type=F32)
        tile = tile.astype(BF16)
        obs_send[b] = tile
        obs_recv[b, PAIRS - 1] = tile
        send_to_all(obs_send.at[b], obs_recv.at[b], obs_ssem.at[b], obs_rsem.at[b])

    def make_dev(f):
        for r in range(ROWS):
            x = state[f, r]
            mean = jnp.sum(x, axis=0, keepdims=True) / MEMBERS
            dev[f, :, r * COLS : (r + 1) * COLS] = (x - mean).astype(BF16)

    def receive(b):
        all_received(obs_recv.at[b], obs_ssem.at[b], obs_rsem.at[b])
        table = gather_rows(obs_recv.at[b], False)
        obs_dev = table.astype(BF16)[:, :MEMBERS]
        weights = table[:, MEMBERS : MEMBERS + 1] + table[:, MEMBERS + 1 : MEMBERS + 2] * table
        weights = weights.astype(BF16).astype(F32)
        weights = jnp.transpose(weights).astype(BF16)[:MEMBERS]
        return obs_dev, weights

    def update(b, f, obs_dev, weights, last):
        gains = []
        for r in range(ROWS):
            lanes = slice(r * COLS, (r + 1) * COLS)
            cov = jnp.dot(obs_dev, dev[f, :, lanes], preferred_element_type=F32)
            gains.append((cov * loc[b, r]).astype(BF16))
        for pair in range(ROWS // 2):
            gain = jnp.concatenate(gains[2 * pair : 2 * pair + 2], axis=1)
            step = jnp.dot(weights, gain, preferred_element_type=F32)
            for i in range(2):
                r = 2 * pair + i
                new = state[f, r] + step[:, i * COLS : (i + 1) * COLS]
                if last:
                    out[f, :, r, :] = new
                else:
                    state[f, r] = new

    send_observations(0)
    for f in range(3):
        make_dev(f)
    all_received(lab_recv, lab_ssem, lab_rsem)
    make_locality(0)
    obs_dev, weights = receive(0)
    update(0, 0, obs_dev, weights, False)
    send_observations(1)
    for f in (1, 2):
        update(0, f, obs_dev, weights, False)
    for f in range(3):
        make_dev(f)
    make_locality(1)
    obs_dev, weights = receive(1)
    for f in range(3):
        update(1, f, obs_dev, weights, True)

    for copy, dl, _ in sent:
        if_band(dl, copy.wait_send)
    all_sent(lab_recv, lab_ssem, lab_rsem)
    for b in range(2):
        all_sent(obs_recv.at[b], obs_ssem.at[b], obs_rsem.at[b])


def per_device(n_lat, n_lon, *args):
    args = [pltpu.with_memory_space_constraint(arg, pltpu.HBM) for arg in args]
    vmem = pltpu.VMEM
    dma = pltpu.SemaphoreType.DMA
    ints = vmem((SLOTS,), jnp.int32)
    floats = vmem((SLOTS,), F32)
    return pl.pallas_call(
        functools.partial(kernel, n_lat, n_lon),
        out_shape=vmem(args[0].shape, F32),
        in_specs=[pl.BlockSpec(memory_space=pltpu.HBM)] * len(args),
        out_specs=pl.BlockSpec(memory_space=vmem),
        scratch_shapes=[
            vmem((3, ROWS, MEMBERS, COLS), F32),
            vmem((ROWS, COLS), F32),
            vmem((32,), F32),
            vmem((256,), F32),
            ints,
            ints,
            ints,
            ints,
            floats,
            floats,
            vmem((ROWS, MEMBERS, COLS), F32),
            vmem((2, ROWS, MEMBERS, COLS), F32),
            vmem((SUB // 2, 2, 4 * MEMBERS + 16, COLS), BF16),
            vmem((SUB // 2, 2, 4 * MEMBERS + 16, COLS), BF16),
            vmem((SUB // 2, MEMBERS + 16, COLS), BF16),
            vmem((SUB // 2, len(SIDES), MEMBERS + 16, COLS), BF16),
            vmem((SUB // 2, 2, SLOTS, COLS), BF16),
            vmem((SUB // 2, len(CORNERS), SLOTS, COLS), BF16),
            vmem((SLOTS, COLS), BF16),
            vmem((PAIRS, SLOTS, COLS), BF16),
            vmem((2, SLOTS, COLS), BF16),
            vmem((2, PAIRS, SLOTS, COLS), BF16),
            vmem((2, ROWS, OBS, COLS), F32),
            vmem((3, MEMBERS, ROWS * COLS), BF16),
            dma((9,)),
            dma((3, ROWS)),
            dma((SUB // 2, 2, 2)),
            dma((SUB // 2, 2, 2)),
            dma((SUB // 2, len(SIDES))),
            dma((SUB // 2, len(SIDES))),
            dma((SUB // 2, len(CORNERS))),
            dma((SUB // 2, len(CORNERS))),
            dma((len(BANDS),)),
            dma((len(BANDS),)),
            dma((2, len(BANDS))),
            dma((2, len(BANDS))),
        ],
        compiler_params=pltpu.CompilerParams(
            collective_id=0, has_side_effects=True, vmem_limit_bytes=60 * 1024 * 1024
        ),
        name="window",
    )(*args)


def solution(mesh):
    return jax.shard_map(
        functools.partial(per_device, mesh.shape["lat"], mesh.shape["lon"]),
        mesh=mesh,
        in_specs=(
            P(None, None, "lat", "lon"),
            P("lat", "lon"),
            P(),
            P(),
            P(("lat", "lon")),
            P(("lat", "lon")),
            P(("lat", "lon")),
            P(("lat", "lon")),
            P(("lat", "lon")),
            P(("lat", "lon")),
        ),
        out_specs=P(None, None, "lat", "lon"),
        check_vma=False,
    )
```

```python
import functools

import jax
import jax.numpy as jnp
from jax import lax
from jax.experimental import pallas as pl
from jax.experimental.pallas import tpu as pltpu
from jax.sharding import PartitionSpec as P

REACH = 3
SUB = 4
MOST = 12
TIMESTEP = 0.5
CORIOLIS_FACTOR = 0.3

MEMBERS = 80
ROWS = 8
COLS = 128
SLOTS = 16
PAIRS = 21
OBS = 256
MESH = pl.DeviceIdType.MESH
F32 = jnp.float32
BF16 = jnp.bfloat16

BANDS = (-2, 2, -3, 3, -1, 1, 0)
SECTORS = (-1, 1, 0)
OFFSETS = [(dl, dn) for dl in BANDS for dn in SECTORS]
SIDES = [(0, -1), (0, 1)]
CORNERS = [(-1, -1), (-1, 1), (1, -1), (1, 1)]


def lanes_of(x, index):
    return jnp.take_along_axis(x, index, axis=1, mode="promise_in_bounds")


def kernel(
    n_lat,
    n_lon,
    state_hbm,
    still_hbm,
    lat_hbm,
    lon_hbm,
    cell_hbm,
    reach_hbm,
    lreach_hbm,
    batch_hbm,
    value_hbm,
    var_hbm,
    out,
    state,
    still,
    lat_tab,
    lon_tab,
    cell,
    reach,
    lreach,
    batch,
    value,
    var,
    work,
    outside,
    ns_send,
    ns_recv,
    ew_send,
    ew_recv,
    corner_send,
    corner_recv,
    lab_send,
    lab_recv,
    obs_send,
    obs_recv,
    loc,
    dev,
    small_sem,
    state_sem,
    ns_ssem,
    ns_rsem,
    ew_ssem,
    ew_rsem,
    corner_ssem,
    corner_rsem,
    lab_ssem,
    lab_rsem,
    obs_ssem,
    obs_rsem,
):
    li = lax.axis_index("lat")
    lo = lax.axis_index("lon")

    def at(dl, dn):
        return (li + dl, lax.rem(lo + dn + n_lon, n_lon))

    def if_band(dl, act):
        if dl == 0:
            act()
        else:
            pl.when((li + dl >= 0) & (li + dl < n_lat))(act)

    def unless_band(dl, act):
        if dl != 0:
            pl.when((li + dl < 0) | (li + dl >= n_lat))(act)

    barrier = pltpu.get_barrier_semaphore()
    for dl in (-1, 1, 0):

        def greet(dl=dl):
            for dn in SECTORS:
                if (dl, dn) != (0, 0):
                    pl.semaphore_signal(barrier, inc=1, device_id=at(dl, dn), device_id_type=MESH)

        if_band(dl, greet)

    still_in = pltpu.make_async_copy(still_hbm, still, small_sem.at[8])
    still_in.start()
    order = [(f, r) for r, q in ((0, 1), (7, 6)) for f, r in ((0, r), (1, r), (2, r), (0, q))]
    order += [(f, r) for r in (1, 6, 2, 5, 3, 4) for f in range(3) if (f, r) not in order]
    rows_in = {}
    for f, r in order:
        copy = pltpu.make_async_copy(state_hbm.at[f, :, r, :], state.at[f, r], state_sem.at[f, r])
        copy.start()
        rows_in[f, r] = copy

    ins = []
    for i, (src, dst) in enumerate(
        (
            (lat_hbm, lat_tab),
            (lon_hbm, lon_tab),
            (cell_hbm, cell),
            (reach_hbm, reach),
            (lreach_hbm, lreach),
            (batch_hbm, batch),
            (value_hbm, value),
            (var_hbm, var),
        )
    ):
        ins.append(pltpu.make_async_copy(src, dst, small_sem.at[i]))
        ins[-1].start()
    def met_all():
        inner = (li > 0) & (li < n_lat - 1)
        pl.when(inner)(lambda: pl.semaphore_wait(barrier, 8))
        pl.when(jnp.logical_not(inner))(lambda: pl.semaphore_wait(barrier, 5))

    for g, dl in enumerate(BANDS):

        def clear(g=g, dl=dl):
            group = pl.ds(3 * g, 3)
            lab_recv[group] = jnp.zeros((3, SLOTS, COLS), BF16)
            for b in range(2):
                obs_recv[b, group] = jnp.zeros((3, SLOTS, COLS), BF16)
            if abs(dl) == 1:
                for t in range(SUB // 2):
                    ns_recv[t, (1 - dl) // 2] = jnp.zeros(ns_recv.shape[2:], BF16)
                    for dn in (-1, 1):
                        i = CORNERS.index((-dl, dn))
                        corner_recv[t, i] = jnp.zeros((SLOTS, COLS), BF16)

        unless_band(dl, clear)

    tile_lane = lax.broadcasted_iota(jnp.int32, (MEMBERS, COLS), 1)
    row_lane = lax.broadcasted_iota(jnp.int32, (1, COLS), 1)

    def as_row(ref, fill):
        x = ref[...].reshape(1, SLOTS)
        return jnp.concatenate([x, jnp.full((1, COLS - SLOTS), fill, x.dtype)], axis=1)

    sub8 = lax.broadcasted_iota(jnp.int32, (8, COLS), 0)
    zeros8 = jnp.zeros((8, COLS), F32)
    zeros_rest = jnp.zeros((COLS - 16, COLS), F32)
    rows_to_lanes = (((1,), (1,)), ((), ()))
    slot_lane = lax.broadcasted_iota(jnp.int32, (SLOTS, COLS), 1)

    def observed():
        for copy in ins:
            copy.wait()

        cell_row = as_row(cell, 0)
        reach_row = as_row(reach, 0).astype(F32)
        lreach_row = as_row(lreach, 0).astype(F32)
        batch_row = as_row(batch, -1)
        value_row = as_row(value, 0.0)
        var_row = as_row(var, 1.0)
        lat_rows = cell_row // (COLS * n_lon) - li * ROWS
        lon_cols = lax.rem(cell_row, COLS * n_lon) - lo * COLS
        lat_rows = jnp.where(row_lane < SLOTS, lat_rows, 0)
        lon_cols = jnp.where(row_lane < SLOTS, lon_cols, 0)
        return lat_rows, lon_cols, reach_row, lreach_row, batch_row, value_row, var_row

    def make_labels():
        slot_of = lax.broadcasted_iota(jnp.int32, (SLOTS, COLS), 0)
        picks = []
        for b in range(2):
            live = (batch_row == b).astype(jnp.int32)
            upto = live
            for s in (1, 2, 4, 8):
                upto = upto + jnp.where(row_lane >= s, pltpu.roll(upto, s, 1), 0)
            rank = jnp.where(live == 1, upto - 1, -1)
            picks.append((slot_of == rank).astype(F32).astype(BF16))

        labels = jnp.where(
            sub8 == 0,
            lat_rows.astype(F32),
            jnp.where(
                sub8 == 1,
                lon_cols.astype(F32),
                jnp.where(sub8 == 2, reach_row, jnp.where(sub8 == 3, lreach_row, 0.0)),
            ),
        )
        label_tile = 0.0
        for b in range(2):
            spread = jnp.concatenate([labels, zeros8] if b == 0 else [zeros8, labels], axis=0)
            spread = jnp.concatenate([spread, zeros_rest], axis=0).astype(BF16)
            label_tile = label_tile + lax.dot_general(
                picks[b], spread, rows_to_lanes, preferred_element_type=F32
            )
        label_tile = label_tile.astype(BF16)
        lab_send[...] = label_tile
        lab_recv[PAIRS - 1] = label_tile
        return picks

    def send_to_all(src, land, ssem, rsem, bands=BANDS):
        for dl in bands:
            g = BANDS.index(dl)

            def send(g=g, dl=dl):
                for dn in SECTORS:
                    if (dl, dn) != (0, 0):
                        pltpu.make_async_remote_copy(
                            src_ref=src,
                            dst_ref=land.at[OFFSETS.index((-dl, -dn))],
                            send_sem=ssem.at[g],
                            recv_sem=rsem.at[BANDS.index(-dl)],
                            device_id=at(dl, dn),
                            device_id_type=MESH,
                        ).start()

            if_band(dl, send)

    def for_all(land, ssem, rsem, act):
        for g, dl in enumerate(BANDS):

            def wait(g=g, dl=dl):
                block = land.at[pl.ds(3 * g, 2 if dl == 0 else 3)]
                act(
                    pltpu.make_async_remote_copy(
                        src_ref=block,
                        dst_ref=block,
                        send_sem=ssem.at[g],
                        recv_sem=rsem.at[g],
                        device_id=at(0, 1),
                        device_id_type=MESH,
                    )
                )

            if_band(dl, wait)

    def all_received(*refs):
        for_all(*refs, lambda copy: copy.wait_recv())

    def all_sent(*refs):
        for_all(*refs, lambda copy: copy.wait_send())

    def coriolis(r):
        row = (li * ROWS + r).astype(F32)
        cor = CORIOLIS_FACTOR * (2.0 * (row + 0.5) / (n_lat * ROWS) - 1.0)
        return TIMESTEP * cor

    def gather_rows(land, adjust):
        pieces = []
        for i in range(PAIRS):
            piece = land[i].astype(F32)[:MOST]
            if adjust:
                dl, dn = OFFSETS[i]
                inside = (li + dl >= 0) & (li + dl < n_lat)
                far = jnp.where(inside, -abs(dl), -100).astype(F32)
                lane = row_lane & 7
                piece = piece + (
                    jnp.where(lane == 0, float(dl * ROWS), 0.0)
                    + jnp.where(lane == 1, float(dn * COLS), 0.0)
                    + jnp.where(lane == 2, far, 0.0)
                    + jnp.where(lane == 3, float(-abs(dn)), 0.0)
                )
            pieces.append(piece)
        pieces.append(jnp.zeros((OBS - PAIRS * MOST, COLS), F32))
        return jnp.concatenate(pieces, axis=0)

    def make_locality(b):
        table = gather_rows(lab_recv, True)
        first = 8 * b
        rows = jnp.broadcast_to(table[:, first : first + 1], (OBS, COLS)).astype(jnp.int32)
        cols = jnp.broadcast_to(table[:, first + 1 : first + 2], (OBS, COLS)).astype(jnp.int32)
        within = (table[:, first + 2 : first + 3] >= 0) & (table[:, first + 3 : first + 4] >= 0)
        within = jnp.broadcast_to(jnp.where(within, 1.0 / (MEMBERS - 1), 0.0), (OBS, COLS))
        lane = lax.broadcasted_iota(jnp.int32, (OBS, COLS), 1)
        away = jnp.abs(lane - cols)
        lon_row = lon_tab[...].reshape(1, 2 * COLS)
        low = jnp.broadcast_to(lon_row[:, :COLS], (OBS, COLS))
        high = jnp.broadcast_to(lon_row[:, COLS:], (OBS, COLS))
        lon_w = jnp.where(
            away < COLS, lanes_of(low, away & (COLS - 1)), lanes_of(high, away & (COLS - 1))
        )
        lon_w = lon_w * within
        lat_row = lat_tab[...].reshape(1, 32)
        lat_row = jnp.concatenate([lat_row, jnp.zeros((1, COLS - 32), F32)], axis=1)
        lat_all = jnp.broadcast_to(lat_row, (OBS, COLS))
        for r in range(ROWS):
            loc[b, r] = lanes_of(lat_all, jnp.abs(rows - r)) * lon_w

    first = tile_lane == 0
    final = tile_lane == COLS - 1
    half = 0.5 * TIMESTEP
    edge = jnp.where(first, half, jnp.where(final, -half, 0.0))
    corner = jnp.where(
        first,
        1.0,
        jnp.where(final, -1.0, jnp.where((tile_lane == 1) | (tile_lane == COLS - 2), half, 0.0)),
    )
    north_live = (li > 0).astype(F32)
    south_live = (li < n_lat - 1).astype(F32)
    sent = []
    bottom = ROWS - 1

    def rolled(x, steps):
        return pltpu.roll(x, steps % COLS, 1)

    def depth(r):
        return half * still[r : r + 1, :]

    def apart(u, outside):
        left = jnp.where(first, outside, rolled(u, 1))
        right = jnp.where(final, outside, rolled(u, -1))
        return right - left

    def at_ends(x, a, b):
        return lanes_of(x, jnp.where(final, b, a))

    def at_four(x, a, b, c, d):
        near = jnp.where(tile_lane == 1, b, a)
        return lanes_of(x, jnp.where(final, d, jnp.where(tile_lane == COLS - 2, c, near)))

    def put(packed, place, x):
        return jnp.where((tile_lane >> 2) == place, rolled(x, 4 * place + 2), packed)

    def middle(ends, second_last, second):
        return jnp.where(
            tile_lane == COLS - 2, second_last, jnp.where(tile_lane == 1, second, ends)
        )

    def labels_to(bands):
        send_to_all(lab_send, lab_recv, lab_ssem, lab_rsem, bands)

    pending = {}

    def finish(*which):
        for r in which:
            if r in pending:
                pending.pop(r)()

    for t in range(SUB // 2):
        packed = jnp.zeros((MEMBERS, COLS), F32)
        corner_tiles = [jnp.zeros((MEMBERS, COLS), F32) for _ in range(2)]
        copies = []
        rows_copies = []
        corner_copies = []

        def send(group, src, dst, ssem, rsem, dl, dn):
            copy = pltpu.make_async_remote_copy(
                src_ref=src,
                dst_ref=dst,
                send_sem=ssem,
                recv_sem=rsem,
                device_id=at(dl, dn),
                device_id_type=MESH,
            )
            if_band(dl, copy.start)
            group.append((copy, dl, -dl))

        def velocities(r):
            if t == 0:
                for key in ((0, r - 1), (0, r), (0, r + 1), (1, r), (2, r)):
                    if key in rows_in:
                        rows_in.pop(key).wait()
            h, u, v = state[0, r], state[1, r], state[2, r]
            left, right = rolled(h, 1), rolled(h, -1)
            turn = coriolis(r)
            new_u = u + turn * v + jnp.where(first, 0.0, half * left)
            new_u = new_u - jnp.where(final, 0.0, half * right)
            new_v = v - turn * u
            if r > 0:
                new_v = new_v + half * state[0, r - 1]
            if r < bottom:
                new_v = new_v - half * state[0, r + 1]
            state[1, r] = new_u
            state[2, r] = new_v
            return middle(new_u, right, left)

        def heights(r):
            h = state[0, r]
            above = state[2, r - 1] if r > 0 else -half * north_live * h
            below = state[2, r + 1] if r < bottom else half * south_live * h
            around = apart(state[1, r], -edge * h) + (below - above)
            work[r] = h - depth(r) * around

        def send_rows(part, rows):
            for side, dl in ((0, -1), (1, 1)):
                send(
                    rows_copies if part else copies,
                    ns_send.at[t, side, rows],
                    ns_recv.at[t, side, rows],
                    ns_ssem.at[t, side, part],
                    ns_rsem.at[t, side, part],
                    dl,
                    0,
                )

        finish(0, 1, 7, 6)
        for side, outer in ((0, 0), (1, bottom)):
            ends = velocities(outer)
            packed = put(packed, outer, ends)
            tile = put(corner_tiles[side], 0, ends)
            tile = put(tile, 2, state[2, outer])
            corner_tiles[side] = put(tile, 3, state[0, outer])
            ns_send[t, side, :MEMBERS] = state[0, outer].astype(BF16)
            ns_send[t, side, MEMBERS : 2 * MEMBERS] = state[2, outer].astype(BF16)
        if t == 0:
            met_all()
        send_rows(0, pl.ds(0, 2 * MEMBERS))
        finish(2, 5)
        for side, inner in ((0, 1), (1, bottom - 1)):
            ends = velocities(inner)
            packed = put(packed, inner, ends)
            tile = put(corner_tiles[side], 1, ends)
            folded = tile[:SLOTS]
            for g in range(1, MEMBERS // SLOTS):
                part = rolled(tile[g * SLOTS : (g + 1) * SLOTS], 16 * g)
                folded = jnp.where((slot_lane >> 4) == g, part, folded)
            corner_send[t, side] = folded.astype(BF16)
        for i, (dl, dn) in enumerate(CORNERS):
            send(
                corner_copies,
                corner_send.at[t, (1 + dl) // 2],
                corner_recv.at[t, i],
                corner_ssem.at[t, i],
                corner_rsem.at[t, i],
                dl,
                dn,
            )
        finish(3, 4)
        for r in (2, 5):
            packed = put(packed, r, velocities(r))
        if t == 0:
            still_in.wait()
        for r in (0, 1, 7, 6):
            heights(r)
        for side, outer, inner, sign in ((0, 0, 1, -half), (1, bottom, bottom - 1, half)):
            second = state[2, outer] - coriolis(outer) * state[1, outer] + sign * work[inner]
            ns_send[t, side, 2 * MEMBERS : 3 * MEMBERS] = work[outer].astype(BF16)
            ns_send[t, side, 3 * MEMBERS : 4 * MEMBERS] = second.astype(BF16)
            if t == 0:
                rows = jnp.concatenate(
                    [depth(outer), depth(inner), jnp.zeros((14, COLS), F32)], axis=0
                )
                ns_send[t, side, 4 * MEMBERS :] = rows.astype(BF16)
        send_rows(1, pl.ds(2 * MEMBERS, 2 * MEMBERS + (16 if t == 0 else 0)))
        for r in (3, 4):
            packed = put(packed, r, velocities(r))
        for r in (2, 3, 4, 5):
            heights(r)
        for r in range(ROWS):
            h = work[r]
            left, right = rolled(h, 1), rolled(h, -1)
            second = state[1, r] + coriolis(r) * state[2, r]
            second = second + jnp.where(final, half * left, -half * right)
            packed = put(packed, ROWS + r, middle(second, right, left))
        ew_send[t, :MEMBERS] = packed.astype(BF16)
        if t == 0:
            rows = jnp.concatenate([half * still[...], zeros8], axis=0)
            ew_send[t, MEMBERS:] = rows.astype(BF16)
        for i, (dl, dn) in enumerate(SIDES):
            rows = pl.ds(0, MEMBERS + (16 if t == 0 else 0))
            send(
                copies,
                ew_send.at[t, rows],
                ew_recv.at[t, i, rows],
                ew_ssem.at[t, i],
                ew_rsem.at[t, i],
                dl,
                dn,
            )
        sent.extend(copies + rows_copies + corner_copies)
        if t == 0:
            (lat_rows, lon_cols, reach_row, lreach_row, batch_row, value_row, var_row) = observed()
            picks = make_labels()
        labels_to((-1, 1, 0) if t == 0 else (-2, 2))
        for copy, _, dl in copies:
            if_band(dl, copy.wait_recv)
        if t == SUB // 2 - 1:
            labels_to((-3, 3))

        def merged(west, east):
            lane = lax.broadcasted_iota(jnp.int32, west.shape, 1)
            return jnp.where((lane & 2) == 0, west.astype(F32), east.astype(F32))

        def from_rows(side, i):
            return ns_recv[t, side, i * MEMBERS : (i + 1) * MEMBERS].astype(F32)

        def edge_depths(side):
            rows = ns_recv[0, side, 4 * MEMBERS :].astype(F32)
            return rows[0:1], rows[1:2]

        south_h, south_v = from_rows(0, 0), from_rows(0, 1)
        north_h, north_v = from_rows(1, 0), from_rows(1, 1)
        ends_d = [
            ew_recv[0, SIDES.index((0, dn)), MEMBERS:].astype(F32)[:ROWS] for dn in (1, -1)
        ]
        end_lane = lax.broadcasted_iota(jnp.int32, (ROWS, COLS), 1)
        d1, d2 = (
            jnp.where(
                end_lane == 0,
                rolled(ends_d[0], k),
                jnp.where(end_lane == COLS - 1, rolled(ends_d[1], -k), 0.0),
            )
            for k in (1, 2)
        )
        top, low = state[0, 0], state[0, bottom]
        top_v = state[2, 0] + half * north_h
        low_v = state[2, bottom] - half * south_h
        state[2, 0] = top_v
        state[2, bottom] = low_v
        north_v = (north_v - half * top) * north_live
        south_v = (south_v + half * low) * south_live
        ends = merged(*(ew_recv[t, SIDES.index((0, dn)), :MEMBERS] for dn in (1, -1)))
        for r in range(ROWS):
            h = state[0, r]
            a, b = 4 * r, 4 * (ROWS + r)
            far_h = at_ends(ends, a, a + 3)
            far_u = at_ends(ends, a + 1, a + 2)
            far_h1 = at_ends(ends, b, b + 3)
            far_u2 = at_ends(ends, b + 1, b + 2)
            u = state[1, r] + edge * far_h
            state[1, r] = u
            above = state[2, r - 1] if r > 0 else north_v
            below = state[2, r + 1] if r < bottom else south_v
            work[r] = h - depth(r) * (apart(u, far_u - edge * h) + (below - above))
            end_d1, end_d2 = d1[r : r + 1], d2[r : r + 1]
            outside[0, r] = far_h1 - end_d1 * (edge * (1.0 / half) * u - half * far_h)
            outside[1, r] = far_u2 - edge * h * (1.0 - half * end_d2)

        for copy, _, dl in corner_copies + rows_copies:
            if_band(dl, copy.wait_recv)
        corners = {}
        for name, dl in (("n", -1), ("s", 1)):
            folded = merged(
                *(corner_recv[t, CORNERS.index((-dl, dn))] for dn in (1, -1))
            )
            x = jnp.concatenate(
                [folded] + [rolled(folded, -16 * g) for g in range(1, MEMBERS // SLOTS)], axis=0
            )
            corners[name] = (
                at_ends(x, 0, 3),
                at_four(x, 1, 0, 3, 2),
                at_four(x, 5, 4, 7, 6),
                at_ends(x, 9, 10),
                at_ends(x, 8, 11),
                at_ends(x, 12, 15),
            )
        n_h, n_row1, n_row2, n_v, n_v_in, n_h_in = corners["n"]
        s_h, s_row1, s_row2, s_v, s_v_in, s_h_in = corners["s"]
        south_h1, south_v2 = from_rows(0, 2), from_rows(0, 3)
        north_h1, north_v2 = from_rows(1, 2), from_rows(1, 3)
        south_d1, south_d2 = edge_depths(0)
        north_d1, north_d2 = edge_depths(1)
        north_h1 = north_h1 - north_d1 * (top_v - half * north_h) + north_d1 * corner * n_row1
        south_h1 = south_h1 + south_d1 * (low_v + half * south_h) + south_d1 * corner * s_row1
        north_h1 = north_h1 * north_live
        south_h1 = south_h1 * south_live
        north_v2 = north_v2 - half * top * (1.0 - half * north_d2)
        north_v2 = north_v2 + half * north_d2 * corner * n_row2 - coriolis(-1) * edge * n_h
        south_v2 = south_v2 + half * low * (1.0 - half * south_d2)
        south_v2 = south_v2 - half * south_d2 * corner * s_row2 - coriolis(ROWS) * edge * s_h
        for r, far_h1, far_u2 in (
            (0, n_v, coriolis(0) * half * n_h + edge * d2[0:1] * n_v_in),
            (1, half * n_h, half * edge * d2[1:2] * n_h_in),
            (6, half * s_h, half * edge * d2[6:7] * s_h_in),
            (7, -s_v, -coriolis(7) * half * s_h - edge * d2[7:8] * s_v_in),
        ):
            outside[0, r] = outside[0, r] + d1[r : r + 1] * far_h1
            outside[1, r] = outside[1, r] + far_u2
        for r in (0, 1, 7, 6, 2, 5, 3, 4):
            h, u, v = work[r], state[1, r], state[2, r]
            above = work[r - 1] if r > 0 else north_h1
            below = work[r + 1] if r < bottom else south_h1
            state[1, r] = u + coriolis(r) * v - half * apart(h, outside[0, r])
            state[2, r] = v - coriolis(r) * u - half * (below - above)
        north_v2 = (north_v2 - half * work[0]) * north_live
        south_v2 = (south_v2 + half * work[bottom]) * south_live

        def last_height(r, north_v2, south_v2):
            h = work[r]
            above = state[2, r - 1] if r > 0 else north_v2
            below = state[2, r + 1] if r < bottom else south_v2
            around = apart(state[1, r], outside[1, r] - edge * h) + (below - above)
            state[0, r] = h - depth(r) * around

        for r in range(ROWS):
            pending[r] = functools.partial(last_height, r, north_v2, south_v2)

    finish(*range(ROWS))

    pick_lane = jnp.broadcast_to(lon_cols, (MEMBERS, COLS))

    def at_observed(tile_of_row, lane):
        found = jnp.zeros(lane.shape, F32)
        for r in range(ROWS):
            found = jnp.where(lat_rows == r, lanes_of(tile_of_row(r), lane), found)
        return found

    def send_observations(b, prior):
        mean = jnp.sum(prior, axis=0, keepdims=True) / MEMBERS
        away = prior - mean
        total = jnp.sum(away * away, axis=0, keepdims=True) / (MEMBERS - 1) + var_row
        shift = (value_row - mean) / total
        spread = -1.0 / (jnp.sqrt(total) * (jnp.sqrt(var_row) + jnp.sqrt(total)))
        coefs = jnp.where(sub8 == 0, shift, jnp.where(sub8 == 1, spread, 0.0))
        rows = jnp.concatenate(
            [away, coefs, jnp.zeros((COLS - MEMBERS - 8, COLS), F32)], axis=0
        ).astype(BF16)
        tile = lax.dot_general(picks[b], rows, rows_to_lanes, preferred_element_type=F32)
        tile = tile.astype(BF16)
        obs_send[b] = tile
        obs_recv[b, PAIRS - 1] = tile
        send_to_all(obs_send.at[b], obs_recv.at[b], obs_ssem.at[b], obs_rsem.at[b])
        return away.astype(BF16)

    def make_dev(f):
        for r in range(ROWS):
            x = state[f, r]
            mean = jnp.sum(x, axis=0, keepdims=True) / MEMBERS
            dev[f, :, r * COLS : (r + 1) * COLS] = (x - mean).astype(BF16)

    def receive(b):
        all_received(obs_recv.at[b], obs_ssem.at[b], obs_rsem.at[b])
        table = gather_rows(obs_recv.at[b], False)
        obs_dev = table.astype(BF16)[:, :MEMBERS]
        weights = table[:, MEMBERS : MEMBERS + 1] + table[:, MEMBERS + 1 : MEMBERS + 2] * table
        weights = weights.astype(BF16).astype(F32)
        weights = jnp.transpose(weights).astype(BF16)[:MEMBERS]
        return obs_dev, weights

    def update(b, f, obs_dev, weights, last):
        gains = []
        for r in range(ROWS):
            lanes = slice(r * COLS, (r + 1) * COLS)
            cov = jnp.dot(obs_dev, dev[f, :, lanes], preferred_element_type=F32)
            gains.append((cov * loc[b, r]).astype(BF16))
        for pair in range(ROWS // 2):
            gain = jnp.concatenate(gains[2 * pair : 2 * pair + 2], axis=1)
            step = jnp.dot(weights, gain, preferred_element_type=F32)
            for i in range(2):
                r = 2 * pair + i
                new = state[f, r] + step[:, i * COLS : (i + 1) * COLS]
                if last:
                    out[f, :, r, :] = new
                else:
                    state[f, r] = new

    prior = at_observed(lambda r: state[0, r], pick_lane)
    prior_dev = send_observations(0, prior)
    for f in range(3):
        make_dev(f)
    all_received(lab_recv, lab_ssem, lab_rsem)
    make_locality(0)
    prior_loc = at_observed(lambda r: loc[0, r], jnp.broadcast_to(lon_cols, (OBS, COLS)))
    obs_dev, weights = receive(0)
    cov = jnp.dot(obs_dev, prior_dev, preferred_element_type=F32)
    gain = (cov * prior_loc).astype(BF16)
    send_observations(1, prior + jnp.dot(weights, gain, preferred_element_type=F32))
    for f in range(3):
        update(0, f, obs_dev, weights, False)
    for f in range(3):
        make_dev(f)
    make_locality(1)
    for copy, dl, _ in sent:
        if_band(dl, copy.wait_send)
    all_sent(lab_recv, lab_ssem, lab_rsem)
    for b in range(2):
        all_sent(obs_recv.at[b], obs_ssem.at[b], obs_rsem.at[b])
    obs_dev, weights = receive(1)
    for f in range(3):
        update(1, f, obs_dev, weights, True)


def per_device(n_lat, n_lon, *args):
    args = [pltpu.with_memory_space_constraint(arg, pltpu.HBM) for arg in args]
    vmem = pltpu.VMEM
    dma = pltpu.SemaphoreType.DMA
    ints = vmem((SLOTS,), jnp.int32)
    floats = vmem((SLOTS,), F32)
    return pl.pallas_call(
        functools.partial(kernel, n_lat, n_lon),
        out_shape=vmem(args[0].shape, F32),
        in_specs=[pl.BlockSpec(memory_space=pltpu.HBM)] * len(args),
        out_specs=pl.BlockSpec(memory_space=vmem),
        scratch_shapes=[
            vmem((3, ROWS, MEMBERS, COLS), F32),
            vmem((ROWS, COLS), F32),
            vmem((32,), F32),
            vmem((256,), F32),
            ints,
            ints,
            ints,
            ints,
            floats,
            floats,
            vmem((ROWS, MEMBERS, COLS), F32),
            vmem((2, ROWS, MEMBERS, COLS), F32),
            vmem((SUB // 2, 2, 4 * MEMBERS + 16, COLS), BF16),
            vmem((SUB // 2, 2, 4 * MEMBERS + 16, COLS), BF16),
            vmem((SUB // 2, MEMBERS + 16, COLS), BF16),
            vmem((SUB // 2, len(SIDES), MEMBERS + 16, COLS), BF16),
            vmem((SUB // 2, 2, SLOTS, COLS), BF16),
            vmem((SUB // 2, len(CORNERS), SLOTS, COLS), BF16),
            vmem((SLOTS, COLS), BF16),
            vmem((PAIRS, SLOTS, COLS), BF16),
            vmem((2, SLOTS, COLS), BF16),
            vmem((2, PAIRS, SLOTS, COLS), BF16),
            vmem((2, ROWS, OBS, COLS), F32),
            vmem((3, MEMBERS, ROWS * COLS), BF16),
            dma((9,)),
            dma((3, ROWS)),
            dma((SUB // 2, 2, 2)),
            dma((SUB // 2, 2, 2)),
            dma((SUB // 2, len(SIDES))),
            dma((SUB // 2, len(SIDES))),
            dma((SUB // 2, len(CORNERS))),
            dma((SUB // 2, len(CORNERS))),
            dma((len(BANDS),)),
            dma((len(BANDS),)),
            dma((2, len(BANDS))),
            dma((2, len(BANDS))),
        ],
        compiler_params=pltpu.CompilerParams(
            collective_id=0, has_side_effects=True, vmem_limit_bytes=60 * 1024 * 1024
        ),
        name="window",
    )(*args)


def solution(mesh):
    return jax.shard_map(
        functools.partial(per_device, mesh.shape["lat"], mesh.shape["lon"]),
        mesh=mesh,
        in_specs=(
            P(None, None, "lat", "lon"),
            P("lat", "lon"),
            P(),
            P(),
            P(("lat", "lon")),
            P(("lat", "lon")),
            P(("lat", "lon")),
            P(("lat", "lon")),
            P(("lat", "lon")),
            P(("lat", "lon")),
        ),
        out_specs=P(None, None, "lat", "lon"),
        check_vma=False,
    )
```

```python
import functools

import jax
import jax.numpy as jnp
from jax import lax
from jax.experimental import pallas as pl
from jax.experimental.pallas import tpu as pltpu
from jax.sharding import PartitionSpec as P

REACH = 3
SUB = 4
MOST = 12
TIMESTEP = 0.5
CORIOLIS_FACTOR = 0.3

MEMBERS = 80
ROWS = 8
COLS = 128
SLOTS = 16
PAIRS = 21
OBS = 256
MESH = pl.DeviceIdType.MESH
F32 = jnp.float32
BF16 = jnp.bfloat16

BANDS = (-2, 2, -3, 3, -1, 1, 0)
SECTORS = (-1, 1, 0)
OFFSETS = [(dl, dn) for dl in BANDS for dn in SECTORS]
SIDES = [(0, -1), (0, 1)]
CORNERS = [(-1, -1), (-1, 1), (1, -1), (1, 1)]


def lanes_of(x, index):
    return jnp.take_along_axis(x, index, axis=1, mode="promise_in_bounds")


def kernel(
    n_lat,
    n_lon,
    state_hbm,
    still_hbm,
    lat_hbm,
    lon_hbm,
    cell_hbm,
    reach_hbm,
    lreach_hbm,
    batch_hbm,
    value_hbm,
    var_hbm,
    out,
    state,
    still,
    lat_tab,
    lon_tab,
    cell,
    reach,
    lreach,
    batch,
    value,
    var,
    work,
    outside,
    ns_send,
    ns_recv,
    ew_send,
    ew_recv,
    corner_send,
    corner_recv,
    lab_send,
    lab_recv,
    obs_send,
    obs_recv,
    loc,
    dev,
    small_sem,
    state_sem,
    ns_ssem,
    ns_rsem,
    ew_ssem,
    ew_rsem,
    corner_ssem,
    corner_rsem,
    lab_ssem,
    lab_rsem,
    obs_ssem,
    obs_rsem,
):
    li = lax.axis_index("lat")
    lo = lax.axis_index("lon")

    def at(dl, dn):
        return (li + dl, lax.rem(lo + dn + n_lon, n_lon))

    def if_band(dl, act):
        if dl == 0:
            act()
        else:
            pl.when((li + dl >= 0) & (li + dl < n_lat))(act)

    def unless_band(dl, act):
        if dl != 0:
            pl.when((li + dl < 0) | (li + dl >= n_lat))(act)

    barrier = pltpu.get_barrier_semaphore()
    for dl in (-1, 1, 0):

        def greet(dl=dl):
            for dn in SECTORS:
                if (dl, dn) != (0, 0):
                    pl.semaphore_signal(barrier, inc=1, device_id=at(dl, dn), device_id_type=MESH)

        if_band(dl, greet)

    still_in = pltpu.make_async_copy(still_hbm, still, small_sem.at[8])
    still_in.start()
    order = [(f, r) for r, q in ((0, 1), (7, 6)) for f, r in ((0, r), (1, r), (2, r), (0, q))]
    order += [(f, r) for r in (1, 6, 2, 5, 3, 4) for f in range(3) if (f, r) not in order]
    rows_in = {}
    for f, r in order:
        copy = pltpu.make_async_copy(state_hbm.at[f, :, r, :], state.at[f, r], state_sem.at[f, r])
        copy.start()
        rows_in[f, r] = copy

    ins = []
    for i, (src, dst) in enumerate(
        (
            (lat_hbm, lat_tab),
            (lon_hbm, lon_tab),
            (cell_hbm, cell),
            (reach_hbm, reach),
            (lreach_hbm, lreach),
            (batch_hbm, batch),
            (value_hbm, value),
            (var_hbm, var),
        )
    ):
        ins.append(pltpu.make_async_copy(src, dst, small_sem.at[i]))
        ins[-1].start()
    def met_all():
        inner = (li > 0) & (li < n_lat - 1)
        pl.when(inner)(lambda: pl.semaphore_wait(barrier, 8))
        pl.when(jnp.logical_not(inner))(lambda: pl.semaphore_wait(barrier, 5))

    for g, dl in enumerate(BANDS):

        def clear(g=g, dl=dl):
            group = pl.ds(3 * g, 3)
            lab_recv[group] = jnp.zeros((3, SLOTS, COLS), BF16)
            for b in range(2):
                obs_recv[b, group] = jnp.zeros((3, SLOTS, COLS), BF16)
            if abs(dl) == 1:
                for t in range(SUB // 2):
                    ns_recv[t, (1 - dl) // 2] = jnp.zeros(ns_recv.shape[2:], BF16)
                    for dn in (-1, 1):
                        i = CORNERS.index((-dl, dn))
                        corner_recv[t, i] = jnp.zeros((SLOTS, COLS), BF16)

        unless_band(dl, clear)

    tile_lane = lax.broadcasted_iota(jnp.int32, (MEMBERS, COLS), 1)
    row_lane = lax.broadcasted_iota(jnp.int32, (1, COLS), 1)

    def as_row(ref, fill):
        x = ref[...].reshape(1, SLOTS)
        return jnp.concatenate([x, jnp.full((1, COLS - SLOTS), fill, x.dtype)], axis=1)

    sub8 = lax.broadcasted_iota(jnp.int32, (8, COLS), 0)
    zeros8 = jnp.zeros((8, COLS), F32)
    zeros_rest = jnp.zeros((COLS - 16, COLS), F32)
    rows_to_lanes = (((1,), (1,)), ((), ()))
    slot_lane = lax.broadcasted_iota(jnp.int32, (SLOTS, COLS), 1)

    def observed():
        for copy in ins:
            copy.wait()

        cell_row = as_row(cell, 0)
        reach_row = as_row(reach, 0).astype(F32)
        lreach_row = as_row(lreach, 0).astype(F32)
        batch_row = as_row(batch, -1)
        value_row = as_row(value, 0.0)
        var_row = as_row(var, 1.0)
        lat_rows = cell_row // (COLS * n_lon) - li * ROWS
        lon_cols = lax.rem(cell_row, COLS * n_lon) - lo * COLS
        lat_rows = jnp.where(row_lane < SLOTS, lat_rows, 0)
        lon_cols = jnp.where(row_lane < SLOTS, lon_cols, 0)
        return lat_rows, lon_cols, reach_row, lreach_row, batch_row, value_row, var_row

    def make_labels():
        slot_of = lax.broadcasted_iota(jnp.int32, (SLOTS, COLS), 0)
        picks = []
        for b in range(2):
            live = (batch_row == b).astype(jnp.int32)
            upto = live
            for s in (1, 2, 4, 8):
                upto = upto + jnp.where(row_lane >= s, pltpu.roll(upto, s, 1), 0)
            rank = jnp.where(live == 1, upto - 1, -1)
            picks.append((slot_of == rank).astype(F32).astype(BF16))

        labels = jnp.where(
            sub8 == 0,
            lat_rows.astype(F32),
            jnp.where(
                sub8 == 1,
                lon_cols.astype(F32),
                jnp.where(sub8 == 2, reach_row, jnp.where(sub8 == 3, lreach_row, 0.0)),
            ),
        )
        label_tile = 0.0
        for b in range(2):
            spread = jnp.concatenate([labels, zeros8] if b == 0 else [zeros8, labels], axis=0)
            spread = jnp.concatenate([spread, zeros_rest], axis=0).astype(BF16)
            label_tile = label_tile + lax.dot_general(
                picks[b], spread, rows_to_lanes, preferred_element_type=F32
            )
        label_tile = label_tile.astype(BF16)
        lab_send[...] = label_tile
        lab_recv[PAIRS - 1] = label_tile
        return picks

    def send_to_all(src, land, ssem, rsem, bands=BANDS):
        for dl in bands:
            g = BANDS.index(dl)

            def send(g=g, dl=dl):
                for dn in SECTORS:
                    if (dl, dn) != (0, 0):
                        pltpu.make_async_remote_copy(
                            src_ref=src,
                            dst_ref=land.at[OFFSETS.index((-dl, -dn))],
                            send_sem=ssem.at[g],
                            recv_sem=rsem.at[BANDS.index(-dl)],
                            device_id=at(dl, dn),
                            device_id_type=MESH,
                        ).start()

            if_band(dl, send)

    def for_all(land, ssem, rsem, act):
        for g, dl in enumerate(BANDS):

            def wait(g=g, dl=dl):
                block = land.at[pl.ds(3 * g, 2 if dl == 0 else 3)]
                act(
                    pltpu.make_async_remote_copy(
                        src_ref=block,
                        dst_ref=block,
                        send_sem=ssem.at[g],
                        recv_sem=rsem.at[g],
                        device_id=at(0, 1),
                        device_id_type=MESH,
                    )
                )

            if_band(dl, wait)

    def all_received(*refs):
        for_all(*refs, lambda copy: copy.wait_recv())

    def all_sent(*refs):
        for_all(*refs, lambda copy: copy.wait_send())

    def coriolis(r):
        row = (li * ROWS + r).astype(F32)
        cor = CORIOLIS_FACTOR * (2.0 * (row + 0.5) / (n_lat * ROWS) - 1.0)
        return TIMESTEP * cor

    def gather_rows(land, adjust):
        pieces = []
        for i in range(PAIRS):
            piece = land[i].astype(F32)[:MOST]
            if adjust:
                dl, dn = OFFSETS[i]
                inside = (li + dl >= 0) & (li + dl < n_lat)
                far = jnp.where(inside, -abs(dl), -100).astype(F32)
                lane = row_lane & 7
                piece = piece + (
                    jnp.where(lane == 0, float(dl * ROWS), 0.0)
                    + jnp.where(lane == 1, float(dn * COLS), 0.0)
                    + jnp.where(lane == 2, far, 0.0)
                    + jnp.where(lane == 3, float(-abs(dn)), 0.0)
                )
            pieces.append(piece)
        pieces.append(jnp.zeros((OBS - PAIRS * MOST, COLS), F32))
        return jnp.concatenate(pieces, axis=0)

    def make_locality(b):
        table = gather_rows(lab_recv, True)
        first = 8 * b
        rows = jnp.broadcast_to(table[:, first : first + 1], (OBS, COLS)).astype(jnp.int32)
        cols = jnp.broadcast_to(table[:, first + 1 : first + 2], (OBS, COLS)).astype(jnp.int32)
        within = (table[:, first + 2 : first + 3] >= 0) & (table[:, first + 3 : first + 4] >= 0)
        within = jnp.broadcast_to(jnp.where(within, 1.0 / (MEMBERS - 1), 0.0), (OBS, COLS))
        lane = lax.broadcasted_iota(jnp.int32, (OBS, COLS), 1)
        away = jnp.abs(lane - cols)
        lon_row = lon_tab[...].reshape(1, 2 * COLS)
        low = jnp.broadcast_to(lon_row[:, :COLS], (OBS, COLS))
        high = jnp.broadcast_to(lon_row[:, COLS:], (OBS, COLS))
        lon_w = jnp.where(
            away < COLS, lanes_of(low, away & (COLS - 1)), lanes_of(high, away & (COLS - 1))
        )
        lon_w = lon_w * within
        lat_row = lat_tab[...].reshape(1, 32)
        lat_row = jnp.concatenate([lat_row, jnp.zeros((1, COLS - 32), F32)], axis=1)
        lat_all = jnp.broadcast_to(lat_row, (OBS, COLS))
        for r in range(ROWS):
            loc[b, r] = lanes_of(lat_all, jnp.abs(rows - r)) * lon_w

    first = tile_lane == 0
    final = tile_lane == COLS - 1
    half = 0.5 * TIMESTEP
    edge = jnp.where(first, half, jnp.where(final, -half, 0.0))
    corner = jnp.where(
        first,
        1.0,
        jnp.where(final, -1.0, jnp.where((tile_lane == 1) | (tile_lane == COLS - 2), half, 0.0)),
    )
    north_live = (li > 0).astype(F32)
    south_live = (li < n_lat - 1).astype(F32)
    sent = []
    bottom = ROWS - 1

    def rolled(x, steps):
        return pltpu.roll(x, steps % COLS, 1)

    def depth(r):
        return half * still[r : r + 1, :]

    def apart(u, outside):
        left = jnp.where(first, outside, rolled(u, 1))
        right = jnp.where(final, outside, rolled(u, -1))
        return right - left

    def at_ends(x, a, b):
        return lanes_of(x, jnp.where(final, b, a))

    def at_four(x, a, b, c, d):
        near = jnp.where(tile_lane == 1, b, a)
        return lanes_of(x, jnp.where(final, d, jnp.where(tile_lane == COLS - 2, c, near)))

    def put(packed, place, x):
        return jnp.where((tile_lane >> 2) == place, rolled(x, 4 * place + 2), packed)

    def middle(ends, second_last, second):
        return jnp.where(
            tile_lane == COLS - 2, second_last, jnp.where(tile_lane == 1, second, ends)
        )

    def labels_to(bands):
        send_to_all(lab_send, lab_recv, lab_ssem, lab_rsem, bands)

    pending = {}

    def finish(*which):
        for r in which:
            if r in pending:
                pending.pop(r)()

    for t in range(SUB // 2):
        packed = jnp.zeros((MEMBERS, COLS), F32)
        corner_tiles = [jnp.zeros((MEMBERS, COLS), F32) for _ in range(2)]
        copies = []
        rows_copies = []
        corner_copies = []

        def send(group, src, dst, ssem, rsem, dl, dn):
            copy = pltpu.make_async_remote_copy(
                src_ref=src,
                dst_ref=dst,
                send_sem=ssem,
                recv_sem=rsem,
                device_id=at(dl, dn),
                device_id_type=MESH,
            )
            if_band(dl, copy.start)
            group.append((copy, dl, -dl))

        def velocities(r):
            if t == 0:
                for key in ((0, r - 1), (0, r), (0, r + 1), (1, r), (2, r)):
                    if key in rows_in:
                        rows_in.pop(key).wait()
            h, u, v = state[0, r], state[1, r], state[2, r]
            left, right = rolled(h, 1), rolled(h, -1)
            turn = coriolis(r)
            new_u = u + turn * v + jnp.where(first, 0.0, half * left)
            new_u = new_u - jnp.where(final, 0.0, half * right)
            new_v = v - turn * u
            if r > 0:
                new_v = new_v + half * state[0, r - 1]
            if r < bottom:
                new_v = new_v - half * state[0, r + 1]
            state[1, r] = new_u
            state[2, r] = new_v
            return middle(new_u, right, left)

        def heights(r):
            h = state[0, r]
            above = state[2, r - 1] if r > 0 else -half * north_live * h
            below = state[2, r + 1] if r < bottom else half * south_live * h
            around = apart(state[1, r], -edge * h) + (below - above)
            work[r] = h - depth(r) * around

        def send_rows(part, rows):
            for side, dl in ((0, -1), (1, 1)):
                send(
                    rows_copies if part else copies,
                    ns_send.at[t, side, rows],
                    ns_recv.at[t, side, rows],
                    ns_ssem.at[t, side, part],
                    ns_rsem.at[t, side, part],
                    dl,
                    0,
                )

        finish(0, 1, 7, 6)
        for side, outer in ((0, 0), (1, bottom)):
            ends = velocities(outer)
            packed = put(packed, outer, ends)
            tile = put(corner_tiles[side], 0, ends)
            tile = put(tile, 2, state[2, outer])
            corner_tiles[side] = put(tile, 3, state[0, outer])
            ns_send[t, side, :MEMBERS] = state[0, outer].astype(BF16)
            ns_send[t, side, MEMBERS : 2 * MEMBERS] = state[2, outer].astype(BF16)
        if t == 0:
            met_all()
        send_rows(0, pl.ds(0, 2 * MEMBERS))
        finish(2, 5)
        for side, inner in ((0, 1), (1, bottom - 1)):
            ends = velocities(inner)
            packed = put(packed, inner, ends)
            tile = put(corner_tiles[side], 1, ends)
            folded = tile[:SLOTS]
            for g in range(1, MEMBERS // SLOTS):
                part = rolled(tile[g * SLOTS : (g + 1) * SLOTS], 16 * g)
                folded = jnp.where((slot_lane >> 4) == g, part, folded)
            corner_send[t, side] = folded.astype(BF16)
        for i, (dl, dn) in enumerate(CORNERS):
            send(
                corner_copies,
                corner_send.at[t, (1 + dl) // 2],
                corner_recv.at[t, i],
                corner_ssem.at[t, i],
                corner_rsem.at[t, i],
                dl,
                dn,
            )
        finish(3, 4)
        for r in (2, 5):
            packed = put(packed, r, velocities(r))
        if t == 0:
            still_in.wait()
        for r in (0, 1, 7, 6):
            heights(r)
        for side, outer, inner, sign in ((0, 0, 1, -half), (1, bottom, bottom - 1, half)):
            second = state[2, outer] - coriolis(outer) * state[1, outer] + sign * work[inner]
            ns_send[t, side, 2 * MEMBERS : 3 * MEMBERS] = work[outer].astype(BF16)
            ns_send[t, side, 3 * MEMBERS : 4 * MEMBERS] = second.astype(BF16)
            if t == 0:
                rows = jnp.concatenate(
                    [depth(outer), depth(inner), jnp.zeros((14, COLS), F32)], axis=0
                )
                ns_send[t, side, 4 * MEMBERS :] = rows.astype(BF16)
        send_rows(1, pl.ds(2 * MEMBERS, 2 * MEMBERS + (16 if t == 0 else 0)))
        for r in (3, 4):
            packed = put(packed, r, velocities(r))
        for r in (2, 3, 4, 5):
            heights(r)
        for r in range(ROWS):
            h = work[r]
            left, right = rolled(h, 1), rolled(h, -1)
            second = state[1, r] + coriolis(r) * state[2, r]
            second = second + jnp.where(final, half * left, -half * right)
            packed = put(packed, ROWS + r, middle(second, right, left))
        ew_send[t, :MEMBERS] = packed.astype(BF16)
        if t == 0:
            rows = jnp.concatenate([half * still[...], zeros8], axis=0)
            ew_send[t, MEMBERS:] = rows.astype(BF16)
        for i, (dl, dn) in enumerate(SIDES):
            rows = pl.ds(0, MEMBERS + (16 if t == 0 else 0))
            send(
                copies,
                ew_send.at[t, rows],
                ew_recv.at[t, i, rows],
                ew_ssem.at[t, i],
                ew_rsem.at[t, i],
                dl,
                dn,
            )
        sent.extend(copies + rows_copies + corner_copies)
        if t == 0:
            (lat_rows, lon_cols, reach_row, lreach_row, batch_row, value_row, var_row) = observed()
            picks = make_labels()
        labels_to((-1, 1, 0) if t == 0 else (-2, 2))
        for copy, _, dl in copies:
            if_band(dl, copy.wait_recv)
        if t == SUB // 2 - 1:
            labels_to((-3, 3))

        def merged(west, east):
            lane = lax.broadcasted_iota(jnp.int32, west.shape, 1)
            return jnp.where((lane & 2) == 0, west.astype(F32), east.astype(F32))

        def from_rows(side, i):
            return ns_recv[t, side, i * MEMBERS : (i + 1) * MEMBERS].astype(F32)

        def edge_depths(side):
            rows = ns_recv[0, side, 4 * MEMBERS :].astype(F32)
            return rows[0:1], rows[1:2]

        south_h, south_v = from_rows(0, 0), from_rows(0, 1)
        north_h, north_v = from_rows(1, 0), from_rows(1, 1)
        ends_d = [
            ew_recv[0, SIDES.index((0, dn)), MEMBERS:].astype(F32)[:ROWS] for dn in (1, -1)
        ]
        end_lane = lax.broadcasted_iota(jnp.int32, (ROWS, COLS), 1)
        d1, d2 = (
            jnp.where(
                end_lane == 0,
                rolled(ends_d[0], k),
                jnp.where(end_lane == COLS - 1, rolled(ends_d[1], -k), 0.0),
            )
            for k in (1, 2)
        )
        top, low = state[0, 0], state[0, bottom]
        top_v = state[2, 0] + half * north_h
        low_v = state[2, bottom] - half * south_h
        state[2, 0] = top_v
        state[2, bottom] = low_v
        north_v = (north_v - half * top) * north_live
        south_v = (south_v + half * low) * south_live
        ends = merged(*(ew_recv[t, SIDES.index((0, dn)), :MEMBERS] for dn in (1, -1)))
        for r in range(ROWS):
            h = state[0, r]
            a, b = 4 * r, 4 * (ROWS + r)
            far_h = at_ends(ends, a, a + 3)
            far_u = at_ends(ends, a + 1, a + 2)
            far_h1 = at_ends(ends, b, b + 3)
            far_u2 = at_ends(ends, b + 1, b + 2)
            u = state[1, r] + edge * far_h
            state[1, r] = u
            above = state[2, r - 1] if r > 0 else north_v
            below = state[2, r + 1] if r < bottom else south_v
            work[r] = h - depth(r) * (apart(u, far_u - edge * h) + (below - above))
            end_d1, end_d2 = d1[r : r + 1], d2[r : r + 1]
            outside[0, r] = far_h1 - end_d1 * (edge * (1.0 / half) * u - half * far_h)
            outside[1, r] = far_u2 - edge * h * (1.0 - half * end_d2)

        for copy, _, dl in corner_copies + rows_copies:
            if_band(dl, copy.wait_recv)
        corners = {}
        for name, dl in (("n", -1), ("s", 1)):
            folded = merged(
                *(corner_recv[t, CORNERS.index((-dl, dn))] for dn in (1, -1))
            )
            x = jnp.concatenate(
                [folded] + [rolled(folded, -16 * g) for g in range(1, MEMBERS // SLOTS)], axis=0
            )
            corners[name] = (
                at_ends(x, 0, 3),
                at_four(x, 1, 0, 3, 2),
                at_four(x, 5, 4, 7, 6),
                at_ends(x, 9, 10),
                at_ends(x, 8, 11),
                at_ends(x, 12, 15),
            )
        n_h, n_row1, n_row2, n_v, n_v_in, n_h_in = corners["n"]
        s_h, s_row1, s_row2, s_v, s_v_in, s_h_in = corners["s"]
        south_h1, south_v2 = from_rows(0, 2), from_rows(0, 3)
        north_h1, north_v2 = from_rows(1, 2), from_rows(1, 3)
        south_d1, south_d2 = edge_depths(0)
        north_d1, north_d2 = edge_depths(1)
        north_h1 = north_h1 - north_d1 * (top_v - half * north_h) + north_d1 * corner * n_row1
        south_h1 = south_h1 + south_d1 * (low_v + half * south_h) + south_d1 * corner * s_row1
        north_h1 = north_h1 * north_live
        south_h1 = south_h1 * south_live
        north_v2 = north_v2 - half * top * (1.0 - half * north_d2)
        north_v2 = north_v2 + half * north_d2 * corner * n_row2 - coriolis(-1) * edge * n_h
        south_v2 = south_v2 + half * low * (1.0 - half * south_d2)
        south_v2 = south_v2 - half * south_d2 * corner * s_row2 - coriolis(ROWS) * edge * s_h
        for r, far_h1, far_u2 in (
            (0, n_v, coriolis(0) * half * n_h + edge * d2[0:1] * n_v_in),
            (1, half * n_h, half * edge * d2[1:2] * n_h_in),
            (6, half * s_h, half * edge * d2[6:7] * s_h_in),
            (7, -s_v, -coriolis(7) * half * s_h - edge * d2[7:8] * s_v_in),
        ):
            outside[0, r] = outside[0, r] + d1[r : r + 1] * far_h1
            outside[1, r] = outside[1, r] + far_u2
        for r in (0, 1, 7, 6, 2, 5, 3, 4):
            h, u, v = work[r], state[1, r], state[2, r]
            above = work[r - 1] if r > 0 else north_h1
            below = work[r + 1] if r < bottom else south_h1
            state[1, r] = u + coriolis(r) * v - half * apart(h, outside[0, r])
            state[2, r] = v - coriolis(r) * u - half * (below - above)
        north_v2 = (north_v2 - half * work[0]) * north_live
        south_v2 = (south_v2 + half * work[bottom]) * south_live

        def last_height(r, north_v2, south_v2):
            h = work[r]
            above = state[2, r - 1] if r > 0 else north_v2
            below = state[2, r + 1] if r < bottom else south_v2
            around = apart(state[1, r], outside[1, r] - edge * h) + (below - above)
            state[0, r] = h - depth(r) * around

        for r in range(ROWS):
            pending[r] = functools.partial(last_height, r, north_v2, south_v2)

    finish(*range(ROWS))

    pick_lane = jnp.broadcast_to(lon_cols, (MEMBERS, COLS))

    def at_observed(tile_of_row, lane):
        found = jnp.zeros(lane.shape, F32)
        for r in range(ROWS):
            found = jnp.where(lat_rows == r, lanes_of(tile_of_row(r), lane), found)
        return found

    def send_observations(b, prior):
        mean = jnp.sum(prior, axis=0, keepdims=True) / MEMBERS
        away = prior - mean
        total = jnp.sum(away * away, axis=0, keepdims=True) / (MEMBERS - 1) + var_row
        shift = (value_row - mean) / total
        spread = -1.0 / (jnp.sqrt(total) * (jnp.sqrt(var_row) + jnp.sqrt(total)))
        coefs = jnp.where(sub8 == 0, shift, jnp.where(sub8 == 1, spread, 0.0))
        rows = jnp.concatenate(
            [away, coefs, jnp.zeros((COLS - MEMBERS - 8, COLS), F32)], axis=0
        ).astype(BF16)
        tile = lax.dot_general(picks[b], rows, rows_to_lanes, preferred_element_type=F32)
        tile = tile.astype(BF16)
        obs_send[b] = tile
        obs_recv[b, PAIRS - 1] = tile
        send_to_all(obs_send.at[b], obs_recv.at[b], obs_ssem.at[b], obs_rsem.at[b])
        return away.astype(BF16)

    def make_dev(f):
        for r in range(ROWS):
            x = state[f, r]
            mean = jnp.sum(x, axis=0, keepdims=True) / MEMBERS
            dev[f, :, r * COLS : (r + 1) * COLS] = (x - mean).astype(BF16)

    def receive(b):
        all_received(obs_recv.at[b], obs_ssem.at[b], obs_rsem.at[b])
        table = gather_rows(obs_recv.at[b], False)
        obs_dev = table.astype(BF16)[:, :MEMBERS]
        weights = table[:, MEMBERS : MEMBERS + 1] + table[:, MEMBERS + 1 : MEMBERS + 2] * table
        weights = weights.astype(BF16).astype(F32)
        weights = jnp.transpose(weights).astype(BF16)[:MEMBERS]
        return obs_dev, weights

    def make_gains(b, f, obs_dev):
        gains = []
        for r in range(ROWS):
            lanes = slice(r * COLS, (r + 1) * COLS)
            cov = jnp.dot(obs_dev, dev[f, :, lanes], preferred_element_type=F32)
            gains.append((cov * loc[b, r]).astype(BF16))
        return gains

    def update(f, gains, weights, last):
        for pair in range(ROWS // 2):
            gain = jnp.concatenate(gains[2 * pair : 2 * pair + 2], axis=1)
            step = jnp.dot(weights, gain, preferred_element_type=F32)
            for i in range(2):
                r = 2 * pair + i
                new = state[f, r] + step[:, i * COLS : (i + 1) * COLS]
                if last:
                    out[f, :, r, :] = new
                else:
                    state[f, r] = new

    prior = at_observed(lambda r: state[0, r], pick_lane)
    prior_dev = send_observations(0, prior)
    for f in range(3):
        make_dev(f)
    all_received(lab_recv, lab_ssem, lab_rsem)
    make_locality(0)
    prior_loc = at_observed(lambda r: loc[0, r], jnp.broadcast_to(lon_cols, (OBS, COLS)))
    obs_dev, weights = receive(0)
    cov = jnp.dot(obs_dev, prior_dev, preferred_element_type=F32)
    gain = (cov * prior_loc).astype(BF16)
    send_observations(1, prior + jnp.dot(weights, gain, preferred_element_type=F32))
    for f in range(3):
        update(f, make_gains(0, f, obs_dev), weights, False)
    for f in range(3):
        make_dev(f)
    make_locality(1)
    for copy, dl, _ in sent:
        if_band(dl, copy.wait_send)
    all_sent(lab_recv, lab_ssem, lab_rsem)
    for b in range(2):
        all_sent(obs_recv.at[b], obs_ssem.at[b], obs_rsem.at[b])
    obs_dev, weights = receive(1)
    gains = make_gains(1, 0, obs_dev)
    for f in range(3):
        ahead = make_gains(1, f + 1, obs_dev) if f < 2 else None
        update(f, gains, weights, True)
        gains = ahead


def per_device(n_lat, n_lon, *args):
    args = [pltpu.with_memory_space_constraint(arg, pltpu.HBM) for arg in args]
    vmem = pltpu.VMEM
    dma = pltpu.SemaphoreType.DMA
    ints = vmem((SLOTS,), jnp.int32)
    floats = vmem((SLOTS,), F32)
    return pl.pallas_call(
        functools.partial(kernel, n_lat, n_lon),
        out_shape=vmem(args[0].shape, F32),
        in_specs=[pl.BlockSpec(memory_space=pltpu.HBM)] * len(args),
        out_specs=pl.BlockSpec(memory_space=vmem),
        scratch_shapes=[
            vmem((3, ROWS, MEMBERS, COLS), F32),
            vmem((ROWS, COLS), F32),
            vmem((32,), F32),
            vmem((256,), F32),
            ints,
            ints,
            ints,
            ints,
            floats,
            floats,
            vmem((ROWS, MEMBERS, COLS), F32),
            vmem((2, ROWS, MEMBERS, COLS), F32),
            vmem((SUB // 2, 2, 4 * MEMBERS + 16, COLS), BF16),
            vmem((SUB // 2, 2, 4 * MEMBERS + 16, COLS), BF16),
            vmem((SUB // 2, MEMBERS + 16, COLS), BF16),
            vmem((SUB // 2, len(SIDES), MEMBERS + 16, COLS), BF16),
            vmem((SUB // 2, 2, SLOTS, COLS), BF16),
            vmem((SUB // 2, len(CORNERS), SLOTS, COLS), BF16),
            vmem((SLOTS, COLS), BF16),
            vmem((PAIRS, SLOTS, COLS), BF16),
            vmem((2, SLOTS, COLS), BF16),
            vmem((2, PAIRS, SLOTS, COLS), BF16),
            vmem((2, ROWS, OBS, COLS), F32),
            vmem((3, MEMBERS, ROWS * COLS), BF16),
            dma((9,)),
            dma((3, ROWS)),
            dma((SUB // 2, 2, 2)),
            dma((SUB // 2, 2, 2)),
            dma((SUB // 2, len(SIDES))),
            dma((SUB // 2, len(SIDES))),
            dma((SUB // 2, len(CORNERS))),
            dma((SUB // 2, len(CORNERS))),
            dma((len(BANDS),)),
            dma((len(BANDS),)),
            dma((2, len(BANDS))),
            dma((2, len(BANDS))),
        ],
        compiler_params=pltpu.CompilerParams(
            collective_id=0, has_side_effects=True, vmem_limit_bytes=60 * 1024 * 1024
        ),
        name="window",
    )(*args)


def solution(mesh):
    return jax.shard_map(
        functools.partial(per_device, mesh.shape["lat"], mesh.shape["lon"]),
        mesh=mesh,
        in_specs=(
            P(None, None, "lat", "lon"),
            P("lat", "lon"),
            P(),
            P(),
            P(("lat", "lon")),
            P(("lat", "lon")),
            P(("lat", "lon")),
            P(("lat", "lon")),
            P(("lat", "lon")),
            P(("lat", "lon")),
        ),
        out_specs=P(None, None, "lat", "lon"),
        check_vma=False,
    )
```
